128 devices in a mesh: dp: 4 (over y), tok: 32 (over x, z, core).
Axes of the slice: x: 4, y: 4, z: 4, core: 2. Of those that a mesh axis runs over, the one named last changes fastest.
Arguments:
- q_tokens: bfloat16 [4, 16384, 1152], P('dp', 'tok'), may hold values from -8 to 8
- k_tokens: bfloat16 [4, 16384, 1152], P('dp', 'tok'), may hold values from -8 to 8
- v_tokens: bfloat16 [4, 16384, 1152], P('dp', 'tok'), may hold values from -6 to 6
- d_attended: bfloat16 [4, 16384, 1152], P('dp', 'tok'), may hold values from -6 to 6
- w_out: bfloat16 [1152, 1152], replicated, may hold values from -0.1875 to 0.1875
- lengths: int32 [4, 64], P('dp'), may hold values from 1 to 4, 128 in all within a row
Outputs:
- attended: bfloat16 [4, 16384, 1152], P('dp', 'tok')
- grad_q: bfloat16 [4, 16384, 1152], P('dp', 'tok')
- grad_k: bfloat16 [4, 16384, 1152], P('dp', 'tok')
- grad_v: bfloat16 [4, 16384, 1152], P('dp', 'tok')
- grad_wo: float32 [1152, 1152], P('tok')
The draws below stay inside these ranges and needn't reach their ends.
All inputs are finite; a program needn't handle non-finite values.
Results may differ from the reference program's by a relative error of at most 0.025.
Values may be sent and summed in bfloat16 or wider, within the bound.
A program may use at most 256 MiB of HBM per device.

```python
import math
import jax
import jax.numpy as jnp
import numpy as np
from jax import lax

D = 1152
HEADS = 16
HEAD_DIM = 72
BLOCK = 128
MOST = 4
NBLK = 128
SLAB = 16384
IMAGES = 64
N_DP = 4


def draw_q_tokens(key, part):
    key = jax.random.fold_in(key, 3)
    shape = (N_DP, SLAB, D)
    base = jnp.clip(1.4 * jax.random.normal(key, shape, jnp.float32), -8.0, 8.0)
    return base.astype(jnp.bfloat16)


def draw_k_tokens(key, part):
    key = jax.random.fold_in(key, 5)
    shape = (N_DP, SLAB, D)
    base = jnp.clip(1.4 * jax.random.normal(key, shape, jnp.float32), -8.0, 8.0)
    return base.astype(jnp.bfloat16)


def strengthened(values, own_key, source, target, blocks, factor):
    owner, partner = [(jnp.arange(values.shape[position]) // (values.shape[position] // blocks)).reshape([-1 if axis == position else 1 for axis in range(values.ndim)]) for position in (source, target)]
    chosen = jax.random.permutation(own_key, blocks)[partner]
    strong = (owner == chosen) | (owner == (partner + blocks // 2) % blocks)
    return jnp.where(strong, factor * values, values)


def steps_of(stream_key, dims, shards, low, high):
    loudness = 1.0
    for axis_at, shards_of in shards:
        draws = jax.random.uniform(jax.random.fold_in(jax.random.fold_in(stream_key, 6), axis_at), (shards_of,), jnp.float32, low / len(shards), high / len(shards))
        loudness = loudness * jnp.repeat(jnp.exp(draws), dims[axis_at] // shards_of).reshape((-1,) + (1,) * (len(dims) - 1 - axis_at))
    return loudness


def split_up(number_of, total, most, slope):
    loads = [(1 << 20) // math.isqrt(rank ** slope) + 1 for rank in range(2, number_of + 1)]
    rest, counts = total - most - (number_of - 1), [1] * (number_of - 1)
    while rest > 0:
        candidates = [i for i in range(number_of - 1) if counts[i] < most]
        whole, remaining = sum([loads[i] for i in candidates]), rest
        for i in candidates:
            extra = min(most - counts[i], max(1, remaining * loads[i] // whole), rest)
            counts[i] = counts[i] + extra
            rest = rest - extra
    return np.array([most] + counts)


def ragged(own_key, number_of, total, bound, skew):
    if number_of == 2:
        one = jax.random.randint(own_key, (), max(1, total - bound), min(bound, total - 1) + 1)
        return jnp.stack([one, total - one])
    sizes = jnp.asarray(split_up(number_of, total, bound, skew), jnp.int32)
    couples = (number_of - 1) // 2
    giver, taker = sizes[1:1 + 2 * couples:2], sizes[2:2 + 2 * couples:2]
    slack = jnp.minimum(giver - 1, bound - taker)
    shifted = jax.random.randint(jax.random.fold_in(own_key, 1), (couples,), 0, 1 << 20) % (slack + 1)
    sizes = sizes.at[1:1 + 2 * couples:2].set(giver - shifted).at[2:2 + 2 * couples:2].set(taker + shifted)
    return sizes[jax.random.permutation(jax.random.fold_in(own_key, 2), number_of)]


def centred(stream_key, dims, scale, bound, split=(), kind=jnp.bfloat16):
    drawn = scale * jax.random.normal(stream_key, dims, jnp.float32)
    if split:
        drawn = drawn * steps_of(stream_key, dims, split, -0.22, 0.18)
    return jnp.clip(drawn, -bound, bound).astype(kind)


def noise_with(rng, extent, width, bound, shards, heavy, kind=jnp.bfloat16):
    values = width * jax.random.normal(rng, extent, jnp.float32)
    if shards:
        values = values * steps_of(rng, extent, shards, -0.22, 0.18)
    return jnp.clip(strengthened(values, jax.random.fold_in(rng, 3), *heavy), -bound, bound).astype(kind)


def setup_inputs(seed: int = 0) -> dict:
    key_of = jax.random.split(jax.random.key(seed), 7)
    q_tokens = draw_q_tokens(jax.random.fold_in(key_of[6], 71), 0)
    k_tokens = draw_k_tokens(jax.random.fold_in(key_of[6], 71), 0)
    v_tokens = noise_with(key_of[2], (N_DP, SLAB, D), 1.0, 6.0, ((0, 4), (1, 32)), (1, 2, 32, 2.75))
    d_attended = centred(key_of[3], (N_DP, SLAB, D), 1.0, 6.0, ((0, 4), (1, 32)))
    w_out = centred(key_of[4], (D, D), D ** -0.5, 0.1875)
    lengths = jax.vmap(lambda own: ragged(own, IMAGES, NBLK, MOST, 0))(jax.random.split(key_of[5], N_DP)).reshape((N_DP, IMAGES)).astype(jnp.int32)
    return dict(q_tokens=q_tokens, k_tokens=k_tokens, v_tokens=v_tokens, d_attended=d_attended, w_out=w_out, lengths=lengths)


masked_score = -1e+30

def image_of_blocks(lengths, count):
    ends = jnp.cumsum(lengths).astype(jnp.int32)
    blocks = jnp.arange(count, dtype=jnp.int32)
    before = (ends[None, :] <= blocks[:, None]).astype(jnp.int32)
    return lax.optimization_barrier(jnp.sum(before, axis=1)).astype(jnp.int32)

def group_pass(q_group, k_group, v_group, dy_group, w_out, lengths):
    nblk = SLAB // BLOCK
    reach = MOST - 1
    span = 4 * BLOCK
    window = (4 + 2 * reach) * BLOCK
    margin = reach * BLOCK
    scale = HEAD_DIM ** (-0.5)
    ids = jnp.repeat(image_of_blocks(lengths, nblk), BLOCK)
    pad_ids = jnp.concatenate([jnp.full((margin,), -1, jnp.int32), ids, jnp.full((margin,), -1, jnp.int32)])
    d_mixed = jnp.dot(dy_group, w_out.T, preferred_element_type=jnp.float32).astype(jnp.bfloat16)
    q_wide = q_group.astype(jnp.float32)
    k_pad = jnp.pad(k_group.astype(jnp.float32), ((margin, margin), (0, 0)))
    v_pad = jnp.pad(v_group.astype(jnp.float32), ((margin, margin), (0, 0)))
    dm_wide = d_mixed.astype(jnp.float32)

    def step(carry, index):
        dk_acc, dv_acc = carry
        first = index * span
        q_rows = lax.dynamic_slice_in_dim(q_wide, first, span, 0).reshape(span, HEADS, HEAD_DIM)
        k_rows = lax.dynamic_slice_in_dim(k_pad, first, window, 0).reshape(window, HEADS, HEAD_DIM)
        v_rows = lax.dynamic_slice_in_dim(v_pad, first, window, 0).reshape(window, HEADS, HEAD_DIM)
        dm_rows = lax.dynamic_slice_in_dim(dm_wide, first, span, 0).reshape(span, HEADS, HEAD_DIM)
        q_ids = lax.dynamic_slice_in_dim(ids, first, span, 0)
        k_ids = lax.dynamic_slice_in_dim(pad_ids, first, window, 0)
        same = q_ids[:, None] == k_ids[None, :]
        scores = jnp.einsum('qhd,khd->hqk', q_rows, k_rows) * scale
        scores = jnp.where(same[None, :, :], scores, masked_score)
        top = lax.optimization_barrier(jnp.max(scores, axis=2, keepdims=True))
        lse = top + jnp.log(lax.optimization_barrier(jnp.sum(jnp.exp(scores - top), axis=2, keepdims=True)))
        probs = jnp.exp(scores - lse)
        probs_low = lax.optimization_barrier(probs.astype(jnp.bfloat16)).astype(jnp.float32)
        mixed = jnp.einsum('hqk,khd->qhd', probs_low, v_rows).astype(jnp.bfloat16)
        mixed_wide = lax.optimization_barrier(mixed).astype(jnp.float32)
        d_probs = jnp.einsum('qhd,khd->hqk', dm_rows, v_rows)
        delta = jnp.einsum('qhd,qhd->hq', dm_rows, mixed_wide)
        d_scores = probs * (d_probs - delta[:, :, None])
        d_scores = lax.optimization_barrier(d_scores.astype(jnp.bfloat16)).astype(jnp.float32)
        grad_q = (jnp.einsum('hqk,khd->qhd', d_scores, k_rows) * scale).astype(jnp.bfloat16)
        dk_part = jnp.einsum('hqk,qhd->khd', d_scores, q_rows) * scale
        dv_part = jnp.einsum('hqk,qhd->khd', probs_low, dm_rows)
        dk_old = lax.dynamic_slice_in_dim(dk_acc, first, window, 0)
        dv_old = lax.dynamic_slice_in_dim(dv_acc, first, window, 0)
        dk_acc = lax.dynamic_update_slice_in_dim(dk_acc, dk_old + dk_part.reshape(window, D), first, 0)
        dv_acc = lax.dynamic_update_slice_in_dim(dv_acc, dv_old + dv_part.reshape(window, D), first, 0)
        return ((dk_acc, dv_acc), (mixed.reshape(span, D), grad_q.reshape(span, D)))
    zeros = jnp.zeros((SLAB + 2 * margin, D), jnp.float32)
    (dk_acc, dv_acc), (mixed_all, grad_q_all) = lax.scan(step, (zeros, zeros), jnp.arange(nblk // 4, dtype=jnp.int32))
    mixed_all = mixed_all.reshape(SLAB, D)
    grad_q_all = grad_q_all.reshape(SLAB, D)
    grad_k = dk_acc[margin:margin + SLAB].astype(jnp.bfloat16)
    grad_v = dv_acc[margin:margin + SLAB].astype(jnp.bfloat16)
    attended = jnp.dot(mixed_all, w_out, preferred_element_type=jnp.float32).astype(jnp.bfloat16)
    weight_term = jnp.dot(mixed_all.T, dy_group, preferred_element_type=jnp.float32)
    return (attended, grad_q_all, grad_k, grad_v, weight_term)

def reference(q_tokens, k_tokens, v_tokens, d_attended, w_out, lengths):
    attended, grad_q, grad_k, grad_v = ([], [], [], [])
    weight_sum = jnp.zeros((D, D), jnp.float32)
    for group in range(N_DP):
        result = group_pass(q_tokens[group], k_tokens[group], v_tokens[group], d_attended[group], w_out, lengths[group])
        attended.append(result[0])
        grad_q.append(result[1])
        grad_k.append(result[2])
        grad_v.append(result[3])
        weight_sum = weight_sum + result[4]
    grad_wo = weight_sum * (1.0 / math.sqrt(N_DP * SLAB))
    return (jnp.stack(attended), jnp.stack(grad_q), jnp.stack(grad_k), jnp.stack(grad_v), grad_wo)
```

```python
import functools
import math

import jax
import jax.numpy as jnp
from jax import lax
from jax.experimental import pallas as pl
from jax.experimental.pallas import tpu as pltpu
from jax.sharding import PartitionSpec as P

HEADS = 16
HEAD_DIM = 72
BLOCK = 128
D = 1152
OWN = 4
SLOTS = 8
WINDOW = 256
SCALE = HEAD_DIM ** (-0.5)
EXP2_SCALE = SCALE * math.log2(math.e)
MESH = pl.DeviceIdType.MESH
NN = (((1,), (0,)), ((), ()))
NT = (((1,), (1,)), ((), ()))
TN = (((0,), (0,)), ((), ()))


def dot(a, b, dims):
    return lax.dot_general(a, b, dims, preferred_element_type=jnp.float32)


def boundary(lengths_ref, edge):
    def step(i, carry):
        start, before, after = carry
        end = start + lengths_ref[0, i]
        hit = jnp.logical_and(start < edge, end > edge)
        return (end, jnp.where(hit, edge - start, before), jnp.where(hit, end - edge, after))

    zero = jnp.int32(0)
    _, before, after = lax.fori_loop(0, lengths_ref.shape[1], step, (zero, zero, zero))
    return before, after


def greet(left, right):
    barrier = pltpu.get_barrier_semaphore()
    for other in (left, right):
        pl.semaphore_signal(barrier, inc=1, device_id={"tok": other}, device_id_type=MESH)
    pl.semaphore_wait(barrier, 2)


def ring_neighbours(count):
    me = lax.axis_index("tok")
    return lax.rem(me + count - 1, count), lax.rem(me + 1, count)


def exchange_kernel(
    count, lengths_ref, q_ref, k_ref, v_ref, dy_ref, w_ref, halo_ref, dm_ref, pack, send_sem, recv_sem
):
    left, right = ring_neighbours(count)
    first = lax.axis_index("tok") * OWN
    greet(left, right)
    copies = []

    def send(side, slot, source):
        copy = pltpu.make_async_remote_copy(
            src_ref=source,
            dst_ref=halo_ref.at[1 - side, slot],
            send_sem=send_sem.at[side, slot],
            recv_sem=recv_sem.at[1 - side, slot],
            device_id={"tok": right if side else left},
            device_id_type=MESH,
        )
        copy.start()
        copies.append(copy)

    near = [slice(0, BLOCK), slice(3 * BLOCK, 4 * BLOCK)]
    far = [slice(BLOCK, 2 * BLOCK), slice(2 * BLOCK, 3 * BLOCK)]
    for side in range(2):
        send(side, 0, k_ref.at[near[side]])
        send(side, 1, v_ref.at[near[side]])
    for side in range(2):
        before, after = boundary(lengths_ref, first + side * OWN)
        shared = jnp.logical_and(before == 2, after == 2)
        pack[side, 0] = jnp.where(shared, k_ref[far[side]], q_ref[near[side]])
        pack[side, 1] = jnp.where(shared, v_ref[far[side]], dy_ref[near[side]])
        send(side, 2, pack.at[side, 0])
        send(side, 3, pack.at[side, 1])
    for part in range(OWN):
        rows = slice(part * BLOCK, (part + 1) * BLOCK)
        dm_ref[rows] = dot(dy_ref[rows], w_ref[...], NT).astype(jnp.bfloat16)
    for copy in copies:
        copy.wait()


def attend(q_buf, k_buf, v_buf, dm_buf, mixed, gq, gk, gv, q_at, q_blocks, k_at, k_blocks):
    q_rows = pl.ds(pl.multiple_of(q_at * BLOCK, BLOCK), q_blocks * BLOCK)
    k_rows = pl.ds(pl.multiple_of(k_at * BLOCK, BLOCK), k_blocks * BLOCK)
    lane = lax.broadcasted_iota(jnp.int32, (1, WINDOW), 1)

    def head(h):
        at = h * HEAD_DIM
        base = jnp.minimum(at // 128, (D - WINDOW) // 128) * 128
        offset = at - base
        window = pl.ds(pl.multiple_of(base, 128), WINDOW)
        inside = jnp.logical_and(lane >= offset, lane < offset + HEAD_DIM)
        keep = jnp.where(inside, 1.0, 0.0).astype(jnp.bfloat16)
        q = q_buf[q_rows, window]
        k = k_buf[k_rows, window]
        v = v_buf[k_rows, window]
        dm = dm_buf[q_rows, window]
        scores = dot(k * keep, q, NT)
        d_probs = dot(v * keep, dm, NT)
        top = jnp.max(scores, axis=0, keepdims=True)
        weights = jnp.exp2((scores - top) * EXP2_SCALE)
        probs = weights * (1.0 / jnp.sum(weights, axis=0, keepdims=True))
        probs_low = probs.astype(jnp.bfloat16)
        product = probs * d_probs
        delta = jnp.sum(product, axis=0, keepdims=True)
        d_scores = (product - probs * delta).astype(jnp.bfloat16)

        def put(ref, rows, new):
            old = ref[rows, window]
            ref[rows, window] = jnp.where(lane < offset, old, new.astype(jnp.bfloat16))

        put(mixed, q_rows, dot(probs_low, v, TN))
        put(gv, k_rows, dot(probs_low, dm, NN))
        put(gq, q_rows, dot(d_scores, k, TN) * SCALE)
        put(gk, k_rows, dot(d_scores, q, NN) * SCALE)

    def two(i, carry):
        head(2 * i)
        head(2 * i + 1)
        return carry

    lax.fori_loop(0, HEADS // 2, two, 0)


def attention_kernel(
    lengths_ref, q_ref, k_ref, v_ref, dy_ref, dm_ref, halo_ref, w_ref,
    att_out, gq_out, gk_out, gv_out, ret_out, gw_out, flags_out,
    q_buf, k_buf, v_buf, dy_buf, dm_buf, w_buf, mixed, gq, gk, gv, att, gw_buf, work, sem,
):
    first = lax.axis_index("tok") * OWN
    last = first + OWN
    own = pl.ds(2 * BLOCK, OWN * BLOCK)

    def block(i):
        return pl.ds(i * BLOCK, BLOCK)

    loads = [
        (q_ref, q_buf.at[own]), (k_ref, k_buf.at[own]), (v_ref, v_buf.at[own]),
        (dm_ref, dm_buf.at[own]), (dy_ref, dy_buf.at[own]), (w_ref, w_buf),
    ]
    for side, (near, far) in enumerate(((1, 0), (6, 7))):
        loads += [
            (halo_ref.at[side, 0], k_buf.at[block(near)]),
            (halo_ref.at[side, 1], v_buf.at[block(near)]),
            (halo_ref.at[side, 2], q_buf.at[block(near)]),
            (halo_ref.at[side, 2], k_buf.at[block(far)]),
            (halo_ref.at[side, 3], dy_buf.at[block(near)]),
            (halo_ref.at[side, 3], v_buf.at[block(far)]),
        ]
    copies = [pltpu.make_async_copy(a, b, sem.at[i]) for i, (a, b) in enumerate(loads)]
    for copy in copies:
        copy.start()

    l_before, l_after = boundary(lengths_ref, first)
    r_before, r_after = boundary(lengths_ref, last)
    l_shared = jnp.logical_and(l_before == 2, l_after == 2)
    r_shared = jnp.logical_and(r_before == 2, r_after == 2)
    l_away = l_after == 1
    l_here = jnp.logical_and(l_before == 1, l_after > 1)
    r_here = r_after == 1
    r_away = jnp.logical_and(r_before == 1, r_after > 1)
    for i, flag in enumerate((l_away, l_shared, r_away, r_shared)):
        flags_out[i] = flag.astype(jnp.int32)

    def collect(i, carry):
        start, number = carry
        end = start + lengths_ref[0, i]
        on_left = jnp.logical_and(start < first, end > first)
        on_right = jnp.logical_and(start < last, end > last)
        within = jnp.logical_and(start >= first, end <= last)
        mine = jnp.logical_or(
            within,
            jnp.logical_or(
                jnp.logical_and(on_left, jnp.logical_not(l_away)),
                jnp.logical_and(on_right, jnp.logical_not(r_away)),
            ),
        )
        shared = jnp.logical_or(
            jnp.logical_and(on_left, l_shared), jnp.logical_and(on_right, r_shared)
        )

        @pl.when(mine)
        def _():
            work[number, 0] = jnp.where(shared, 5, end - start)
            work[number, 1] = start - first + 2

        return end, number + mine.astype(jnp.int32)

    _, number = lax.fori_loop(
        0, lengths_ref.shape[1], collect, (jnp.int32(0), jnp.int32(0))
    )
    for copy in copies:
        copy.wait()

    for here, slot in ((l_here, 1), (r_here, 6)):
        @pl.when(here)
        def _():
            dm_buf[block(slot)] = dot(dy_buf[block(slot)], w_buf[...], NT).astype(jnp.bfloat16)

    bufs = (q_buf, k_buf, v_buf, dm_buf, mixed, gq, gk, gv)

    def image(i, carry):
        kind, at = work[i, 0], work[i, 1]
        for blocks in range(1, OWN + 1):
            @pl.when(kind == blocks)
            def _():
                attend(*bufs, at, blocks, at, blocks)

        @pl.when(kind == 5)
        def _():
            attend(*bufs, jnp.where(at == 0, 2, 4), 2, at, 4)

        return carry

    lax.fori_loop(0, number, image, 0)

    idle = (
        (jnp.logical_not(l_here), 1), (l_away, 2), (r_away, 5), (jnp.logical_not(r_here), 6)
    )
    for flag, slot in idle:
        @pl.when(flag)
        def _():
            mixed[block(slot)] = jnp.zeros((BLOCK, D), jnp.bfloat16)

    for slot in range(1, 7):
        att[block(slot)] = dot(mixed[block(slot)], w_buf[...], NN).astype(jnp.bfloat16)

    stores = [
        (att.at[own], att_out), (gq.at[own], gq_out), (gk.at[own], gk_out), (gv.at[own], gv_out),
    ]
    for side, near in enumerate((1, 6)):
        stores += [
            (gk.at[block(near)], ret_out.at[side, 0]), (gv.at[block(near)], ret_out.at[side, 1]),
        ]
    outs = [pltpu.make_async_copy(a, b, sem.at[i]) for i, (a, b) in enumerate(stores)]
    for copy in outs:
        copy.start()
    for side, (near, far, shared) in enumerate(((1, 0, l_shared), (6, 7, r_shared))):
        for at, (first_choice, second_choice) in enumerate(((gk, gq), (gv, att))):
            index = len(stores) + 2 * side + at

            @pl.when(shared)
            def _():
                pltpu.make_async_copy(
                    first_choice.at[block(far)], ret_out.at[side, 2 + at], sem.at[index]
                ).start()

            @pl.when(jnp.logical_not(shared))
            def _():
                pltpu.make_async_copy(
                    second_choice.at[block(near)], ret_out.at[side, 2 + at], sem.at[index]
                ).start()

    rows = pl.ds(BLOCK, 6 * BLOCK)

    def weight(i, carry):
        lanes = pl.ds(pl.multiple_of(i * 128, 128), 128)
        gw_buf[lanes] = dot(mixed[rows, lanes], dy_buf[rows], TN).astype(jnp.bfloat16)
        return carry

    lax.fori_loop(0, D // 128, weight, 0)
    gw = pltpu.make_async_copy(gw_buf, gw_out, sem.at[len(loads) - 1])
    gw.start()
    for copy in outs:
        copy.wait()
    for side in range(2):
        for at in range(2):
            index = len(stores) + 2 * side + at
            pltpu.make_async_copy(
                gk.at[block(0)], ret_out.at[side, 2 + at], sem.at[index]
            ).wait()
    gw.wait()


def return_kernel(count, ret_ref, back_ref, send_sem, recv_sem):
    left, right = ring_neighbours(count)
    greet(left, right)
    copies = []
    for side in range(2):
        for slot in range(4):
            copy = pltpu.make_async_remote_copy(
                src_ref=ret_ref.at[side, slot],
                dst_ref=back_ref.at[1 - side, slot],
                send_sem=send_sem.at[side, slot],
                recv_sem=recv_sem.at[1 - side, slot],
                device_id={"tok": right if side else left},
                device_id_type=MESH,
            )
            copy.start()
            copies.append(copy)
    for copy in copies:
        copy.wait()


def settle_kernel(
    flags_ref, back_ref, att_in, gq_in, gk_in, gv_in, att_out, gq_out, gk_out, gv_out, own, extra, sem
):
    def block(i):
        return pl.ds(i * BLOCK, BLOCK)

    for side, (near, far) in enumerate(((0, 1), (3, 2))):
        moved = [
            pltpu.make_async_copy(back_ref.at[side, slot], out.at[block(near)], sem.at[side, slot])
            for slot, out in enumerate((gk_out, gv_out, gq_out, att_out))
        ]
        parts = ((gk_out, near, 0), (gv_out, near, 1), (gk_out, far, 2), (gv_out, far, 3))
        ours = [
            pltpu.make_async_copy(out.at[block(at)], own.at[side, slot], sem.at[side, slot])
            for out, at, slot in parts
        ]
        theirs = [
            pltpu.make_async_copy(
                back_ref.at[side, slot], extra.at[side, slot], sem.at[side, 4 + slot]
            )
            for _, _, slot in parts
        ]
        done = [
            pltpu.make_async_copy(own.at[side, slot], out.at[block(at)], sem.at[side, slot])
            for out, at, slot in parts
        ]

        @pl.when(flags_ref[2 * side] == 1)
        def _():
            for copy in moved:
                copy.start()
            for copy in moved:
                copy.wait()

        @pl.when(flags_ref[2 * side + 1] == 1)
        def _():
            for copy in ours + theirs:
                copy.start()
            for copy in ours + theirs:
                copy.wait()
            for slot in range(4):
                total = own[side, slot].astype(jnp.float32) + extra[side, slot].astype(jnp.float32)
                own[side, slot] = total.astype(jnp.bfloat16)
            for copy in done:
                copy.start()
            for copy in done:
                copy.wait()


def on_device(q_tokens, k_tokens, v_tokens, d_attended, w_out, lengths):
    rows, width = q_tokens.shape[1:]
    count = lax.axis_size("tok")
    norm = 1.0 / math.sqrt(lax.axis_size("dp") * count * rows)
    q, k, v, dy = q_tokens[0], k_tokens[0], v_tokens[0], d_attended[0]
    low = jnp.bfloat16
    vmem, smem, anywhere = (
        pl.BlockSpec(memory_space=space) for space in (pltpu.VMEM, pltpu.SMEM, pl.ANY)
    )
    token_shape = jax.ShapeDtypeStruct((rows, width), low)
    halo_shape = jax.ShapeDtypeStruct((2, 4, BLOCK, width), low)
    big = 58 * 1024 * 1024

    halo, dm = pl.pallas_call(
        functools.partial(exchange_kernel, count),
        out_shape=(halo_shape, token_shape),
        in_specs=[smem] + [vmem] * 5,
        out_specs=(anywhere, vmem),
        scratch_shapes=[
            pltpu.VMEM((2, 2, BLOCK, width), low),
            pltpu.SemaphoreType.DMA((2, 4)),
            pltpu.SemaphoreType.DMA((2, 4)),
        ],
        compiler_params=pltpu.CompilerParams(
            collective_id=0, has_side_effects=True, vmem_limit_bytes=32 * 1024 * 1024
        ),
        name="exchange",
    )(lengths, q, k, v, dy, w_out)

    slab = pltpu.VMEM((SLOTS * BLOCK, width), low)
    att, gq, gk, gv, ret, gw, flags = pl.pallas_call(
        attention_kernel,
        out_shape=(
            token_shape, token_shape, token_shape, token_shape, halo_shape,
            jax.ShapeDtypeStruct((width, width), low),
            jax.ShapeDtypeStruct((4,), jnp.int32),
        ),
        in_specs=[smem] + [anywhere] * 7,
        out_specs=(anywhere,) * 6 + (smem,),
        scratch_shapes=[slab] * 5
        + [pltpu.VMEM((width, width), low)]
        + [slab] * 5
        + [
            pltpu.VMEM((width, width), low),
            pltpu.SMEM((8, 2), jnp.int32),
            pltpu.SemaphoreType.DMA((18,)),
        ],
        compiler_params=pltpu.CompilerParams(vmem_limit_bytes=big),
        name="attention",
    )(lengths, q, k, v, dy, dm, halo, w_out)

    back = pl.pallas_call(
        functools.partial(return_kernel, count),
        out_shape=halo_shape,
        in_specs=[anywhere],
        out_specs=anywhere,
        scratch_shapes=[pltpu.SemaphoreType.DMA((2, 4)), pltpu.SemaphoreType.DMA((2, 4))],
        compiler_params=pltpu.CompilerParams(collective_id=1, has_side_effects=True),
        name="give_back",
    )(ret)

    att, gq, gk, gv = pl.pallas_call(
        settle_kernel,
        out_shape=(token_shape,) * 4,
        in_specs=[smem] + [anywhere] * 5,
        out_specs=(anywhere,) * 4,
        scratch_shapes=[
            pltpu.VMEM((2, 4, BLOCK, width), low),
            pltpu.VMEM((2, 4, BLOCK, width), low),
            pltpu.SemaphoreType.DMA((2, 8)),
        ],
        input_output_aliases={2: 0, 3: 1, 4: 2, 5: 3},
        name="settle",
    )(flags, back, att, gq, gk, gv)

    summed = lax.psum_scatter(gw, "tok", scatter_dimension=0, tiled=True)
    grad_rows = lax.psum(summed, "dp").astype(jnp.float32) * norm
    return (att[None], gq[None], gk[None], gv[None], grad_rows)


def solution(mesh):
    tokens = P("dp", "tok", None)
    return jax.shard_map(
        on_device,
        mesh=mesh,
        in_specs=(tokens, tokens, tokens, tokens, P(), P("dp", None)),
        out_specs=(tokens, tokens, tokens, tokens, P("tok", None)),
        check_vma=False,
    )
```

```python
import functools
import math

import jax
import jax.numpy as jnp
from jax import lax
from jax.experimental import pallas as pl
from jax.experimental.pallas import tpu as pltpu
from jax.sharding import PartitionSpec as P

HEADS = 16
HEAD_DIM = 72
BLOCK = 128
D = 1152
OWN = 4
SLOTS = 8
WINDOW = 256
SCALE = HEAD_DIM ** (-0.5)
EXP2_SCALE = SCALE * math.log2(math.e)
PART = 36
PAD = 48
SIDE = 4
MESH = pl.DeviceIdType.MESH
NN = (((1,), (0,)), ((), ()))
NT = (((1,), (1,)), ((), ()))
TN = (((0,), (0,)), ((), ()))


def dot(a, b, dims):
    return lax.dot_general(a, b, dims, preferred_element_type=jnp.float32)


def boundary(lengths_ref, edge):
    def step(i, carry):
        start, before, after = carry
        end = start + lengths_ref[0, i]
        hit = jnp.logical_and(start < edge, end > edge)
        return (end, jnp.where(hit, edge - start, before), jnp.where(hit, end - edge, after))

    zero = jnp.int32(0)
    _, before, after = lax.fori_loop(0, lengths_ref.shape[1], step, (zero, zero, zero))
    return before, after


def greet(others):
    barrier = pltpu.get_barrier_semaphore()
    for other in others:
        where = other if isinstance(other, dict) else {"tok": other}
        pl.semaphore_signal(barrier, inc=1, device_id=where, device_id_type=MESH)
    pl.semaphore_wait(barrier, len(others))


def ring_neighbours(count):
    me = lax.axis_index("tok")
    return lax.rem(me + count - 1, count), lax.rem(me + 1, count)


def exchange_kernel(
    count, lengths_ref, q_ref, k_ref, v_ref, dy_ref, w_ref, halo_ref, dm_ref,
    dy_buf, w_buf, near_buf, far_buf, pack, load_sem, send_sem, recv_sem,
):
    left, right = ring_neighbours(count)
    first = lax.axis_index("tok") * OWN
    near = [pl.ds(0, BLOCK), pl.ds(3 * BLOCK, BLOCK)]
    far = [pl.ds(BLOCK, BLOCK), pl.ds(2 * BLOCK, BLOCK)]
    loads = []
    for side in range(2):
        loads += [
            (q_ref.at[near[side]], near_buf.at[side]),
            (k_ref.at[far[side]], far_buf.at[side, 0]),
            (v_ref.at[far[side]], far_buf.at[side, 1]),
        ]
    loads += [(dy_ref, dy_buf), (w_ref, w_buf)]
    loads = [pltpu.make_async_copy(a, b, load_sem.at[i]) for i, (a, b) in enumerate(loads)]
    for load in loads:
        load.start()
    greet((left, right))
    copies = []

    def send(side, slot, source):
        copy = pltpu.make_async_remote_copy(
            src_ref=source,
            dst_ref=halo_ref.at[1 - side, slot],
            send_sem=send_sem.at[side, slot],
            recv_sem=recv_sem.at[1 - side, slot],
            device_id={"tok": right if side else left},
            device_id_type=MESH,
        )
        copy.start()
        copies.append(copy)

    for side in range(2):
        send(side, 0, k_ref.at[near[side]])
        send(side, 1, v_ref.at[near[side]])
    for load in loads[:-1]:
        load.wait()
    for side in range(2):
        before, after = boundary(lengths_ref, first + side * OWN)
        shared = jnp.logical_and(before == 2, after == 2)
        pack[side, 0] = jnp.where(shared, far_buf[side, 0], near_buf[side])
        pack[side, 1] = jnp.where(shared, far_buf[side, 1], dy_buf[near[side]])
        send(side, 2, pack.at[side, 0])
        send(side, 3, pack.at[side, 1])
    loads[-1].wait()
    for part in range(OWN):
        rows = slice(part * BLOCK, (part + 1) * BLOCK)
        dm_ref[rows] = dot(dy_buf[rows], w_buf[...], NT).astype(jnp.bfloat16)
    for copy in copies:
        copy.wait()


def attend(q_buf, k_buf, v_buf, dm_buf, mixed, gq, gk, gv, q_at, q_blocks, k_at, k_blocks):
    q_rows = pl.ds(pl.multiple_of(q_at * BLOCK, BLOCK), q_blocks * BLOCK)
    k_rows = pl.ds(pl.multiple_of(k_at * BLOCK, BLOCK), k_blocks * BLOCK)
    lane = lax.broadcasted_iota(jnp.int32, (1, WINDOW), 1)

    def head(h):
        at = h * HEAD_DIM
        base = jnp.minimum(at // 128, (D - WINDOW) // 128) * 128
        offset = at - base
        window = pl.ds(pl.multiple_of(base, 128), WINDOW)
        inside = jnp.logical_and(lane >= offset, lane < offset + HEAD_DIM)
        keep = jnp.where(inside, 1.0, 0.0).astype(jnp.bfloat16)
        q = q_buf[q_rows, window]
        k = k_buf[k_rows, window]
        v = v_buf[k_rows, window]
        dm = dm_buf[q_rows, window]
        scores = dot(k * keep, q, NT)
        d_probs = dot(v * keep, dm, NT)
        top = jnp.max(scores, axis=0, keepdims=True)
        weights = jnp.exp2((scores - top) * EXP2_SCALE)
        probs = weights * (1.0 / jnp.sum(weights, axis=0, keepdims=True))
        probs_low = probs.astype(jnp.bfloat16)
        product = probs * d_probs
        delta = jnp.sum(product, axis=0, keepdims=True)
        d_scores = (product - probs * delta).astype(jnp.bfloat16)

        def put(ref, rows, new):
            old = ref[rows, window]
            ref[rows, window] = jnp.where(lane < offset, old, new.astype(jnp.bfloat16))

        put(mixed, q_rows, dot(probs_low, v, TN))
        put(gv, k_rows, dot(probs_low, dm, NN))
        put(gq, q_rows, dot(d_scores, k, TN) * SCALE)
        put(gk, k_rows, dot(d_scores, q, NN) * SCALE)

    def two(i, carry):
        head(2 * i)
        head(2 * i + 1)
        return carry

    lax.fori_loop(0, HEADS // 2, two, 0)


def attention_kernel(
    lengths_ref, q_ref, k_ref, v_ref, dy_ref, dm_ref, halo_ref, w_ref,
    att_out, gq_out, gk_out, gv_out, ret_out, gw_out, flags_out,
    q_buf, k_buf, v_buf, dy_buf, dm_buf, w_buf, mixed, gq, gk, gv, att, gw_buf, gw_parts, work, sem,
):
    first = lax.axis_index("tok") * OWN
    last = first + OWN
    own = pl.ds(2 * BLOCK, OWN * BLOCK)

    def block(i):
        return pl.ds(i * BLOCK, BLOCK)

    loads = [
        (q_ref, q_buf.at[own]), (k_ref, k_buf.at[own]), (v_ref, v_buf.at[own]),
        (dm_ref, dm_buf.at[own]), (dy_ref, dy_buf.at[own]), (w_ref, w_buf),
    ]
    for side, (near, far) in enumerate(((1, 0), (6, 7))):
        loads += [
            (halo_ref.at[side, 0], k_buf.at[block(near)]),
            (halo_ref.at[side, 1], v_buf.at[block(near)]),
            (halo_ref.at[side, 2], q_buf.at[block(near)]),
            (halo_ref.at[side, 2], k_buf.at[block(far)]),
            (halo_ref.at[side, 3], dy_buf.at[block(near)]),
            (halo_ref.at[side, 3], v_buf.at[block(far)]),
        ]
    copies = [pltpu.make_async_copy(a, b, sem.at[i]) for i, (a, b) in enumerate(loads)]
    for copy in copies:
        copy.start()

    l_before, l_after = boundary(lengths_ref, first)
    r_before, r_after = boundary(lengths_ref, last)
    l_shared = jnp.logical_and(l_before == 2, l_after == 2)
    r_shared = jnp.logical_and(r_before == 2, r_after == 2)
    l_away = l_after == 1
    l_here = jnp.logical_and(l_before == 1, l_after > 1)
    r_here = r_after == 1
    r_away = jnp.logical_and(r_before == 1, r_after > 1)
    for i, flag in enumerate((l_away, l_shared, r_away, r_shared)):
        flags_out[i] = flag.astype(jnp.int32)

    def collect(i, carry):
        start, number = carry
        end = start + lengths_ref[0, i]
        on_left = jnp.logical_and(start < first, end > first)
        on_right = jnp.logical_and(start < last, end > last)
        within = jnp.logical_and(start >= first, end <= last)
        mine = jnp.logical_or(
            within,
            jnp.logical_or(
                jnp.logical_and(on_left, jnp.logical_not(l_away)),
                jnp.logical_and(on_right, jnp.logical_not(r_away)),
            ),
        )
        shared = jnp.logical_or(
            jnp.logical_and(on_left, l_shared), jnp.logical_and(on_right, r_shared)
        )

        @pl.when(mine)
        def _():
            work[number, 0] = jnp.where(shared, 5, end - start)
            work[number, 1] = start - first + 2

        return end, number + mine.astype(jnp.int32)

    _, number = lax.fori_loop(
        0, lengths_ref.shape[1], collect, (jnp.int32(0), jnp.int32(0))
    )
    for copy in copies:
        copy.wait()

    for here, slot in ((l_here, 1), (r_here, 6)):
        @pl.when(here)
        def _():
            dm_buf[block(slot)] = dot(dy_buf[block(slot)], w_buf[...], NT).astype(jnp.bfloat16)

    bufs = (q_buf, k_buf, v_buf, dm_buf, mixed, gq, gk, gv)

    def image(i, carry):
        kind, at = work[i, 0], work[i, 1]
        for blocks in range(1, OWN + 1):
            @pl.when(kind == blocks)
            def _():
                attend(*bufs, at, blocks, at, blocks)

        @pl.when(kind == 5)
        def _():
            attend(*bufs, jnp.where(at == 0, 2, 4), 2, at, 4)

        return carry

    lax.fori_loop(0, number, image, 0)

    idle = (
        (jnp.logical_not(l_here), 1), (l_away, 2), (r_away, 5), (jnp.logical_not(r_here), 6)
    )
    for flag, slot in idle:
        @pl.when(flag)
        def _():
            mixed[block(slot)] = jnp.zeros((BLOCK, D), jnp.bfloat16)

    for slot in range(1, 7):
        att[block(slot)] = dot(mixed[block(slot)], w_buf[...], NN).astype(jnp.bfloat16)

    stores = [
        (att.at[own], att_out), (gq.at[own], gq_out), (gk.at[own], gk_out), (gv.at[own], gv_out),
    ]
    for side, near in enumerate((1, 6)):
        stores += [
            (gk.at[block(near)], ret_out.at[side, 0]), (gv.at[block(near)], ret_out.at[side, 1]),
        ]
    outs = [pltpu.make_async_copy(a, b, sem.at[i]) for i, (a, b) in enumerate(stores)]
    for copy in outs:
        copy.start()
    for side, (near, far, shared) in enumerate(((1, 0, l_shared), (6, 7, r_shared))):
        for at, (first_choice, second_choice) in enumerate(((gk, gq), (gv, att))):
            index = len(stores) + 2 * side + at

            @pl.when(shared)
            def _():
                pltpu.make_async_copy(
                    first_choice.at[block(far)], ret_out.at[side, 2 + at], sem.at[index]
                ).start()

            @pl.when(jnp.logical_not(shared))
            def _():
                pltpu.make_async_copy(
                    second_choice.at[block(near)], ret_out.at[side, 2 + at], sem.at[index]
                ).start()

    rows = pl.ds(BLOCK, 6 * BLOCK)

    def weight(i, carry):
        lanes = pl.ds(pl.multiple_of(i * 128, 128), 128)
        gw_buf[lanes] = dot(mixed[rows, lanes], dy_buf[rows], TN)
        return carry

    lax.fori_loop(0, D // 128, weight, 0)
    gw_buf[D:] = jnp.zeros((PAD - PART, D), jnp.float32)
    for part in range(D // PART):
        x, z, core = part // 8, part // 2 % 4, part % 2
        place = (z, x) if core else (x, z)
        chunk = gw_buf[part * PART : part * PART + PAD]
        gw_parts[core, place[0], place[1]] = chunk.astype(jnp.bfloat16)
    gw = pltpu.make_async_copy(gw_parts, gw_out, sem.at[len(loads) - 1])
    gw.start()
    for copy in outs:
        copy.wait()
    for side in range(2):
        for at in range(2):
            index = len(stores) + 2 * side + at
            pltpu.make_async_copy(
                gk.at[block(0)], ret_out.at[side, 2 + at], sem.at[index]
            ).wait()
    gw.wait()


def finish_kernel(
    count, ret_ref, gw_ref, back_ref, sum_ref,
    mine, sibling, total, second, third, fourth, fifth,
    ret_send, ret_recv, load_sem, one_send, one_recv, sends, recvs,
):
    left, right = ring_neighbours(count)
    me, y = lax.axis_index("tok"), lax.axis_index("dp")
    core, z, x = lax.rem(me, 2), lax.rem(me // 2, SIDE), me // (2 * SIDE)
    own = pltpu.make_async_copy(gw_ref.at[core], mine, load_sem)
    own.start()

    def device(x, y, z, core):
        return {"dp": y, "tok": (x * SIDE + z) * 2 + core}

    def turned(at, step):
        return lax.rem(at + step, SIDE)

    other = device(x, y, z, 1 - core)
    steps = range(1, SIDE)
    along_x = [device(turned(x, step), y, z, core) for step in steps]
    along_y = [device(x, turned(y, step), z, core) for step in steps]
    along_z = [device(x, y, turned(z, step), core) for step in steps]
    greet([left, right, other] + along_x + along_y + along_z)

    one = []
    for row in range(SIDE):
        copy = pltpu.make_async_remote_copy(
            src_ref=gw_ref.at[1 - core, row],
            dst_ref=sibling.at[row],
            send_sem=one_send.at[row],
            recv_sem=one_recv.at[row],
            device_id=other,
            device_id_type=MESH,
        )
        copy.start()
        one.append(copy)
    copies = []
    for side in range(2):
        for slot in range(4):
            copy = pltpu.make_async_remote_copy(
                src_ref=ret_ref.at[side, slot],
                dst_ref=back_ref.at[1 - side, slot],
                send_sem=ret_send.at[side, slot],
                recv_sem=ret_recv.at[1 - side, slot],
                device_id={"tok": right if side else left},
                device_id_type=MESH,
            )
            copy.start()
            copies.append(copy)

    own.wait()
    for row in range(SIDE):
        one[row].wait()
        for column in range(SIDE):
            both = mine[row, column].astype(jnp.float32) + sibling[row, column].astype(jnp.float32)
            total[row, column] = both.astype(jnp.bfloat16)

    def spread(stage, source, landing, first_axis):
        at = jnp.where(first_axis, x, y)
        started = []
        for step in steps:
            there = turned(at, step)
            where = device(
                jnp.where(first_axis, there, x), jnp.where(first_axis, y, there), z, core
            )
            copy = pltpu.make_async_remote_copy(
                src_ref=source.at[there],
                dst_ref=landing.at[step - 1],
                send_sem=sends.at[stage, step - 1],
                recv_sem=recvs.at[stage, step - 1],
                device_id=where,
                device_id_type=MESH,
            )
            copy.start()
            started.append(copy)
        return at, started

    at, started = spread(0, total, second, core == 0)
    for copy in started:
        copy.wait()
    for column in range(SIDE):
        whole = total[at, column].astype(jnp.float32)
        for step in range(SIDE - 1):
            whole = whole + second[step, column].astype(jnp.float32)
        mine[0, column] = whole.astype(jnp.bfloat16)
    at, started = spread(1, mine.at[0], third, core == 1)
    for copy in started:
        copy.wait()
    whole = mine[0, at].astype(jnp.float32)
    for step in range(SIDE - 1):
        whole = whole + third[step].astype(jnp.float32)
    sum_ref[...] = whole.astype(jnp.bfloat16)

    gap = lax.rem(z - y + SIDE, SIDE)

    def to_plane(step):
        return pltpu.make_async_remote_copy(
            src_ref=sum_ref,
            dst_ref=fourth.at[step - 1],
            send_sem=sends.at[2, step - 1],
            recv_sem=recvs.at[2, step - 1],
            device_id=device(x, y, turned(z, SIDE - step), core),
            device_id_type=MESH,
        )

    def to_row(step):
        return pltpu.make_async_remote_copy(
            src_ref=fifth.at[0],
            dst_ref=fifth.at[1],
            send_sem=sends.at[3, step - 1],
            recv_sem=recvs.at[3, 0],
            device_id=device(x, turned(y, step), z, core),
            device_id_type=MESH,
        )

    for step in steps:
        @pl.when(gap == step)
        def _():
            copy = to_plane(step)
            copy.start()
            copy.wait_send()

    @pl.when(gap == 0)
    def _():
        for step in steps:
            to_plane(step).wait_recv()
        whole = sum_ref[...].astype(jnp.float32)
        for step in range(SIDE - 1):
            whole = whole + fourth[step].astype(jnp.float32)
        fifth[0] = whole.astype(jnp.bfloat16)
        started = [to_row(step) for step in steps]
        for copy in started:
            copy.start()
        for copy in started:
            copy.wait_send()
        sum_ref[...] = fifth[0]

    @pl.when(gap != 0)
    def _():
        to_row(1).wait_recv()
        sum_ref[...] = fifth[1]

    for copy in copies:
        copy.wait()


def settle_kernel(
    norm, flags_ref, sum_ref, back_ref, att_in, gq_in, gk_in, gv_in,
    att_out, gq_out, gk_out, gv_out, rows_ref, own, extra, sem,
):
    def block(i):
        return pl.ds(i * BLOCK, BLOCK)

    rows_ref[...] = sum_ref[:PART].astype(jnp.float32) * norm
    for side, (near, far) in enumerate(((0, 1), (3, 2))):
        parts = ((gk_out, near, 0), (gv_out, near, 1), (gk_out, far, 2), (gv_out, far, 3))
        ours = [
            pltpu.make_async_copy(out.at[block(at)], own.at[side, slot], sem.at[side, slot])
            for out, at, slot in parts
        ]
        theirs = [
            pltpu.make_async_copy(
                back_ref.at[side, slot], extra.at[side, slot], sem.at[side, 4 + slot]
            )
            for slot in range(4)
        ]
        moved = [
            pltpu.make_async_copy(extra.at[side, slot], out.at[block(near)], sem.at[side, slot])
            for slot, out in enumerate((gk_out, gv_out, gq_out, att_out))
        ]
        added = [
            pltpu.make_async_copy(own.at[side, slot], out.at[block(at)], sem.at[side, slot])
            for out, at, slot in parts
        ]

        @pl.when(flags_ref[2 * side] == 1)
        def _():
            for copy in theirs:
                copy.start()
            for copy in theirs:
                copy.wait()
            for copy in moved:
                copy.start()
            for copy in moved:
                copy.wait()

        @pl.when(flags_ref[2 * side + 1] == 1)
        def _():
            for copy in ours + theirs:
                copy.start()
            for copy in ours + theirs:
                copy.wait()
            for slot in range(4):
                both = own[side, slot].astype(jnp.float32) + extra[side, slot].astype(jnp.float32)
                own[side, slot] = both.astype(jnp.bfloat16)
            for copy in added:
                copy.start()
            for copy in added:
                copy.wait()


def on_device(q_tokens, k_tokens, v_tokens, d_attended, w_out, lengths):
    rows, width = q_tokens.shape[1:]
    count = lax.axis_size("tok")
    norm = 1.0 / math.sqrt(lax.axis_size("dp") * count * rows)
    q, k, v, dy = q_tokens[0], k_tokens[0], v_tokens[0], d_attended[0]
    low = jnp.bfloat16
    vmem, smem, anywhere = (
        pl.BlockSpec(memory_space=space) for space in (pltpu.VMEM, pltpu.SMEM, pl.ANY)
    )
    token_shape = jax.ShapeDtypeStruct((rows, width), low)
    halo_shape = jax.ShapeDtypeStruct((2, 4, BLOCK, width), low)
    parts_shape = jax.ShapeDtypeStruct((2, SIDE, SIDE, PAD, width), low)
    big = 58 * 1024 * 1024

    halo, dm = pl.pallas_call(
        functools.partial(exchange_kernel, count),
        out_shape=(halo_shape, token_shape),
        in_specs=[smem] + [anywhere] * 5,
        out_specs=(anywhere, vmem),
        scratch_shapes=[
            pltpu.VMEM((rows, width), low),
            pltpu.VMEM((width, width), low),
            pltpu.VMEM((2, BLOCK, width), low),
            pltpu.VMEM((2, 2, BLOCK, width), low),
            pltpu.VMEM((2, 2, BLOCK, width), low),
            pltpu.SemaphoreType.DMA((8,)),
            pltpu.SemaphoreType.DMA((2, 4)),
            pltpu.SemaphoreType.DMA((2, 4)),
        ],
        compiler_params=pltpu.CompilerParams(
            collective_id=0, has_side_effects=True, vmem_limit_bytes=big
        ),
        name="exchange",
    )(lengths, q, k, v, dy, w_out)

    slab = pltpu.VMEM((SLOTS * BLOCK, width), low)
    att, gq, gk, gv, ret, gw, flags = pl.pallas_call(
        attention_kernel,
        out_shape=(
            token_shape, token_shape, token_shape, token_shape, halo_shape,
            parts_shape,
            jax.ShapeDtypeStruct((4,), jnp.int32),
        ),
        in_specs=[smem] + [anywhere] * 7,
        out_specs=(anywhere,) * 6 + (smem,),
        scratch_shapes=[slab] * 5
        + [pltpu.VMEM((width, width), low)]
        + [slab] * 5
        + [
            pltpu.VMEM((width + PAD - PART, width), jnp.float32),
            pltpu.VMEM(parts_shape.shape, low),
            pltpu.SMEM((8, 2), jnp.int32),
            pltpu.SemaphoreType.DMA((18,)),
        ],
        compiler_params=pltpu.CompilerParams(vmem_limit_bytes=big),
        name="attention",
    )(lengths, q, k, v, dy, dm, halo, w_out)

    piece = pltpu.VMEM((SIDE - 1, PAD, width), low)
    quarter = pltpu.VMEM((SIDE, SIDE, PAD, width), low)
    dma = pltpu.SemaphoreType.DMA
    back, summed = pl.pallas_call(
        functools.partial(finish_kernel, count),
        out_shape=(halo_shape, jax.ShapeDtypeStruct((PAD, width), low)),
        in_specs=[anywhere] * 2,
        out_specs=(anywhere, vmem),
        scratch_shapes=[
            quarter, quarter, quarter,
            pltpu.VMEM((SIDE - 1, SIDE, PAD, width), low),
            piece, piece,
            pltpu.VMEM((2, PAD, width), low),
            dma((2, 4)), dma((2, 4)), dma, dma((SIDE,)), dma((SIDE,)),
            dma((4, SIDE - 1)), dma((4, SIDE - 1)),
        ],
        compiler_params=pltpu.CompilerParams(
            collective_id=1, has_side_effects=True, vmem_limit_bytes=big
        ),
        name="finish",
    )(ret, gw)

    att, gq, gk, gv, grad_rows = pl.pallas_call(
        functools.partial(settle_kernel, norm),
        out_shape=(token_shape,) * 4 + (jax.ShapeDtypeStruct((PART, width), jnp.float32),),
        in_specs=[smem, vmem] + [anywhere] * 5,
        out_specs=(anywhere,) * 4 + (vmem,),
        scratch_shapes=[
            pltpu.VMEM((2, 4, BLOCK, width), low),
            pltpu.VMEM((2, 4, BLOCK, width), low),
            dma((2, 8)),
        ],
        input_output_aliases={3: 0, 4: 1, 5: 2, 6: 3},
        compiler_params=pltpu.CompilerParams(vmem_limit_bytes=big),
        name="settle",
    )(flags, summed, back, att, gq, gk, gv)
    return (att[None], gq[None], gk[None], gv[None], grad_rows)


def solution(mesh):
    tokens = P("dp", "tok", None)
    return jax.shard_map(
        on_device,
        mesh=mesh,
        in_specs=(tokens, tokens, tokens, tokens, P(), P("dp", None)),
        out_specs=(tokens, tokens, tokens, tokens, P("tok", None)),
        check_vma=False,
    )
```

```python
import functools
import math

import jax
import jax.numpy as jnp
from jax import lax
from jax.experimental import pallas as pl
from jax.experimental.pallas import tpu as pltpu
from jax.sharding import PartitionSpec as P

HEADS = 16
HEAD_DIM = 72
BLOCK = 128
D = 1152
OWN = 4
SLOTS = 8
WINDOW = 256
SCALE = HEAD_DIM ** (-0.5)
EXP2_SCALE = SCALE * math.log2(math.e)
PART = 36
PIECE = 384
PIECES = D // PIECE
PACKED = 112
SIDE = 4
MESH = pl.DeviceIdType.MESH
NN = (((1,), (0,)), ((), ()))
NT = (((1,), (1,)), ((), ()))
TN = (((0,), (0,)), ((), ()))


def dot(a, b, dims):
    return lax.dot_general(a, b, dims, preferred_element_type=jnp.float32)


def boundary(lengths_ref, edge):
    def step(i, carry):
        start, before, after = carry
        end = start + lengths_ref[0, i]
        hit = jnp.logical_and(start < edge, end > edge)
        return (end, jnp.where(hit, edge - start, before), jnp.where(hit, end - edge, after))

    zero = jnp.int32(0)
    _, before, after = lax.fori_loop(0, lengths_ref.shape[1], step, (zero, zero, zero))
    return before, after


def greet(others):
    barrier = pltpu.get_barrier_semaphore()
    for other in others:
        where = other if isinstance(other, dict) else {"tok": other}
        pl.semaphore_signal(barrier, inc=1, device_id=where, device_id_type=MESH)
    pl.semaphore_wait(barrier, len(others))


def ring_neighbours(count):
    me = lax.axis_index("tok")
    return lax.rem(me + count - 1, count), lax.rem(me + 1, count)


def exchange_kernel(
    count, lengths_ref, q_ref, k_ref, v_ref, dy_ref, w_ref, halo_ref, dm_ref,
    dy_buf, w_buf, near_buf, far_buf, pack, load_sem, send_sem, recv_sem,
):
    left, right = ring_neighbours(count)
    first = lax.axis_index("tok") * OWN
    near = [pl.ds(0, BLOCK), pl.ds(3 * BLOCK, BLOCK)]
    far = [pl.ds(BLOCK, BLOCK), pl.ds(2 * BLOCK, BLOCK)]
    loads = []
    for side in range(2):
        loads += [
            (q_ref.at[near[side]], near_buf.at[side]),
            (k_ref.at[far[side]], far_buf.at[side, 0]),
            (v_ref.at[far[side]], far_buf.at[side, 1]),
        ]
    loads += [(dy_ref, dy_buf), (w_ref, w_buf)]
    loads = [pltpu.make_async_copy(a, b, load_sem.at[i]) for i, (a, b) in enumerate(loads)]
    for load in loads:
        load.start()
    greet((left, right))
    copies = []

    def send(side, slot, source):
        copy = pltpu.make_async_remote_copy(
            src_ref=source,
            dst_ref=halo_ref.at[1 - side, slot],
            send_sem=send_sem.at[side, slot],
            recv_sem=recv_sem.at[1 - side, slot],
            device_id={"tok": right if side else left},
            device_id_type=MESH,
        )
        copy.start()
        copies.append(copy)

    for side in range(2):
        send(side, 0, k_ref.at[near[side]])
        send(side, 1, v_ref.at[near[side]])
    for load in loads[:-1]:
        load.wait()
    for side in range(2):
        before, after = boundary(lengths_ref, first + side * OWN)
        shared = jnp.logical_and(before == 2, after == 2)
        pack[side, 0] = jnp.where(shared, far_buf[side, 0], near_buf[side])
        pack[side, 1] = jnp.where(shared, far_buf[side, 1], dy_buf[near[side]])
        send(side, 2, pack.at[side, 0])
        send(side, 3, pack.at[side, 1])
    loads[-1].wait()
    for part in range(OWN):
        rows = slice(part * BLOCK, (part + 1) * BLOCK)
        dm_ref[rows] = dot(dy_buf[rows], w_buf[...], NT).astype(jnp.bfloat16)
    for copy in copies:
        copy.wait()


def attend(q_buf, k_buf, v_buf, dm_buf, mixed, gq, gk, gv, q_at, q_blocks, k_at, k_blocks):
    q_rows = pl.ds(pl.multiple_of(q_at * BLOCK, BLOCK), q_blocks * BLOCK)
    k_rows = pl.ds(pl.multiple_of(k_at * BLOCK, BLOCK), k_blocks * BLOCK)
    lane = lax.broadcasted_iota(jnp.int32, (1, WINDOW), 1)

    group = {1: 8, 2: 4, 3: 2, 4: 2}[k_blocks]

    def several(i, carry):
        heads = []
        for j in range(group):
            at = (group * i + j) * HEAD_DIM
            base = jnp.minimum(at // 128, (D - WINDOW) // 128) * 128
            offset = at - base
            window = pl.ds(pl.multiple_of(base, 128), WINDOW)
            inside = jnp.logical_and(lane >= offset, lane < offset + HEAD_DIM)
            keep = jnp.where(inside, 1.0, 0.0).astype(jnp.bfloat16)
            heads.append((offset, window, keep))
        probs_of, ds_of = [], []
        for offset, window, keep in heads:
            scores = dot(k_buf[k_rows, window] * keep, q_buf[q_rows, window], NT)
            d_probs = dot(v_buf[k_rows, window] * keep, dm_buf[q_rows, window], NT)
            top = jnp.max(scores, axis=0, keepdims=True)
            weights = jnp.exp2((scores - top) * EXP2_SCALE)
            probs = weights * (1.0 / jnp.sum(weights, axis=0, keepdims=True))
            product = probs * d_probs
            delta = jnp.sum(product, axis=0, keepdims=True)
            probs_of.append(probs.astype(jnp.bfloat16))
            ds_of.append((product - probs * delta).astype(jnp.bfloat16))
        news = []
        for (offset, window, keep), p, ds in zip(heads, probs_of, ds_of):
            news.append((
                dot(p, v_buf[k_rows, window], TN), dot(p, dm_buf[q_rows, window], NN),
                dot(ds, k_buf[k_rows, window], TN) * SCALE, dot(ds, q_buf[q_rows, window], NN) * SCALE,
            ))
        for (offset, window, keep), new in zip(heads, news):
            for ref, rows, value in zip((mixed, gv, gq, gk), (q_rows, k_rows, q_rows, k_rows), new):
                old = ref[rows, window]
                ref[rows, window] = jnp.where(lane < offset, old, value.astype(jnp.bfloat16))
        return carry

    lax.fori_loop(0, HEADS // group, several, 0)


def attention_kernel(
    lengths_ref, q_ref, k_ref, v_ref, dm_ref, halo_ref, w_ref,
    mixed_out, gq_out, gk_out, gv_out, ret_out, flags_out,
    q_buf, k_buf, v_buf, dm_buf, w_buf, dy_buf, mixed, gq, gk, gv, att, work, sem,
):
    first = lax.axis_index("tok") * OWN
    last = first + OWN
    own = pl.ds(2 * BLOCK, OWN * BLOCK)

    def block(i):
        return pl.ds(i * BLOCK, BLOCK)

    loads = [
        (q_ref, q_buf.at[own]), (k_ref, k_buf.at[own]), (v_ref, v_buf.at[own]),
        (dm_ref, dm_buf.at[own]), (w_ref, w_buf),
    ]
    for side, (near, far) in enumerate(((1, 0), (6, 7))):
        loads += [
            (halo_ref.at[side, 0], k_buf.at[block(near)]),
            (halo_ref.at[side, 1], v_buf.at[block(near)]),
            (halo_ref.at[side, 2], q_buf.at[block(near)]),
            (halo_ref.at[side, 2], k_buf.at[block(far)]),
            (halo_ref.at[side, 3], dy_buf.at[side]),
            (halo_ref.at[side, 3], v_buf.at[block(far)]),
        ]
    copies = [pltpu.make_async_copy(a, b, sem.at[i]) for i, (a, b) in enumerate(loads)]
    for copy in copies:
        copy.start()

    l_before, l_after = boundary(lengths_ref, first)
    r_before, r_after = boundary(lengths_ref, last)
    l_shared = jnp.logical_and(l_before == 2, l_after == 2)
    r_shared = jnp.logical_and(r_before == 2, r_after == 2)
    l_away = l_after == 1
    l_here = jnp.logical_and(l_before == 1, l_after > 1)
    r_here = r_after == 1
    r_away = jnp.logical_and(r_before == 1, r_after > 1)
    for i, flag in enumerate((l_away, l_shared, r_away, r_shared)):
        flags_out[i] = flag.astype(jnp.int32)

    def collect(i, carry):
        start, number = carry
        end = start + lengths_ref[0, i]
        on_left = jnp.logical_and(start < first, end > first)
        on_right = jnp.logical_and(start < last, end > last)
        within = jnp.logical_and(start >= first, end <= last)
        mine = jnp.logical_or(
            within,
            jnp.logical_or(
                jnp.logical_and(on_left, jnp.logical_not(l_away)),
                jnp.logical_and(on_right, jnp.logical_not(r_away)),
            ),
        )
        shared = jnp.logical_or(
            jnp.logical_and(on_left, l_shared), jnp.logical_and(on_right, r_shared)
        )

        @pl.when(mine)
        def _():
            work[number, 0] = jnp.where(shared, 5, end - start)
            work[number, 1] = start - first + 2

        return end, number + mine.astype(jnp.int32)

    _, number = lax.fori_loop(
        0, lengths_ref.shape[1], collect, (jnp.int32(0), jnp.int32(0))
    )
    for copy in copies:
        copy.wait()

    for side, (here, slot) in enumerate(((l_here, 1), (r_here, 6))):
        @pl.when(here)
        def _():
            dm_buf[block(slot)] = dot(dy_buf[side], w_buf[...], NT).astype(jnp.bfloat16)

    bufs = (q_buf, k_buf, v_buf, dm_buf, mixed, gq, gk, gv)

    def image(i, carry):
        kind, at = work[i, 0], work[i, 1]
        for blocks in range(1, OWN + 1):
            @pl.when(kind == blocks)
            def _():
                attend(*bufs, at, blocks, at, blocks)

        @pl.when(kind == 5)
        def _():
            attend(*bufs, jnp.where(at == 0, 2, 4), 2, at, 4)

        return carry

    lax.fori_loop(0, number, image, 0)

    idle = (
        (jnp.logical_not(l_here), 1), (l_away, 2), (r_away, 5), (jnp.logical_not(r_here), 6)
    )
    for flag, slot in idle:
        @pl.when(flag)
        def _():
            mixed[block(slot)] = jnp.zeros((BLOCK, D), jnp.bfloat16)

    stores = [
        (mixed.at[pl.ds(BLOCK, 6 * BLOCK)], mixed_out),
        (gq.at[own], gq_out), (gk.at[own], gk_out), (gv.at[own], gv_out),
    ]
    for side, near in enumerate((1, 6)):
        stores += [
            (gk.at[block(near)], ret_out.at[side, 0]), (gv.at[block(near)], ret_out.at[side, 1]),
        ]
    outs = [pltpu.make_async_copy(a, b, sem.at[i]) for i, (a, b) in enumerate(stores)]
    for copy in outs:
        copy.start()
    for side, (here, slot) in enumerate(((l_here, 1), (r_here, 6))):
        @pl.when(here)
        def _():
            att[side] = dot(mixed[block(slot)], w_buf[...], NN).astype(jnp.bfloat16)

    for side, (near, far, shared) in enumerate(((1, 0, l_shared), (6, 7, r_shared))):
        choices = (
            (gk.at[block(far)], gq.at[block(near)]), (gv.at[block(far)], att.at[side])
        )
        for at, (if_shared, if_moved) in enumerate(choices):
            index = len(stores) + 2 * side + at
            to = ret_out.at[side, 2 + at]

            @pl.when(shared)
            def _():
                pltpu.make_async_copy(if_shared, to, sem.at[index]).start()

            @pl.when(jnp.logical_not(shared))
            def _():
                pltpu.make_async_copy(if_moved, to, sem.at[index]).start()

    for side in range(2):
        for at in range(2):
            index = len(stores) + 2 * side + at
            pltpu.make_async_copy(
                gk.at[block(0)], ret_out.at[side, 2 + at], sem.at[index]
            ).wait()
    for copy in outs:
        copy.wait()


def finish_kernel(
    count, ret_ref, mixed_ref, dy_ref, halo_ref, w_ref, back_ref, sum_ref, att_ref,
    mixed, dy, w_buf, acc, stage, parts, sibling, total, second, half, third, whole, fourth, fifth,
    load_sem, ret_send, ret_recv, one_send, one_recv, sends, recvs,
):
    left, right = ring_neighbours(count)
    me, y = lax.axis_index("tok"), lax.axis_index("dp")
    core, z, x = lax.rem(me, 2), lax.rem(me // 2, SIDE), me // (2 * SIDE)
    loads = [
        (mixed_ref, mixed),
        (halo_ref.at[0, 3], dy.at[pl.ds(0, BLOCK)]),
        (dy_ref, dy.at[pl.ds(BLOCK, OWN * BLOCK)]),
        (halo_ref.at[1, 3], dy.at[pl.ds((OWN + 1) * BLOCK, BLOCK)]),
        (w_ref, w_buf),
    ]
    loads = [pltpu.make_async_copy(a, b, load_sem.at[i]) for i, (a, b) in enumerate(loads)]
    for load in loads:
        load.start()

    def device(x, y, z, core):
        return {"dp": y, "tok": (x * SIDE + z) * 2 + core}

    def turned(at, step):
        return lax.rem(at + step, SIDE)

    other = device(x, y, z, 1 - core)
    steps = range(1, SIDE)
    along_x = [device(turned(x, step), y, z, core) for step in steps]
    along_y = [device(x, turned(y, step), z, core) for step in steps]
    along_z = [device(x, y, turned(z, step), core) for step in steps]
    greet([left, right, other] + along_x + along_y + along_z)

    def remote(source, landing, send_sem, recv_sem, where):
        return pltpu.make_async_remote_copy(
            src_ref=source, dst_ref=landing, send_sem=send_sem, recv_sem=recv_sem,
            device_id=where, device_id_type=MESH,
        )

    copies = []
    for side in range(2):
        for slot in range(4):
            copy = remote(
                ret_ref.at[side, slot], back_ref.at[1 - side, slot],
                ret_send.at[side, slot], ret_recv.at[1 - side, slot],
                {"tok": right if side else left},
            )
            copy.start()
            copies.append(copy)

    for load in loads[:-1]:
        load.wait()
    stage[...] = jnp.zeros_like(stage)
    one = []
    for piece in range(PIECES):
        columns = slice(piece * PIECE, (piece + 1) * PIECE)

        def weight(i, carry):
            lanes = pl.ds(pl.multiple_of(i * 128, 128), 128)
            acc[lanes] = dot(mixed[:, lanes], dy[:, columns], TN)
            return carry

        lax.fori_loop(0, D // 128, weight, 0)
        for part in range(D // PART):
            px, pz, pcore = part // 8, part // 2 % 4, part % 2
            place = (pz, px) if pcore else (px, pz)
            for tile in range(PIECE // 128):
                stage[tile * PART : (tile + 1) * PART] = acc[
                    part * PART : (part + 1) * PART, tile * 128 : (tile + 1) * 128
                ]
            parts[piece, pcore, place[0], place[1]] = stage[...].astype(jnp.bfloat16)
        copy = remote(
            parts.at[piece, 1 - core], sibling.at[piece], one_send.at[piece], one_recv.at[piece],
            other,
        )
        copy.start()
        one.append(copy)

    def spread(stage_at, piece, source, landing, x_axis):
        at = jnp.where(x_axis, x, y)
        started = []
        for step in steps:
            there = turned(at, step)
            where = device(jnp.where(x_axis, there, x), jnp.where(x_axis, y, there), z, core)
            copy = remote(
                source.at[there], landing.at[step - 1],
                sends.at[stage_at, piece, step - 1], recvs.at[stage_at, piece, step - 1], where,
            )
            copy.start()
            started.append(copy)
        return at, started

    def add(*values):
        result = values[0].astype(jnp.float32)
        for value in values[1:]:
            result = result + value.astype(jnp.float32)
        return result.astype(jnp.bfloat16)

    twos = []
    for piece in range(PIECES):
        one[piece].wait()
        for row in range(SIDE):
            total[piece, row] = add(parts[piece, core, row], sibling[piece, row])
        twos.append(spread(0, piece, total.at[piece], second.at[piece], core == 0))

    loads[-1].wait()
    for part in range(OWN):
        rows = slice(part * BLOCK, (part + 1) * BLOCK)
        ours = mixed[(part + 1) * BLOCK : (part + 2) * BLOCK]
        att_ref[rows] = dot(ours, w_buf[...], NN).astype(jnp.bfloat16)

    threes = []
    for piece in range(PIECES):
        at, started = twos[piece]
        for copy in started:
            copy.wait()
        half[piece] = add(total[piece, at], *[second[piece, step - 1] for step in steps])
        threes.append(spread(1, piece, half.at[piece], third.at[piece], core == 1))

    gap = lax.rem(z - y + SIDE, SIDE)

    def to_plane(piece, step):
        return remote(
            whole.at[piece], fourth.at[piece, step - 1],
            sends.at[2, piece, step - 1], recvs.at[2, piece, step - 1],
            device(x, y, turned(z, SIDE - step), core),
        )

    def to_row(piece, step):
        return remote(
            fifth.at[0, piece], fifth.at[1, piece],
            sends.at[3, piece, step - 1], recvs.at[3, piece, 0],
            device(x, turned(y, step), z, core),
        )

    for piece in range(PIECES):
        at, started = threes[piece]
        for copy in started:
            copy.wait()
        whole[piece] = add(half[piece, at], *[third[piece, step - 1] for step in steps])
        for step in steps:
            @pl.when(gap == step)
            def _():
                to_plane(piece, step).start()

    @pl.when(gap == 0)
    def _():
        for piece in range(PIECES):
            for step in steps:
                to_plane(piece, step).wait_recv()
            fifth[0, piece] = add(whole[piece], *[fourth[piece, step - 1] for step in steps])
            for step in steps:
                to_row(piece, step).start()
        for piece in range(PIECES):
            for step in steps:
                to_row(piece, step).wait_send()
        sum_ref[...] = fifth[0]

    @pl.when(gap != 0)
    def _():
        for piece in range(PIECES):
            to_row(piece, 1).wait_recv()
        sum_ref[...] = fifth[1]

    for piece in range(PIECES):
        for step in steps:
            @pl.when(gap == step)
            def _():
                to_plane(piece, step).wait_send()

    for copy in copies:
        copy.wait()


def settle_kernel(
    norm, flags_ref, sum_ref, back_ref, att_in, gq_in, gk_in, gv_in,
    att_out, gq_out, gk_out, gv_out, rows_ref, own, extra, sem,
):
    def block(i):
        return pl.ds(i * BLOCK, BLOCK)

    sides = []
    for side, (near, far) in enumerate(((0, 1), (3, 2))):
        parts = ((gk_out, near, 0), (gv_out, near, 1), (gk_out, far, 2), (gv_out, far, 3))
        ours = [
            pltpu.make_async_copy(out.at[block(at)], own.at[side, slot], sem.at[side, slot])
            for out, at, slot in parts
        ]
        theirs = [
            pltpu.make_async_copy(
                back_ref.at[side, slot], extra.at[side, slot], sem.at[side, 4 + slot]
            )
            for slot in range(4)
        ]
        moved = [
            pltpu.make_async_copy(extra.at[side, slot], out.at[block(near)], sem.at[side, slot])
            for slot, out in enumerate((gk_out, gv_out, gq_out, att_out))
        ]
        added = [
            pltpu.make_async_copy(own.at[side, slot], out.at[block(at)], sem.at[side, slot])
            for out, at, slot in parts
        ]
        away, shared = flags_ref[2 * side] == 1, flags_ref[2 * side + 1] == 1
        sides.append((side, ours, theirs, moved, added, away, shared))

    for side, ours, theirs, moved, added, away, shared in sides:
        for copy in theirs:
            copy.start()

        @pl.when(shared)
        def _():
            for copy in ours:
                copy.start()

    for piece in range(PIECES):
        for tile in range(PIECE // 128):
            lanes = slice(piece * PIECE + tile * 128, piece * PIECE + (tile + 1) * 128)
            part = sum_ref[piece].astype(jnp.float32)[tile * PART : (tile + 1) * PART]
            rows_ref[:, lanes] = part * norm

    for side, ours, theirs, moved, added, away, shared in sides:
        for copy in theirs:
            copy.wait()

        @pl.when(away)
        def _():
            for copy in moved:
                copy.start()

        @pl.when(shared)
        def _():
            for slot in range(4):
                ours[slot].wait()
                both = own[side, slot].astype(jnp.float32) + extra[side, slot].astype(jnp.float32)
                own[side, slot] = both.astype(jnp.bfloat16)
                added[slot].start()

    for side, ours, theirs, moved, added, away, shared in sides:
        @pl.when(jnp.logical_or(away, shared))
        def _():
            for copy in added:
                copy.wait()


def on_device(q_tokens, k_tokens, v_tokens, d_attended, w_out, lengths):
    rows, width = q_tokens.shape[1:]
    count = lax.axis_size("tok")
    norm = 1.0 / math.sqrt(lax.axis_size("dp") * count * rows)
    q, k, v, dy = q_tokens[0], k_tokens[0], v_tokens[0], d_attended[0]
    low = jnp.bfloat16
    vmem, smem, anywhere = (
        pl.BlockSpec(memory_space=space) for space in (pltpu.VMEM, pltpu.SMEM, pl.ANY)
    )
    token_shape = jax.ShapeDtypeStruct((rows, width), low)
    halo_shape = jax.ShapeDtypeStruct((2, 4, BLOCK, width), low)
    big = 58 * 1024 * 1024

    halo, dm = pl.pallas_call(
        functools.partial(exchange_kernel, count),
        out_shape=(halo_shape, token_shape),
        in_specs=[smem] + [anywhere] * 5,
        out_specs=(anywhere, vmem),
        scratch_shapes=[
            pltpu.VMEM((rows, width), low),
            pltpu.VMEM((width, width), low),
            pltpu.VMEM((2, BLOCK, width), low),
            pltpu.VMEM((2, 2, BLOCK, width), low),
            pltpu.VMEM((2, 2, BLOCK, width), low),
            pltpu.SemaphoreType.DMA((8,)),
            pltpu.SemaphoreType.DMA((2, 4)),
            pltpu.SemaphoreType.DMA((2, 4)),
        ],
        compiler_params=pltpu.CompilerParams(
            collective_id=0, has_side_effects=True, vmem_limit_bytes=big
        ),
        name="exchange",
    )(lengths, q, k, v, dy, w_out)

    dma = pltpu.SemaphoreType.DMA
    slab = pltpu.VMEM((SLOTS * BLOCK, width), low)
    square = pltpu.VMEM((width, width), low)
    sides = pltpu.VMEM((2, BLOCK, width), low)
    mixed_shape = jax.ShapeDtypeStruct(((OWN + 2) * BLOCK, width), low)
    mixed, gq, gk, gv, ret, flags = pl.pallas_call(
        attention_kernel,
        out_shape=(
            mixed_shape, token_shape, token_shape, token_shape, halo_shape,
            jax.ShapeDtypeStruct((4,), jnp.int32),
        ),
        in_specs=[smem] + [anywhere] * 6,
        out_specs=(anywhere,) * 5 + (smem,),
        scratch_shapes=[slab] * 4 + [square, sides] + [slab] * 4
        + [sides, pltpu.SMEM((8, 2), jnp.int32), dma((17,))],
        compiler_params=pltpu.CompilerParams(vmem_limit_bytes=big),
        name="attention",
    )(lengths, q, k, v, dm, halo, w_out)

    sum_shape = jax.ShapeDtypeStruct((PIECES, PACKED, 128), low)

    def pieces(*sizes):
        return pltpu.VMEM((PIECES, *sizes, PACKED, 128), low)

    slab = pltpu.VMEM(mixed_shape.shape, low)
    back, summed, att = pl.pallas_call(
        functools.partial(finish_kernel, count),
        out_shape=(halo_shape, sum_shape, token_shape),
        in_specs=[anywhere] * 5,
        out_specs=(anywhere, vmem, vmem),
        scratch_shapes=[
            slab, slab, square,
            pltpu.VMEM((width, PIECE), jnp.float32),
            pltpu.VMEM((PACKED, 128), jnp.float32),
            pieces(2, SIDE, SIDE), pieces(SIDE, SIDE), pieces(SIDE, SIDE),
            pieces(SIDE - 1, SIDE), pieces(SIDE), pieces(SIDE - 1),
            pieces(), pieces(SIDE - 1),
            pltpu.VMEM((2, PIECES, PACKED, 128), low),
            dma((5,)), dma((2, 4)), dma((2, 4)), dma((PIECES,)), dma((PIECES,)),
            dma((4, PIECES, SIDE - 1)), dma((4, PIECES, SIDE - 1)),
        ],
        compiler_params=pltpu.CompilerParams(
            collective_id=1, has_side_effects=True, vmem_limit_bytes=big
        ),
        name="finish",
    )(ret, mixed, dy, halo, w_out)

    att, gq, gk, gv, grad_rows = pl.pallas_call(
        functools.partial(settle_kernel, norm),
        out_shape=(token_shape,) * 4 + (jax.ShapeDtypeStruct((PART, width), jnp.float32),),
        in_specs=[smem, vmem] + [anywhere] * 5,
        out_specs=(anywhere,) * 4 + (vmem,),
        scratch_shapes=[
            pltpu.VMEM((2, 4, BLOCK, width), low),
            pltpu.VMEM((2, 4, BLOCK, width), low),
            dma((2, 8)),
        ],
        input_output_aliases={3: 0, 4: 1, 5: 2, 6: 3},
        compiler_params=pltpu.CompilerParams(vmem_limit_bytes=big),
        name="settle",
    )(flags, summed, back, att, gq, gk, gv)
    return (att[None], gq[None], gk[None], gv[None], grad_rows)


def solution(mesh):
    tokens = P("dp", "tok", None)
    return jax.shard_map(
        on_device,
        mesh=mesh,
        in_specs=(tokens, tokens, tokens, tokens, P(), P("dp", None)),
        out_specs=(tokens, tokens, tokens, tokens, P("tok", None)),
        check_vma=False,
    )
```

```python
import functools
import math

import jax
import jax.numpy as jnp
from jax import lax
from jax.experimental import pallas as pl
from jax.experimental.pallas import tpu as pltpu
from jax.sharding import PartitionSpec as P

HEADS = 16
HEAD_DIM = 72
BLOCK = 128
D = 1152
OWN = 4
SLOTS = 8
WINDOW = 256
SCALE = HEAD_DIM ** (-0.5)
EXP2_SCALE = SCALE * math.log2(math.e)
PART = 36
PIECE = 384
PIECES = D // PIECE
PACKED = 112
SIDE = 4
MESH = pl.DeviceIdType.MESH
NN = (((1,), (0,)), ((), ()))
NT = (((1,), (1,)), ((), ()))
TN = (((0,), (0,)), ((), ()))


def dot(a, b, dims):
    return lax.dot_general(a, b, dims, preferred_element_type=jnp.float32)


def boundary(lengths_ref, edge):
    def step(i, carry):
        start, before, after = carry
        end = start + lengths_ref[0, i]
        hit = jnp.logical_and(start < edge, end > edge)
        return (end, jnp.where(hit, edge - start, before), jnp.where(hit, end - edge, after))

    zero = jnp.int32(0)
    _, before, after = lax.fori_loop(0, lengths_ref.shape[1], step, (zero, zero, zero))
    return before, after


def greet(others):
    for other in others:
        where = other if isinstance(other, dict) else {"tok": other}
        pl.semaphore_signal(
            pltpu.get_barrier_semaphore(), inc=1, device_id=where, device_id_type=MESH
        )


def meet(others):
    pl.semaphore_wait(pltpu.get_barrier_semaphore(), len(others))


def ring_neighbours(count):
    me = lax.axis_index("tok")
    return lax.rem(me + count - 1, count), lax.rem(me + 1, count)


def exchange_kernel(
    count, lengths_ref, q_ref, k_ref, v_ref, dy_ref, w_ref, halo_ref, dm_ref,
    dy_buf, w_buf, near_buf, far_buf, pack, load_sem, send_sem, recv_sem,
):
    left, right = ring_neighbours(count)
    first = lax.axis_index("tok") * OWN
    near = [pl.ds(0, BLOCK), pl.ds(3 * BLOCK, BLOCK)]
    far = [pl.ds(BLOCK, BLOCK), pl.ds(2 * BLOCK, BLOCK)]
    loads = []
    for side in range(2):
        loads += [
            (q_ref.at[near[side]], near_buf.at[side]),
            (k_ref.at[far[side]], far_buf.at[side, 0]),
            (v_ref.at[far[side]], far_buf.at[side, 1]),
        ]
    loads += [(dy_ref, dy_buf), (w_ref, w_buf)]
    loads = [pltpu.make_async_copy(a, b, load_sem.at[i]) for i, (a, b) in enumerate(loads)]
    for load in loads:
        load.start()
    greet((left, right))
    meet((left, right))
    copies = []

    def send(side, slot, source):
        copy = pltpu.make_async_remote_copy(
            src_ref=source,
            dst_ref=halo_ref.at[1 - side, slot],
            send_sem=send_sem.at[side, slot],
            recv_sem=recv_sem.at[1 - side, slot],
            device_id={"tok": right if side else left},
            device_id_type=MESH,
        )
        copy.start()
        copies.append(copy)

    for side in range(2):
        send(side, 0, k_ref.at[near[side]])
        send(side, 1, v_ref.at[near[side]])
    for load in loads[:-1]:
        load.wait()
    for side in range(2):
        before, after = boundary(lengths_ref, first + side * OWN)
        shared = jnp.logical_and(before == 2, after == 2)
        pack[side, 0] = jnp.where(shared, far_buf[side, 0], near_buf[side])
        pack[side, 1] = jnp.where(shared, far_buf[side, 1], dy_buf[near[side]])
        send(side, 2, pack.at[side, 0])
        send(side, 3, pack.at[side, 1])
    loads[-1].wait()
    for part in range(OWN):
        rows = slice(part * BLOCK, (part + 1) * BLOCK)
        dm_ref[rows] = dot(dy_buf[rows], w_buf[...], NT).astype(jnp.bfloat16)
    for copy in copies:
        copy.wait()


def attend(q_buf, k_buf, v_buf, dm_buf, mixed, gq, gk, gv, q_at, q_blocks, k_at, k_blocks):
    q_rows = pl.ds(pl.multiple_of(q_at * BLOCK, BLOCK), q_blocks * BLOCK)
    k_rows = pl.ds(pl.multiple_of(k_at * BLOCK, BLOCK), k_blocks * BLOCK)
    lane = lax.broadcasted_iota(jnp.int32, (1, WINDOW), 1)

    group = {1: 8, 2: 4, 3: 2, 4: 2}[k_blocks]

    def several(i, carry):
        heads = []
        for j in range(group):
            at = (group * i + j) * HEAD_DIM
            base = jnp.minimum(at // 128, (D - WINDOW) // 128) * 128
            offset = at - base
            window = pl.ds(pl.multiple_of(base, 128), WINDOW)
            inside = jnp.logical_and(lane >= offset, lane < offset + HEAD_DIM)
            keep = jnp.where(inside, 1.0, 0.0).astype(jnp.bfloat16)
            heads.append((offset, window, keep))
        probs_of, ds_of = [], []
        for offset, window, keep in heads:
            scores = dot(k_buf[k_rows, window] * keep, q_buf[q_rows, window], NT)
            d_probs = dot(v_buf[k_rows, window] * keep, dm_buf[q_rows, window], NT)
            top = jnp.max(scores, axis=0, keepdims=True)
            weights = jnp.exp2((scores - top) * EXP2_SCALE)
            probs = weights * (1.0 / jnp.sum(weights, axis=0, keepdims=True))
            product = probs * d_probs
            delta = jnp.sum(product, axis=0, keepdims=True)
            probs_of.append(probs.astype(jnp.bfloat16))
            ds_of.append((product - probs * delta).astype(jnp.bfloat16))
        news = []
        for (offset, window, keep), p, ds in zip(heads, probs_of, ds_of):
            news.append((
                dot(p, v_buf[k_rows, window], TN), dot(p, dm_buf[q_rows, window], NN),
                dot(ds, k_buf[k_rows, window], TN) * SCALE, dot(ds, q_buf[q_rows, window], NN) * SCALE,
            ))
        for (offset, window, keep), new in zip(heads, news):
            for ref, rows, value in zip((mixed, gv, gq, gk), (q_rows, k_rows, q_rows, k_rows), new):
                old = ref[rows, window]
                ref[rows, window] = jnp.where(lane < offset, old, value.astype(jnp.bfloat16))
        return carry

    lax.fori_loop(0, HEADS // group, several, 0)


def attention_kernel(
    lengths_ref, q_ref, k_ref, v_ref, dm_ref, halo_ref, w_ref,
    mixed_out, gq_out, gk_out, gv_out, ret_out, flags_out,
    q_buf, k_buf, v_buf, dm_buf, w_buf, dy_buf, mixed, gq, gk, gv, att, work, sem, halo_sem, store_sem,
):
    first = lax.axis_index("tok") * OWN
    last = first + OWN
    own = pl.ds(2 * BLOCK, OWN * BLOCK)

    def block(i):
        return pl.ds(i * BLOCK, BLOCK)

    loads = [
        (q_ref, q_buf.at[own]), (k_ref, k_buf.at[own]), (v_ref, v_buf.at[own]),
        (dm_ref, dm_buf.at[own]), (w_ref, w_buf),
    ]
    loads = [pltpu.make_async_copy(a, b, sem.at[i]) for i, (a, b) in enumerate(loads)]
    w_load = loads.pop()
    for load in loads:
        load.start()

    l_before, l_after = boundary(lengths_ref, first)
    r_before, r_after = boundary(lengths_ref, last)
    l_shared = jnp.logical_and(l_before == 2, l_after == 2)
    r_shared = jnp.logical_and(r_before == 2, r_after == 2)
    l_away = l_after == 1
    l_here = jnp.logical_and(l_before == 1, l_after > 1)
    r_here = r_after == 1
    r_away = jnp.logical_and(r_before == 1, r_after > 1)
    for i, flag in enumerate((l_away, l_shared, r_away, r_shared)):
        flags_out[i] = flag.astype(jnp.int32)

    halo_loads = []
    for side, (near, far, here, shared) in enumerate(
        ((1, 0, l_here, l_shared), (6, 7, r_here, r_shared))
    ):
        def load(slot, to, side=side):
            return pltpu.make_async_copy(halo_ref.at[side, slot], to, halo_sem.at[side, slot])

        both = [load(0, k_buf.at[block(near)]), load(1, v_buf.at[block(near)])]
        if_here = [load(2, q_buf.at[block(near)]), load(3, dy_buf.at[side])]
        if_shared = [load(2, k_buf.at[block(far)]), load(3, v_buf.at[block(far)])]
        halo_loads += [(here, both + if_here), (shared, both + if_shared)]
    for flag, some in halo_loads:
        @pl.when(flag)
        def _():
            for load in some:
                load.start()

    w_load.start()

    def collect(i, carry):
        start, number = carry
        end = start + lengths_ref[0, i]
        on_left = jnp.logical_and(start < first, end > first)
        on_right = jnp.logical_and(start < last, end > last)
        within = jnp.logical_and(start >= first, end <= last)
        mine = jnp.logical_or(
            within,
            jnp.logical_or(
                jnp.logical_and(on_left, jnp.logical_not(l_away)),
                jnp.logical_and(on_right, jnp.logical_not(r_away)),
            ),
        )
        shared = jnp.logical_or(
            jnp.logical_and(on_left, l_shared), jnp.logical_and(on_right, r_shared)
        )

        @pl.when(mine)
        def _():
            work[number, 0] = jnp.where(shared, 5, end - start)
            work[number, 1] = start - first + 2

        return end, number + mine.astype(jnp.int32)

    _, number = lax.fori_loop(
        0, lengths_ref.shape[1], collect, (jnp.int32(0), jnp.int32(0))
    )
    for load in loads:
        load.wait()
    for flag, some in halo_loads:
        @pl.when(flag)
        def _():
            for load in some:
                load.wait()

    w_load.wait()
    for side, (here, slot) in enumerate(((l_here, 1), (r_here, 6))):
        @pl.when(here)
        def _():
            dm_buf[block(slot)] = dot(dy_buf[side], w_buf[...], NT).astype(jnp.bfloat16)

    bufs = (q_buf, k_buf, v_buf, dm_buf, mixed, gq, gk, gv)

    def store(index, slot):
        if index == 0:
            return pltpu.make_async_copy(
                mixed.at[rows_of(slot)], mixed_out.at[rows_of(slot - 1)], store_sem.at[0, slot]
            )
        ref, out = ((gq, gq_out), (gk, gk_out), (gv, gv_out))[index - 1]
        return pltpu.make_async_copy(
            ref.at[rows_of(slot)], out.at[rows_of(slot - 2)], store_sem.at[index, slot]
        )

    def rows_of(slot):
        return pl.ds(pl.multiple_of(slot * BLOCK, BLOCK), BLOCK)

    def store_all(slot, indices):
        for index in indices:
            if index == 0:
                store(0, slot).start()
            else:
                @pl.when(jnp.logical_and(slot >= 2, slot < 2 + OWN))
                def _():
                    store(index, slot).start()

    def image(i, carry):
        kind, at = work[i, 0], work[i, 1]
        for blocks in range(1, OWN + 1):
            @pl.when(kind == blocks)
            def _():
                attend(*bufs, at, blocks, at, blocks)
                for j in range(blocks):
                    store_all(at + j, range(4))

        @pl.when(kind == 5)
        def _():
            q_at = jnp.where(at == 0, 2, 4)
            attend(*bufs, q_at, 2, at, 4)
            for j in range(2):
                store_all(q_at + j, range(4))

        return carry

    lax.fori_loop(0, number, image, 0)

    idle = (
        (jnp.logical_not(l_here), 1), (l_away, 2), (r_away, 5), (jnp.logical_not(r_here), 6)
    )
    for flag, slot in idle:
        @pl.when(flag)
        def _():
            mixed[block(slot)] = jnp.zeros((BLOCK, D), jnp.bfloat16)
            store_all(jnp.int32(slot), range(4))

    def give(side, slot, source):
        return pltpu.make_async_copy(source, ret_out.at[side, slot], halo_sem.at[side, slot])

    gives = []
    for side, (near, far, here, shared) in enumerate(
        ((1, 0, l_here, l_shared), (6, 7, r_here, r_shared))
    ):
        both = [give(side, 0, gk.at[block(near)]), give(side, 1, gv.at[block(near)])]
        if_here = [give(side, 2, gq.at[block(near)]), give(side, 3, att.at[side])]
        if_shared = [give(side, 2, gk.at[block(far)]), give(side, 3, gv.at[block(far)])]

        @pl.when(here)
        def _():
            for copy in both + if_here[:1]:
                copy.start()
            att[side] = dot(mixed[block(near)], w_buf[...], NN).astype(jnp.bfloat16)
            if_here[1].start()

        @pl.when(shared)
        def _():
            for copy in both + if_shared:
                copy.start()

        gives += [(here, both + if_here), (shared, both + if_shared)]
    for flag, some in gives:
        @pl.when(flag)
        def _():
            for copy in some:
                copy.wait()

    for slot in range(1, 3 + OWN):
        for index in range(4):
            if index == 0 or 2 <= slot < 2 + OWN:
                store(index, slot).wait()


def finish_kernel(
    count, ret_ref, mixed_ref, dy_ref, halo_ref, w_ref, back_ref, sum_ref, att_ref,
    mixed, turned_mixed, dy, w_buf, att, acc, stage, parts, sibling, total, second, half, third, whole, fourth, fifth,
    load_sem, ret_send, ret_recv, one_send, one_recv, sends, recvs,
):
    left, right = ring_neighbours(count)
    me, y = lax.axis_index("tok"), lax.axis_index("dp")
    core, z, x = lax.rem(me, 2), lax.rem(me // 2, SIDE), me // (2 * SIDE)
    loads = [
        (mixed_ref, mixed),
        (halo_ref.at[0, 3], dy.at[pl.ds(0, BLOCK)]),
        (dy_ref, dy.at[pl.ds(BLOCK, OWN * BLOCK)]),
        (halo_ref.at[1, 3], dy.at[pl.ds((OWN + 1) * BLOCK, BLOCK)]),
        (w_ref, w_buf),
    ]
    loads = [pltpu.make_async_copy(a, b, load_sem.at[i]) for i, (a, b) in enumerate(loads)]
    for load in loads:
        load.start()

    def device(x, y, z, core):
        return {"dp": y, "tok": (x * SIDE + z) * 2 + core}

    def turned(at, step):
        return lax.rem(at + step, SIDE)

    other = device(x, y, z, 1 - core)
    steps = range(1, SIDE)
    along_x = [device(turned(x, step), y, z, core) for step in steps]
    along_y = [device(x, turned(y, step), z, core) for step in steps]
    along_z = [device(x, y, turned(z, step), core) for step in steps]
    others = [left, right, other] + along_x + along_y + along_z
    greet(others)
    copies = []

    def remote(source, landing, send_sem, recv_sem, where):
        return pltpu.make_async_remote_copy(
            src_ref=source, dst_ref=landing, send_sem=send_sem, recv_sem=recv_sem,
            device_id=where, device_id_type=MESH,
        )

    def send(*args):
        copy = remote(*args)
        copy.start()
        copies.append(copy)
        return copy

    for load in loads[:-1]:
        load.wait()
    for tile in range(D // 128):
        lanes = slice(tile * 128, (tile + 1) * 128)
        turned_mixed[lanes] = mixed[:, lanes].T
    stage[...] = jnp.zeros_like(stage)

    def product(piece):
        columns = slice(piece * PIECE, (piece + 1) * PIECE)

        def weight(i, carry):
            at = pl.ds(pl.multiple_of(i * PIECE, PIECE), PIECE)
            acc[at] = dot(turned_mixed[at], dy[:, columns], NN)
            return carry

        lax.fori_loop(0, D // PIECE, weight, 0)
        for part in range(D // PART):
            px, pz, pcore = part // 8, part // 2 % 4, part % 2
            place = (pz, px) if pcore else (px, pz)
            for tile in range(PIECE // 128):
                stage[tile * PART : (tile + 1) * PART] = acc[
                    part * PART : (part + 1) * PART, tile * 128 : (tile + 1) * 128
                ]
            parts[piece, pcore, place[0], place[1]] = stage[...].astype(jnp.bfloat16)

    def to_sibling(piece):
        return send(
            parts.at[piece, 1 - core], sibling.at[piece], one_send.at[piece], one_recv.at[piece],
            other,
        )

    def spread(stage_at, piece, source, landing, x_axis):
        at = jnp.where(x_axis, x, y)
        started = []
        for step in steps:
            there = turned(at, step)
            where = device(jnp.where(x_axis, there, x), jnp.where(x_axis, y, there), z, core)
            started.append(send(
                source.at[there], landing.at[step - 1],
                sends.at[stage_at, piece, step - 1], recvs.at[stage_at, piece, step - 1], where,
            ))
        return at, started

    def add(*values):
        result = values[0].astype(jnp.float32)
        for value in values[1:]:
            result = result + value.astype(jnp.float32)
        return result.astype(jnp.bfloat16)

    twos, threes = [], []

    def second_stage(piece):
        one[piece].wait_recv()
        for row in range(SIDE):
            total[piece, row] = add(parts[piece, core, row], sibling[piece, row])
        twos.append(spread(0, piece, total.at[piece], second.at[piece], core == 0))

    def third_stage(piece):
        at, started = twos[piece]
        for copy in started:
            copy.wait_recv()
        half[piece] = add(total[piece, at], *[second[piece, step - 1] for step in steps])
        threes.append(spread(1, piece, half.at[piece], third.at[piece], core == 1))

    product(0)
    meet(others)
    one = [to_sibling(0)]
    returns = []
    for side in range(2):
        for slot in range(4):
            returns.append(send(
                ret_ref.at[side, slot], back_ref.at[1 - side, slot],
                ret_send.at[side, slot], ret_recv.at[1 - side, slot],
                {"tok": right if side else left},
            ))
    for piece in range(1, PIECES):
        product(piece)
        one.append(to_sibling(piece))
        second_stage(piece - 1)
    second_stage(PIECES - 1)

    loads[-1].wait()
    for part in range(OWN):
        rows = slice(part * BLOCK, (part + 1) * BLOCK)
        ours = mixed[(part + 1) * BLOCK : (part + 2) * BLOCK]
        att[rows] = dot(ours, w_buf[...], NN).astype(jnp.bfloat16)
    att_store = pltpu.make_async_copy(att, att_ref, load_sem.at[0])
    att_store.start()
    for piece in range(PIECES):
        third_stage(piece)

    gap = lax.rem(z - y + SIDE, SIDE)

    def to_plane(piece, step):
        return remote(
            whole.at[piece], fourth.at[piece, step - 1],
            sends.at[2, piece, step - 1], recvs.at[2, piece, step - 1],
            device(x, y, turned(z, SIDE - step), core),
        )

    def to_row(piece, step):
        return remote(
            fifth.at[0, piece], fifth.at[1, piece],
            sends.at[3, piece, step - 1], recvs.at[3, piece, 0],
            device(x, turned(y, step), z, core),
        )

    for piece in range(PIECES):
        at, started = threes[piece]
        for copy in started:
            copy.wait_recv()
        whole[piece] = add(half[piece, at], *[third[piece, step - 1] for step in steps])
        for step in steps:
            @pl.when(gap == step)
            def _():
                to_plane(piece, step).start()

    @pl.when(gap == 0)
    def _():
        for piece in range(PIECES):
            for step in steps:
                to_plane(piece, step).wait_recv()
            fifth[0, piece] = add(whole[piece], *[fourth[piece, step - 1] for step in steps])
            for step in steps:
                to_row(piece, step).start()
        for piece in range(PIECES):
            for step in steps:
                to_row(piece, step).wait_send()
        sum_ref[...] = fifth[0]

    @pl.when(gap != 0)
    def _():
        for piece in range(PIECES):
            to_row(piece, 1).wait_recv()
        sum_ref[...] = fifth[1]

    for piece in range(PIECES):
        for step in steps:
            @pl.when(gap == step)
            def _():
                to_plane(piece, step).wait_send()

    for copy in returns:
        copy.wait_recv()
    for copy in copies:
        copy.wait_send()
    att_store.wait()


def settle_kernel(
    norm, flags_ref, sum_ref, back_ref, att_in, gq_in, gk_in, gv_in,
    att_out, gq_out, gk_out, gv_out, rows_ref, own, extra, att, sem, att_sem,
):
    def block(i):
        return pl.ds(i * BLOCK, BLOCK)

    att_load = pltpu.make_async_copy(att_in, att, att_sem.at[0])
    att_load.start()
    sides = []
    for side, (near, far) in enumerate(((0, 1), (3, 2))):
        parts = ((gk_out, near, 0), (gv_out, near, 1), (gk_out, far, 2), (gv_out, far, 3))
        ours = [
            pltpu.make_async_copy(out.at[block(at)], own.at[side, slot], sem.at[side, slot])
            for out, at, slot in parts
        ]
        theirs = [
            pltpu.make_async_copy(
                back_ref.at[side, slot], extra.at[side, slot], sem.at[side, 4 + slot]
            )
            for slot in range(4)
        ]
        moved = [
            pltpu.make_async_copy(extra.at[side, slot], out.at[block(near)], sem.at[side, slot])
            for slot, out in enumerate((gk_out, gv_out, gq_out))
        ]
        added = [
            pltpu.make_async_copy(own.at[side, slot], out.at[block(at)], sem.at[side, slot])
            for out, at, slot in parts
        ]
        away, shared = flags_ref[2 * side] == 1, flags_ref[2 * side + 1] == 1
        sides.append((side, ours, theirs, moved, added, away, shared))

    for side, ours, theirs, moved, added, away, shared in sides:
        for copy in theirs:
            copy.start()

        @pl.when(shared)
        def _():
            for copy in ours:
                copy.start()

    for piece in range(PIECES):
        for tile in range(PIECE // 128):
            lanes = slice(piece * PIECE + tile * 128, piece * PIECE + (tile + 1) * 128)
            part = sum_ref[piece].astype(jnp.float32)[tile * PART : (tile + 1) * PART]
            rows_ref[:, lanes] = part * norm

    att_load.wait()
    for side, ours, theirs, moved, added, away, shared in sides:
        for copy in theirs:
            copy.wait()

        @pl.when(away)
        def _():
            att[3 * side * BLOCK : (3 * side + 1) * BLOCK] = extra[side, 3]

        @pl.when(away)
        def _():
            for copy in moved:
                copy.start()

        @pl.when(shared)
        def _():
            for slot in range(4):
                ours[slot].wait()
                both = own[side, slot].astype(jnp.float32) + extra[side, slot].astype(jnp.float32)
                own[side, slot] = both.astype(jnp.bfloat16)
                added[slot].start()

    att_store = pltpu.make_async_copy(att, att_out, att_sem.at[0])
    att_store.start()
    for side, ours, theirs, moved, added, away, shared in sides:
        @pl.when(away)
        def _():
            for copy in moved:
                copy.wait()

        @pl.when(shared)
        def _():
            for copy in added:
                copy.wait()

    att_store.wait()


def on_device(q_tokens, k_tokens, v_tokens, d_attended, w_out, lengths):
    rows, width = q_tokens.shape[1:]
    count = lax.axis_size("tok")
    norm = 1.0 / math.sqrt(lax.axis_size("dp") * count * rows)
    q, k, v, dy = q_tokens[0], k_tokens[0], v_tokens[0], d_attended[0]
    low = jnp.bfloat16
    vmem, smem, anywhere = (
        pl.BlockSpec(memory_space=space) for space in (pltpu.VMEM, pltpu.SMEM, pl.ANY)
    )
    token_shape = jax.ShapeDtypeStruct((rows, width), low)
    halo_shape = jax.ShapeDtypeStruct((2, 4, BLOCK, width), low)
    big = 58 * 1024 * 1024

    halo, dm = pl.pallas_call(
        functools.partial(exchange_kernel, count),
        out_shape=(halo_shape, token_shape),
        in_specs=[smem] + [anywhere] * 5,
        out_specs=(anywhere, vmem),
        scratch_shapes=[
            pltpu.VMEM((rows, width), low),
            pltpu.VMEM((width, width), low),
            pltpu.VMEM((2, BLOCK, width), low),
            pltpu.VMEM((2, 2, BLOCK, width), low),
            pltpu.VMEM((2, 2, BLOCK, width), low),
            pltpu.SemaphoreType.DMA((8,)),
            pltpu.SemaphoreType.DMA((2, 4)),
            pltpu.SemaphoreType.DMA((2, 4)),
        ],
        compiler_params=pltpu.CompilerParams(
            collective_id=0, has_side_effects=True, vmem_limit_bytes=big
        ),
        name="exchange",
    )(lengths, q, k, v, dy, w_out)

    dma = pltpu.SemaphoreType.DMA
    slab = pltpu.VMEM((SLOTS * BLOCK, width), low)
    square = pltpu.VMEM((width, width), low)
    sides = pltpu.VMEM((2, BLOCK, width), low)
    mixed_shape = jax.ShapeDtypeStruct(((OWN + 2) * BLOCK, width), low)
    mixed, gq, gk, gv, ret, flags = pl.pallas_call(
        attention_kernel,
        out_shape=(
            mixed_shape, token_shape, token_shape, token_shape, halo_shape,
            jax.ShapeDtypeStruct((4,), jnp.int32),
        ),
        in_specs=[smem] + [anywhere] * 6,
        out_specs=(anywhere,) * 5 + (smem,),
        scratch_shapes=[slab] * 4 + [square, sides] + [slab] * 4
        + [sides, pltpu.SMEM((8, 2), jnp.int32), dma((5,)), dma((2, 4)), dma((4, SLOTS))],
        compiler_params=pltpu.CompilerParams(vmem_limit_bytes=big),
        name="attention",
    )(lengths, q, k, v, dm, halo, w_out)

    sum_shape = jax.ShapeDtypeStruct((PIECES, PACKED, 128), low)

    def pieces(*sizes):
        return pltpu.VMEM((PIECES, *sizes, PACKED, 128), low)

    slab = pltpu.VMEM(mixed_shape.shape, low)
    back, summed, att = pl.pallas_call(
        functools.partial(finish_kernel, count),
        out_shape=(halo_shape, sum_shape, token_shape),
        in_specs=[anywhere] * 5,
        out_specs=(anywhere, vmem, anywhere),
        scratch_shapes=[
            slab, pltpu.VMEM(mixed_shape.shape[::-1], low), slab, square,
            pltpu.VMEM((rows, width), low),
            pltpu.VMEM((width, PIECE), jnp.float32),
            pltpu.VMEM((PACKED, 128), jnp.float32),
            pieces(2, SIDE, SIDE), pieces(SIDE, SIDE), pieces(SIDE, SIDE),
            pieces(SIDE - 1, SIDE), pieces(SIDE), pieces(SIDE - 1),
            pieces(), pieces(SIDE - 1),
            pltpu.VMEM((2, PIECES, PACKED, 128), low),
            dma((5,)), dma((2, 4)), dma((2, 4)), dma((PIECES,)), dma((PIECES,)),
            dma((4, PIECES, SIDE - 1)), dma((4, PIECES, SIDE - 1)),
        ],
        compiler_params=pltpu.CompilerParams(
            collective_id=1, has_side_effects=True, vmem_limit_bytes=big
        ),
        name="finish",
    )(ret, mixed, dy, halo, w_out)

    att, gq, gk, gv, grad_rows = pl.pallas_call(
        functools.partial(settle_kernel, norm),
        out_shape=(token_shape,) * 4 + (jax.ShapeDtypeStruct((PART, width), jnp.float32),),
        in_specs=[smem, vmem] + [anywhere] * 5,
        out_specs=(anywhere,) * 4 + (vmem,),
        scratch_shapes=[
            pltpu.VMEM((2, 4, BLOCK, width), low),
            pltpu.VMEM((2, 4, BLOCK, width), low),
            pltpu.VMEM((rows, width), low),
            dma((2, 8)), dma((1,)),
        ],
        input_output_aliases={4: 1, 5: 2, 6: 3},
        compiler_params=pltpu.CompilerParams(vmem_limit_bytes=big),
        name="settle",
    )(flags, summed, back, att, gq, gk, gv)
    return (att[None], gq[None], gk[None], gv[None], grad_rows)


def solution(mesh):
    tokens = P("dp", "tok", None)
    return jax.shard_map(
        on_device,
        mesh=mesh,
        in_specs=(tokens, tokens, tokens, tokens, P(), P("dp", None)),
        out_specs=(tokens, tokens, tokens, tokens, P("tok", None)),
        check_vma=False,
    )
```

```python
import functools
import math

import jax
import jax.numpy as jnp
from jax import lax
from jax.experimental import pallas as pl
from jax.experimental.pallas import tpu as pltpu
from jax.sharding import PartitionSpec as P

HEADS = 16
HEAD_DIM = 72
BLOCK = 128
D = 1152
OWN = 4
SLOTS = 8
WINDOW = 256
SCALE = HEAD_DIM ** (-0.5)
EXP2_SCALE = SCALE * math.log2(math.e)
PART = 36
PIECE = 384
PIECES = D // PIECE
PACKED = 112
SIDE = 4
MESH = pl.DeviceIdType.MESH
NN = (((1,), (0,)), ((), ()))
NT = (((1,), (1,)), ((), ()))
TN = (((0,), (0,)), ((), ()))


def dot(a, b, dims):
    return lax.dot_general(a, b, dims, preferred_element_type=jnp.float32)


def boundaries(lengths_ref, edges):
    def step(i, carry):
        start, counts = carry
        end = start + lengths_ref[0, i]
        new = []
        for edge, (before, after) in zip(edges, counts):
            hit = jnp.logical_and(start < edge, end > edge)
            new.append((jnp.where(hit, edge - start, before), jnp.where(hit, end - edge, after)))
        return end, tuple(new)

    zero = jnp.int32(0)
    start = (zero, tuple((zero, zero) for _ in edges))
    return lax.fori_loop(0, lengths_ref.shape[1], step, start)[1]


def plans(lengths_ref, first):
    counts = boundaries(lengths_ref, [first - OWN, first, first + OWN, first + 2 * OWN])

    def is_pair(pair, before, after):
        return jnp.logical_and(pair[0] == before, pair[1] == after)

    result = []
    for at in (1, 2):
        here = counts[at]
        left_full = is_pair(counts[at - 1], 1, 3)
        right_full = is_pair(counts[at + 1], 3, 1)
        only_left = jnp.logical_and(left_full, jnp.logical_not(right_full))
        only_right = jnp.logical_and(right_full, jnp.logical_not(left_full))
        to_left = (
            is_pair(here, 3, 1)
            | (is_pair(here, 2, 1) & right_full)
            | (is_pair(here, 1, 1) & only_right)
        )
        to_right = (
            is_pair(here, 1, 3)
            | (is_pair(here, 1, 2) & left_full)
            | (is_pair(here, 1, 1) & only_left)
        )
        shared = (here[0] > 0) & jnp.logical_not(to_left | to_right)
        result.append((here[0], here[1], to_left, to_right, shared))
    return result


def greet(others):
    for other in others:
        where = other if isinstance(other, dict) else {"tok": other}
        pl.semaphore_signal(
            pltpu.get_barrier_semaphore(), inc=1, device_id=where, device_id_type=MESH
        )


def meet(others):
    pl.semaphore_wait(pltpu.get_barrier_semaphore(), len(others))


def ring_neighbours(count):
    me = lax.axis_index("tok")
    return lax.rem(me + count - 1, count), lax.rem(me + 1, count)


def exchange_kernel(
    count, lengths_ref, q_ref, k_ref, v_ref, dy_ref, w_ref, halo_ref, dm_ref,
    dy_buf, w_buf, near_buf, far_buf, pack, load_sem, send_sem, recv_sem,
):
    left, right = ring_neighbours(count)
    first = lax.axis_index("tok") * OWN
    near = [pl.ds(0, BLOCK), pl.ds(3 * BLOCK, BLOCK)]
    far = [pl.ds(BLOCK, BLOCK), pl.ds(2 * BLOCK, BLOCK)]
    loads = []
    for side in range(2):
        loads += [
            (q_ref.at[near[side]], near_buf.at[side]),
            (k_ref.at[far[side]], far_buf.at[side, 0]),
            (v_ref.at[far[side]], far_buf.at[side, 1]),
        ]
    loads += [(dy_ref, dy_buf), (w_ref, w_buf)]
    loads = [pltpu.make_async_copy(a, b, load_sem.at[i]) for i, (a, b) in enumerate(loads)]
    for load in loads:
        load.start()
    greet((left, right))
    meet((left, right))
    copies = []

    def send(side, slot, source):
        copy = pltpu.make_async_remote_copy(
            src_ref=source,
            dst_ref=halo_ref.at[1 - side, slot],
            send_sem=send_sem.at[side, slot],
            recv_sem=recv_sem.at[1 - side, slot],
            device_id={"tok": right if side else left},
            device_id_type=MESH,
        )
        copy.start()
        copies.append(copy)

    for side in range(2):
        send(side, 0, k_ref.at[near[side]])
        send(side, 1, v_ref.at[near[side]])
    for load in loads[:-1]:
        load.wait()
    edges = plans(lengths_ref, first)
    for side in range(2):
        shared = edges[side][-1]
        pack[side, 0] = jnp.where(shared, far_buf[side, 0], near_buf[side])
        pack[side, 1] = jnp.where(shared, far_buf[side, 1], dy_buf[near[side]])
        send(side, 2, pack.at[side, 0])
        send(side, 3, pack.at[side, 1])
    loads[-1].wait()
    for part in range(OWN):
        rows = slice(part * BLOCK, (part + 1) * BLOCK)
        dm_ref[rows] = dot(dy_buf[rows], w_buf[...], NT).astype(jnp.bfloat16)
    for copy in copies:
        copy.wait()


def attend(q_buf, k_buf, v_buf, dm_buf, mixed, gq, gk, gv, q_at, q_blocks, k_at, k_blocks):
    q_rows = pl.ds(pl.multiple_of(q_at * BLOCK, BLOCK), q_blocks * BLOCK)
    k_rows = pl.ds(pl.multiple_of(k_at * BLOCK, BLOCK), k_blocks * BLOCK)
    lane = lax.broadcasted_iota(jnp.int32, (1, WINDOW), 1)

    group = {1: 8, 2: 4, 3: 2, 4: 2}[k_blocks]

    def several(i, carry):
        heads = []
        for j in range(group):
            at = (group * i + j) * HEAD_DIM
            base = jnp.minimum(at // 128, (D - WINDOW) // 128) * 128
            offset = at - base
            window = pl.ds(pl.multiple_of(base, 128), WINDOW)
            inside = jnp.logical_and(lane >= offset, lane < offset + HEAD_DIM)
            keep = jnp.where(inside, 1.0, 0.0).astype(jnp.bfloat16)
            heads.append((offset, window, keep))
        probs_of, ds_of = [], []
        for offset, window, keep in heads:
            scores = dot(k_buf[k_rows, window] * keep, q_buf[q_rows, window], NT)
            d_probs = dot(v_buf[k_rows, window] * keep, dm_buf[q_rows, window], NT)
            top = jnp.max(scores, axis=0, keepdims=True)
            weights = jnp.exp2((scores - top) * EXP2_SCALE)
            probs = weights * (1.0 / jnp.sum(weights, axis=0, keepdims=True))
            product = probs * d_probs
            delta = jnp.sum(product, axis=0, keepdims=True)
            probs_of.append(probs.astype(jnp.bfloat16))
            ds_of.append((product - probs * delta).astype(jnp.bfloat16))
        news = []
        for (offset, window, keep), p, ds in zip(heads, probs_of, ds_of):
            news.append((
                dot(p, v_buf[k_rows, window], TN), dot(p, dm_buf[q_rows, window], NN),
                dot(ds, k_buf[k_rows, window], TN) * SCALE, dot(ds, q_buf[q_rows, window], NN) * SCALE,
            ))
        for (offset, window, keep), new in zip(heads, news):
            for ref, rows, value in zip((mixed, gv, gq, gk), (q_rows, k_rows, q_rows, k_rows), new):
                old = ref[rows, window]
                ref[rows, window] = jnp.where(lane < offset, old, value.astype(jnp.bfloat16))
        return carry

    lax.fori_loop(0, HEADS // group, several, 0)


def attention_kernel(
    lengths_ref, q_ref, k_ref, v_ref, dm_ref, halo_ref, w_ref,
    mixed_out, gq_out, gk_out, gv_out, ret_out, flags_out,
    q_buf, k_buf, v_buf, dm_buf, w_buf, dy_buf, mixed, gq, gk, gv, att, work, sem, halo_sem, store_sem,
):
    first = lax.axis_index("tok") * OWN
    last = first + OWN
    own = pl.ds(2 * BLOCK, OWN * BLOCK)

    def block(i):
        return pl.ds(i * BLOCK, BLOCK)

    loads = [
        (q_ref, q_buf.at[own]), (k_ref, k_buf.at[own]), (v_ref, v_buf.at[own]),
        (dm_ref, dm_buf.at[own]), (w_ref, w_buf),
    ]
    loads = [pltpu.make_async_copy(a, b, sem.at[i]) for i, (a, b) in enumerate(loads)]
    w_load = loads.pop()
    for load in loads:
        load.start()

    left_edge, right_edge = plans(lengths_ref, first)
    l_before, l_after, l_away, l_here, l_shared = left_edge
    r_before, r_after, r_here, r_away, r_shared = right_edge
    flags = (
        l_away, l_shared, l_shared & (l_after == 2), r_away, r_shared, r_shared & (r_before == 2)
    )
    for i, flag in enumerate(flags):
        flags_out[i] = flag.astype(jnp.int32)

    halo_loads = []
    for side, (near, far, here, shared) in enumerate(
        ((1, 0, l_here, l_shared), (6, 7, r_here, r_shared))
    ):
        def load(slot, to, side=side):
            return pltpu.make_async_copy(halo_ref.at[side, slot], to, halo_sem.at[side, slot])

        both = [load(0, k_buf.at[block(near)]), load(1, v_buf.at[block(near)])]
        if_here = [load(2, q_buf.at[block(near)]), load(3, dy_buf.at[side])]
        if_shared = [load(2, k_buf.at[block(far)]), load(3, v_buf.at[block(far)])]
        halo_loads += [(here, both + if_here), (shared, both + if_shared)]
    for flag, some in halo_loads:
        @pl.when(flag)
        def _():
            for load in some:
                load.start()

    w_load.start()

    def collect(i, carry):
        start, number = carry
        end = start + lengths_ref[0, i]
        on_left = jnp.logical_and(start < first, end > first)
        on_right = jnp.logical_and(start < last, end > last)
        within = jnp.logical_and(start >= first, end <= last)
        mine = (
            within
            | (on_left & jnp.logical_not(l_away))
            | (on_right & jnp.logical_not(r_away))
        )
        shared = (on_left & l_shared) | (on_right & r_shared)
        own_blocks = jnp.where(on_left, l_after, r_before)

        @pl.when(mine)
        def _():
            k_at = start - first + 2
            work[number, 0] = jnp.where(shared, own_blocks * 8 + end - start, end - start)
            work[number, 1] = jnp.where(shared & on_left, 2, k_at)
            work[number, 2] = k_at

        return end, number + mine.astype(jnp.int32)

    _, number = lax.fori_loop(
        0, lengths_ref.shape[1], collect, (jnp.int32(0), jnp.int32(0))
    )
    for load in loads:
        load.wait()
    for flag, some in halo_loads:
        @pl.when(flag)
        def _():
            for load in some:
                load.wait()

    w_load.wait()
    for side, (here, slot) in enumerate(((l_here, 1), (r_here, 6))):
        @pl.when(here)
        def _():
            dm_buf[block(slot)] = dot(dy_buf[side], w_buf[...], NT).astype(jnp.bfloat16)

    bufs = (q_buf, k_buf, v_buf, dm_buf, mixed, gq, gk, gv)

    def store(index, slot):
        if index == 0:
            return pltpu.make_async_copy(
                mixed.at[rows_of(slot)], mixed_out.at[rows_of(slot - 1)], store_sem.at[0, slot]
            )
        ref, out = ((gq, gq_out), (gk, gk_out), (gv, gv_out))[index - 1]
        return pltpu.make_async_copy(
            ref.at[rows_of(slot)], out.at[rows_of(slot - 2)], store_sem.at[index, slot]
        )

    def rows_of(slot):
        return pl.ds(pl.multiple_of(slot * BLOCK, BLOCK), BLOCK)

    def store_all(slot, indices):
        for index in indices:
            if index == 0:
                store(0, slot).start()
            else:
                @pl.when(jnp.logical_and(slot >= 2, slot < 2 + OWN))
                def _():
                    store(index, slot).start()

    def image(i, carry):
        kind, q_at, k_at = work[i, 0], work[i, 1], work[i, 2]
        for q_blocks, k_blocks in ((1, 1), (2, 2), (3, 3), (4, 4), (1, 2), (1, 3), (2, 3), (2, 4)):
            @pl.when(kind == (k_blocks if q_blocks == k_blocks else q_blocks * 8 + k_blocks))
            def _():
                attend(*bufs, q_at, q_blocks, k_at, k_blocks)
                for j in range(q_blocks):
                    store_all(q_at + j, range(4))

        return carry

    lax.fori_loop(0, number, image, 0)

    idle = (
        (jnp.logical_not(l_here), 1), (l_away, 2), (r_away, 5), (jnp.logical_not(r_here), 6)
    )
    for flag, slot in idle:
        @pl.when(flag)
        def _():
            mixed[block(slot)] = jnp.zeros((BLOCK, D), jnp.bfloat16)
            store_all(jnp.int32(slot), range(4))

    def give(side, slot, source):
        return pltpu.make_async_copy(source, ret_out.at[side, slot], halo_sem.at[side, slot])

    gives = []
    for side, (near, far, here, shared) in enumerate(
        ((1, 0, l_here, l_shared), (6, 7, r_here, r_shared))
    ):
        both = [give(side, 0, gk.at[block(near)]), give(side, 1, gv.at[block(near)])]
        if_here = [give(side, 2, gq.at[block(near)]), give(side, 3, att.at[side])]
        if_shared = [give(side, 2, gk.at[block(far)]), give(side, 3, gv.at[block(far)])]

        @pl.when(here)
        def _():
            for copy in both + if_here[:1]:
                copy.start()
            att[side] = dot(mixed[block(near)], w_buf[...], NN).astype(jnp.bfloat16)
            if_here[1].start()

        @pl.when(shared)
        def _():
            for copy in both + if_shared:
                copy.start()

        gives += [(here, both + if_here), (shared, both + if_shared)]
    for flag, some in gives:
        @pl.when(flag)
        def _():
            for copy in some:
                copy.wait()

    for slot in range(1, 3 + OWN):
        for index in range(4):
            if index == 0 or 2 <= slot < 2 + OWN:
                store(index, slot).wait()


def finish_kernel(
    count, ret_ref, mixed_ref, dy_ref, halo_ref, w_ref, back_ref, sum_ref, att_ref,
    mixed, turned_mixed, dy, w_buf, att, acc, stage, parts, sibling, total, second, half, third, whole, fourth, fifth,
    load_sem, ret_send, ret_recv, one_send, one_recv, sends, recvs,
):
    left, right = ring_neighbours(count)
    me, y = lax.axis_index("tok"), lax.axis_index("dp")
    core, z, x = lax.rem(me, 2), lax.rem(me // 2, SIDE), me // (2 * SIDE)
    loads = [
        (mixed_ref, mixed),
        (halo_ref.at[0, 3], dy.at[pl.ds(0, BLOCK)]),
        (dy_ref, dy.at[pl.ds(BLOCK, OWN * BLOCK)]),
        (halo_ref.at[1, 3], dy.at[pl.ds((OWN + 1) * BLOCK, BLOCK)]),
        (w_ref, w_buf),
    ]
    loads = [pltpu.make_async_copy(a, b, load_sem.at[i]) for i, (a, b) in enumerate(loads)]
    for load in loads:
        load.start()

    def device(x, y, z, core):
        return {"dp": y, "tok": (x * SIDE + z) * 2 + core}

    def turned(at, step):
        return lax.rem(at + step, SIDE)

    other = device(x, y, z, 1 - core)
    steps = range(1, SIDE)
    along_x = [device(turned(x, step), y, z, core) for step in steps]
    along_y = [device(x, turned(y, step), z, core) for step in steps]
    along_z = [device(x, y, turned(z, step), core) for step in steps]
    others = [left, right, other] + along_x + along_y + along_z
    greet(others)
    copies = []

    def remote(source, landing, send_sem, recv_sem, where):
        return pltpu.make_async_remote_copy(
            src_ref=source, dst_ref=landing, send_sem=send_sem, recv_sem=recv_sem,
            device_id=where, device_id_type=MESH,
        )

    def send(*args):
        copy = remote(*args)
        copy.start()
        copies.append(copy)
        return copy

    for load in loads[:-1]:
        load.wait()
    for tile in range(D // 128):
        lanes = slice(tile * 128, (tile + 1) * 128)
        turned_mixed[lanes] = mixed[:, lanes].T
    stage[...] = jnp.zeros_like(stage)

    def x_first(piece, on_core_0):
        return on_core_0 if piece < PIECES - 1 else False

    def product(piece):
        columns = slice(piece * PIECE, (piece + 1) * PIECE)

        def weight(i, carry):
            at = pl.ds(pl.multiple_of(i * PIECE, PIECE), PIECE)
            acc[at] = dot(turned_mixed[at], dy[:, columns], NN)
            return carry

        lax.fori_loop(0, D // PIECE, weight, 0)
        for part in range(D // PART):
            px, pz, pcore = part // 8, part // 2 % 4, part % 2
            place = (px, pz) if x_first(piece, pcore == 0) else (pz, px)
            for tile in range(PIECE // 128):
                stage[tile * PART : (tile + 1) * PART] = acc[
                    part * PART : (part + 1) * PART, tile * 128 : (tile + 1) * 128
                ]
            parts[piece, pcore, place[0], place[1]] = stage[...].astype(jnp.bfloat16)

    def to_sibling(piece):
        return send(
            parts.at[piece, 1 - core], sibling.at[piece], one_send.at[piece], one_recv.at[piece],
            other,
        )

    def spread(stage_at, piece, source, landing, x_axis):
        at = jnp.where(x_axis, x, y)
        started = []
        for step in steps:
            there = turned(at, step)
            where = device(jnp.where(x_axis, there, x), jnp.where(x_axis, y, there), z, core)
            started.append(send(
                source.at[there], landing.at[step - 1],
                sends.at[stage_at, piece, step - 1], recvs.at[stage_at, piece, step - 1], where,
            ))
        return at, started

    def add(*values):
        result = values[0].astype(jnp.float32)
        for value in values[1:]:
            result = result + value.astype(jnp.float32)
        return result.astype(jnp.bfloat16)

    twos, threes = [], []

    def second_stage(piece):
        one[piece].wait_recv()
        for row in range(SIDE):
            total[piece, row] = add(parts[piece, core, row], sibling[piece, row])
        twos.append(spread(0, piece, total.at[piece], second.at[piece], x_first(piece, core == 0)))

    def third_stage(piece):
        at, started = twos[piece]
        for copy in started:
            copy.wait_recv()
        half[piece] = add(total[piece, at], *[second[piece, step - 1] for step in steps])
        threes.append(spread(1, piece, half.at[piece], third.at[piece], jnp.logical_not(x_first(piece, core == 0))))

    product(0)
    meet(others)
    one = [to_sibling(0)]
    returns = []
    for side in range(2):
        for slot in range(4):
            returns.append(send(
                ret_ref.at[side, slot], back_ref.at[1 - side, slot],
                ret_send.at[side, slot], ret_recv.at[1 - side, slot],
                {"tok": right if side else left},
            ))
    for piece in range(1, PIECES):
        product(piece)
        one.append(to_sibling(piece))
        second_stage(piece - 1)
    second_stage(PIECES - 1)

    loads[-1].wait()
    for part in range(OWN):
        rows = slice(part * BLOCK, (part + 1) * BLOCK)
        ours = mixed[(part + 1) * BLOCK : (part + 2) * BLOCK]
        att[rows] = dot(ours, w_buf[...], NN).astype(jnp.bfloat16)
    att_store = pltpu.make_async_copy(att, att_ref, load_sem.at[0])
    att_store.start()
    for piece in range(PIECES):
        third_stage(piece)

    gap = lax.rem(z - y + SIDE, SIDE)

    def to_plane(piece, step):
        return remote(
            whole.at[piece], fourth.at[piece, step - 1],
            sends.at[2, piece, step - 1], recvs.at[2, piece, step - 1],
            device(x, y, turned(z, SIDE - step), core),
        )

    def to_row(piece, step):
        return remote(
            fifth.at[0, piece], fifth.at[1, piece],
            sends.at[3, piece, step - 1], recvs.at[3, piece, 0],
            device(x, turned(y, step), z, core),
        )

    for piece in range(PIECES):
        at, started = threes[piece]
        for copy in started:
            copy.wait_recv()
        whole[piece] = add(half[piece, at], *[third[piece, step - 1] for step in steps])
        for step in steps:
            @pl.when(gap == step)
            def _():
                to_plane(piece, step).start()

    @pl.when(gap == 0)
    def _():
        for piece in range(PIECES):
            for step in steps:
                to_plane(piece, step).wait_recv()
            fifth[0, piece] = add(whole[piece], *[fourth[piece, step - 1] for step in steps])
            for step in steps:
                to_row(piece, step).start()
        for piece in range(PIECES):
            for step in steps:
                to_row(piece, step).wait_send()
        sum_ref[...] = fifth[0]

    @pl.when(gap != 0)
    def _():
        for piece in range(PIECES):
            to_row(piece, 1).wait_recv()
        sum_ref[...] = fifth[1]

    for piece in range(PIECES):
        for step in steps:
            @pl.when(gap == step)
            def _():
                to_plane(piece, step).wait_send()

    for copy in returns:
        copy.wait_recv()
    for copy in copies:
        copy.wait_send()
    att_store.wait()


def settle_kernel(
    norm, flags_ref, sum_ref, back_ref, att_in, gq_in, gk_in, gv_in,
    att_out, gq_out, gk_out, gv_out, rows_ref, own, extra, att, sem, att_sem,
):
    def block(i):
        return pl.ds(i * BLOCK, BLOCK)

    att_load = pltpu.make_async_copy(att_in, att, att_sem.at[0])
    att_load.start()
    sides = []
    for side, (near, far) in enumerate(((0, 1), (3, 2))):
        parts = ((gk_out, near, 0), (gv_out, near, 1), (gk_out, far, 2), (gv_out, far, 3))
        ours = [
            pltpu.make_async_copy(out.at[block(at)], own.at[side, slot], sem.at[side, slot])
            for out, at, slot in parts
        ]
        theirs = [
            pltpu.make_async_copy(
                back_ref.at[side, slot], extra.at[side, slot], sem.at[side, 4 + slot]
            )
            for slot in range(4)
        ]
        moved = [
            pltpu.make_async_copy(extra.at[side, slot], out.at[block(near)], sem.at[side, slot])
            for slot, out in enumerate((gk_out, gv_out, gq_out))
        ]
        added = [
            pltpu.make_async_copy(own.at[side, slot], out.at[block(at)], sem.at[side, slot])
            for out, at, slot in parts
        ]
        away, shared, both = (flags_ref[3 * side + i] == 1 for i in range(3))
        sides.append((side, ours, theirs, moved, added, away, shared, both))

    for side, ours, theirs, moved, added, away, shared, both in sides:
        for copy in theirs:
            copy.start()

        @pl.when(shared)
        def _():
            for copy in ours:
                copy.start()

    for piece in range(PIECES):
        for tile in range(PIECE // 128):
            lanes = slice(piece * PIECE + tile * 128, piece * PIECE + (tile + 1) * 128)
            part = sum_ref[piece].astype(jnp.float32)[tile * PART : (tile + 1) * PART]
            rows_ref[:, lanes] = part * norm

    att_load.wait()
    for side, ours, theirs, moved, added, away, shared, both in sides:
        for copy in theirs:
            copy.wait()

        @pl.when(away)
        def _():
            att[3 * side * BLOCK : (3 * side + 1) * BLOCK] = extra[side, 3]

        @pl.when(away)
        def _():
            for copy in moved:
                copy.start()

        @pl.when(shared)
        def _():
            for slot in range(4):
                ours[slot].wait()
                total = own[side, slot].astype(jnp.float32)
                other = extra[side, slot].astype(jnp.float32)
                if slot >= 2:
                    other = jnp.where(both, other, 0.0)
                own[side, slot] = (total + other).astype(jnp.bfloat16)
                added[slot].start()

    att_store = pltpu.make_async_copy(att, att_out, att_sem.at[0])
    att_store.start()
    for side, ours, theirs, moved, added, away, shared, both in sides:
        @pl.when(away)
        def _():
            for copy in moved:
                copy.wait()

        @pl.when(shared)
        def _():
            for copy in added:
                copy.wait()

    att_store.wait()


def on_device(q_tokens, k_tokens, v_tokens, d_attended, w_out, lengths):
    rows, width = q_tokens.shape[1:]
    count = lax.axis_size("tok")
    norm = 1.0 / math.sqrt(lax.axis_size("dp") * count * rows)
    q, k, v, dy = q_tokens[0], k_tokens[0], v_tokens[0], d_attended[0]
    low = jnp.bfloat16
    vmem, smem, anywhere = (
        pl.BlockSpec(memory_space=space) for space in (pltpu.VMEM, pltpu.SMEM, pl.ANY)
    )
    token_shape = jax.ShapeDtypeStruct((rows, width), low)
    halo_shape = jax.ShapeDtypeStruct((2, 4, BLOCK, width), low)
    big = 58 * 1024 * 1024

    halo, dm = pl.pallas_call(
        functools.partial(exchange_kernel, count),
        out_shape=(halo_shape, token_shape),
        in_specs=[smem] + [anywhere] * 5,
        out_specs=(anywhere, vmem),
        scratch_shapes=[
            pltpu.VMEM((rows, width), low),
            pltpu.VMEM((width, width), low),
            pltpu.VMEM((2, BLOCK, width), low),
            pltpu.VMEM((2, 2, BLOCK, width), low),
            pltpu.VMEM((2, 2, BLOCK, width), low),
            pltpu.SemaphoreType.DMA((8,)),
            pltpu.SemaphoreType.DMA((2, 4)),
            pltpu.SemaphoreType.DMA((2, 4)),
        ],
        compiler_params=pltpu.CompilerParams(
            collective_id=0, has_side_effects=True, vmem_limit_bytes=big
        ),
        name="exchange",
    )(lengths, q, k, v, dy, w_out)

    dma = pltpu.SemaphoreType.DMA
    slab = pltpu.VMEM((SLOTS * BLOCK, width), low)
    square = pltpu.VMEM((width, width), low)
    sides = pltpu.VMEM((2, BLOCK, width), low)
    mixed_shape = jax.ShapeDtypeStruct(((OWN + 2) * BLOCK, width), low)
    mixed, gq, gk, gv, ret, flags = pl.pallas_call(
        attention_kernel,
        out_shape=(
            mixed_shape, token_shape, token_shape, token_shape, halo_shape,
            jax.ShapeDtypeStruct((6,), jnp.int32),
        ),
        in_specs=[smem] + [anywhere] * 6,
        out_specs=(anywhere,) * 5 + (smem,),
        scratch_shapes=[slab] * 4 + [square, sides] + [slab] * 4
        + [sides, pltpu.SMEM((8, 3), jnp.int32), dma((5,)), dma((2, 4)), dma((4, SLOTS))],
        compiler_params=pltpu.CompilerParams(vmem_limit_bytes=big),
        name="attention",
    )(lengths, q, k, v, dm, halo, w_out)

    sum_shape = jax.ShapeDtypeStruct((PIECES, PACKED, 128), low)

    def pieces(*sizes):
        return pltpu.VMEM((PIECES, *sizes, PACKED, 128), low)

    slab = pltpu.VMEM(mixed_shape.shape, low)
    back, summed, att = pl.pallas_call(
        functools.partial(finish_kernel, count),
        out_shape=(halo_shape, sum_shape, token_shape),
        in_specs=[anywhere] * 5,
        out_specs=(anywhere, vmem, anywhere),
        scratch_shapes=[
            slab, pltpu.VMEM(mixed_shape.shape[::-1], low), slab, square,
            pltpu.VMEM((rows, width), low),
            pltpu.VMEM((width, PIECE), jnp.float32),
            pltpu.VMEM((PACKED, 128), jnp.float32),
            pieces(2, SIDE, SIDE), pieces(SIDE, SIDE), pieces(SIDE, SIDE),
            pieces(SIDE - 1, SIDE), pieces(SIDE), pieces(SIDE - 1),
            pieces(), pieces(SIDE - 1),
            pltpu.VMEM((2, PIECES, PACKED, 128), low),
            dma((5,)), dma((2, 4)), dma((2, 4)), dma((PIECES,)), dma((PIECES,)),
            dma((4, PIECES, SIDE - 1)), dma((4, PIECES, SIDE - 1)),
        ],
        compiler_params=pltpu.CompilerParams(
            collective_id=1, has_side_effects=True, vmem_limit_bytes=big
        ),
        name="finish",
    )(ret, mixed, dy, halo, w_out)

    att, gq, gk, gv, grad_rows = pl.pallas_call(
        functools.partial(settle_kernel, norm),
        out_shape=(token_shape,) * 4 + (jax.ShapeDtypeStruct((PART, width), jnp.float32),),
        in_specs=[smem, vmem] + [anywhere] * 5,
        out_specs=(anywhere,) * 4 + (vmem,),
        scratch_shapes=[
            pltpu.VMEM((2, 4, BLOCK, width), low),
            pltpu.VMEM((2, 4, BLOCK, width), low),
            pltpu.VMEM((rows, width), low),
            dma((2, 8)), dma((1,)),
        ],
        input_output_aliases={4: 1, 5: 2, 6: 3},
        compiler_params=pltpu.CompilerParams(vmem_limit_bytes=big),
        name="settle",
    )(flags, summed, back, att, gq, gk, gv)
    return (att[None], gq[None], gk[None], gv[None], grad_rows)


def solution(mesh):
    tokens = P("dp", "tok", None)
    return jax.shard_map(
        on_device,
        mesh=mesh,
        in_specs=(tokens, tokens, tokens, tokens, P(), P("dp", None)),
        out_specs=(tokens, tokens, tokens, tokens, P("tok", None)),
        check_vma=False,
    )
```

```python
import functools
import math

import jax
import jax.numpy as jnp
from jax import lax
from jax.experimental import pallas as pl
from jax.experimental.pallas import tpu as pltpu
from jax.sharding import PartitionSpec as P

HEADS = 16
HEAD_DIM = 72
BLOCK = 128
D = 1152
OWN = 4
SLOTS = 8
WINDOW = 256
SCALE = HEAD_DIM ** (-0.5)
EXP2_SCALE = SCALE * math.log2(math.e)
PART = 36
PIECE = 384
PIECES = D // PIECE
PACKED = 112
SIDE = 4
MESH = pl.DeviceIdType.MESH
NN = (((1,), (0,)), ((), ()))
NT = (((1,), (1,)), ((), ()))
TN = (((0,), (0,)), ((), ()))


def dot(a, b, dims):
    return lax.dot_general(a, b, dims, preferred_element_type=jnp.float32)


def boundaries(lengths_ref, edges):
    def step(i, carry):
        start, counts = carry
        end = start + lengths_ref[0, i]
        new = []
        for edge, (before, after) in zip(edges, counts):
            hit = jnp.logical_and(start < edge, end > edge)
            new.append((jnp.where(hit, edge - start, before), jnp.where(hit, end - edge, after)))
        return end, tuple(new)

    zero = jnp.int32(0)
    start = (zero, tuple((zero, zero) for _ in edges))
    return lax.fori_loop(0, lengths_ref.shape[1], step, start)[1]


def plans(lengths_ref, first):
    counts = boundaries(lengths_ref, [first - OWN, first, first + OWN, first + 2 * OWN])

    def is_pair(pair, before, after):
        return jnp.logical_and(pair[0] == before, pair[1] == after)

    result = []
    for at in (1, 2):
        here = counts[at]
        left_full = is_pair(counts[at - 1], 1, 3)
        right_full = is_pair(counts[at + 1], 3, 1)
        only_left = jnp.logical_and(left_full, jnp.logical_not(right_full))
        only_right = jnp.logical_and(right_full, jnp.logical_not(left_full))
        to_left = (
            is_pair(here, 3, 1)
            | (is_pair(here, 2, 1) & right_full)
            | (is_pair(here, 1, 1) & only_right)
        )
        to_right = (
            is_pair(here, 1, 3)
            | (is_pair(here, 1, 2) & left_full)
            | (is_pair(here, 1, 1) & only_left)
        )
        shared = (here[0] > 0) & jnp.logical_not(to_left | to_right)
        result.append((here[0], here[1], to_left, to_right, shared))
    return result


def greet(others):
    for other in others:
        where = other if isinstance(other, dict) else {"tok": other}
        pl.semaphore_signal(
            pltpu.get_barrier_semaphore(), inc=1, device_id=where, device_id_type=MESH
        )


def meet(others):
    pl.semaphore_wait(pltpu.get_barrier_semaphore(), len(others))


def ring_neighbours(count):
    me = lax.axis_index("tok")
    return lax.rem(me + count - 1, count), lax.rem(me + 1, count)


def exchange_kernel(
    count, lengths_ref, q_ref, k_ref, v_ref, dy_ref, w_ref, halo_ref, dm_ref,
    dy_buf, w_buf, near_buf, far_buf, pack, load_sem, send_sem, recv_sem,
):
    left, right = ring_neighbours(count)
    first = lax.axis_index("tok") * OWN
    near = [pl.ds(0, BLOCK), pl.ds(3 * BLOCK, BLOCK)]
    far = [pl.ds(BLOCK, BLOCK), pl.ds(2 * BLOCK, BLOCK)]
    loads = []
    for side in range(2):
        loads += [
            (q_ref.at[near[side]], near_buf.at[side]),
            (k_ref.at[far[side]], far_buf.at[side, 0]),
            (v_ref.at[far[side]], far_buf.at[side, 1]),
        ]
    loads += [(dy_ref, dy_buf), (w_ref, w_buf)]
    loads = [pltpu.make_async_copy(a, b, load_sem.at[i]) for i, (a, b) in enumerate(loads)]
    for load in loads:
        load.start()
    greet((left, right))
    meet((left, right))
    copies = []

    def send(side, slot, source):
        copy = pltpu.make_async_remote_copy(
            src_ref=source,
            dst_ref=halo_ref.at[1 - side, slot],
            send_sem=send_sem.at[side, slot],
            recv_sem=recv_sem.at[1 - side, slot],
            device_id={"tok": right if side else left},
            device_id_type=MESH,
        )
        copy.start()
        copies.append(copy)

    for side in range(2):
        send(side, 0, k_ref.at[near[side]])
        send(side, 1, v_ref.at[near[side]])
    for load in loads[:-1]:
        load.wait()
    edges = plans(lengths_ref, first)
    for side in range(2):
        shared = edges[side][-1]
        pack[side, 0] = jnp.where(shared, far_buf[side, 0], near_buf[side])
        pack[side, 1] = jnp.where(shared, far_buf[side, 1], dy_buf[near[side]])
        send(side, 2, pack.at[side, 0])
        send(side, 3, pack.at[side, 1])
    loads[-1].wait()
    for part in range(OWN):
        rows = slice(part * BLOCK, (part + 1) * BLOCK)
        dm_ref[rows] = dot(dy_buf[rows], w_buf[...], NT).astype(jnp.bfloat16)
    for copy in copies:
        copy.wait()


def attend(q_buf, k_buf, v_buf, dm_buf, mixed, gq, gk, gv, q_at, q_blocks, k_at, k_blocks):
    q_rows = pl.ds(pl.multiple_of(q_at * BLOCK, BLOCK), q_blocks * BLOCK)
    k_rows = pl.ds(pl.multiple_of(k_at * BLOCK, BLOCK), k_blocks * BLOCK)
    lane = lax.broadcasted_iota(jnp.int32, (1, WINDOW), 1)

    group = {1: 8, 2: 4, 3: 2, 4: 2}[k_blocks]

    def several(i, carry):
        heads = []
        for j in range(group):
            at = (group * i + j) * HEAD_DIM
            base = jnp.minimum(at // 128, (D - WINDOW) // 128) * 128
            offset = at - base
            window = pl.ds(pl.multiple_of(base, 128), WINDOW)
            inside = jnp.logical_and(lane >= offset, lane < offset + HEAD_DIM)
            keep = jnp.where(inside, 1.0, 0.0).astype(jnp.bfloat16)
            heads.append((offset, window, keep))
        probs_of, ds_of = [], []
        for offset, window, keep in heads:
            scores = dot(k_buf[k_rows, window] * keep, q_buf[q_rows, window], NT)
            d_probs = dot(v_buf[k_rows, window] * keep, dm_buf[q_rows, window], NT)
            top = jnp.max(scores, axis=0, keepdims=True)
            weights = jnp.exp2((scores - top) * EXP2_SCALE)
            probs = weights * (1.0 / jnp.sum(weights, axis=0, keepdims=True))
            product = probs * d_probs
            delta = jnp.sum(product, axis=0, keepdims=True)
            probs_of.append(probs.astype(jnp.bfloat16))
            ds_of.append((product - probs * delta).astype(jnp.bfloat16))
        news = []
        for (offset, window, keep), p, ds in zip(heads, probs_of, ds_of):
            news.append((
                dot(p, v_buf[k_rows, window], TN), dot(p, dm_buf[q_rows, window], NN),
                dot(ds, k_buf[k_rows, window], TN) * SCALE, dot(ds, q_buf[q_rows, window], NN) * SCALE,
            ))
        for (offset, window, keep), new in zip(heads, news):
            for ref, rows, value in zip((mixed, gv, gq, gk), (q_rows, k_rows, q_rows, k_rows), new):
                old = ref[rows, window]
                ref[rows, window] = jnp.where(lane < offset, old, value.astype(jnp.bfloat16))
        return carry

    lax.fori_loop(0, HEADS // group, several, 0)


def attention_kernel(
    lengths_ref, q_ref, k_ref, v_ref, dm_ref, halo_ref, w_ref,
    mixed_out, gq_out, gk_out, gv_out, ret_out, flags_out,
    q_buf, k_buf, v_buf, dm_buf, w_buf, dy_buf, mixed, gq, gk, gv, att, work, sem, halo_sem, store_sem,
):
    first = lax.axis_index("tok") * OWN
    last = first + OWN
    own = pl.ds(2 * BLOCK, OWN * BLOCK)

    def block(i):
        return pl.ds(i * BLOCK, BLOCK)

    loads = [
        (q_ref, q_buf.at[own]), (k_ref, k_buf.at[own]), (v_ref, v_buf.at[own]),
        (dm_ref, dm_buf.at[own]), (w_ref, w_buf),
    ]
    loads = [pltpu.make_async_copy(a, b, sem.at[i]) for i, (a, b) in enumerate(loads)]
    w_load = loads.pop()
    for load in loads:
        load.start()

    left_edge, right_edge = plans(lengths_ref, first)
    l_before, l_after, l_away, l_here, l_shared = left_edge
    r_before, r_after, r_here, r_away, r_shared = right_edge
    flags = (
        l_away, l_shared, l_shared & (l_after == 2), r_away, r_shared, r_shared & (r_before == 2)
    )
    for i, flag in enumerate(flags):
        flags_out[i] = flag.astype(jnp.int32)

    halo_loads = []
    for side, (near, far, here, shared) in enumerate(
        ((1, 0, l_here, l_shared), (6, 7, r_here, r_shared))
    ):
        def load(slot, to, side=side):
            return pltpu.make_async_copy(halo_ref.at[side, slot], to, halo_sem.at[side, slot])

        both = [load(0, k_buf.at[block(near)]), load(1, v_buf.at[block(near)])]
        if_here = [load(2, q_buf.at[block(near)]), load(3, dy_buf.at[side])]
        if_shared = [load(2, k_buf.at[block(far)]), load(3, v_buf.at[block(far)])]
        halo_loads += [(here, both + if_here), (shared, both + if_shared)]
    for flag, some in halo_loads:
        @pl.when(flag)
        def _():
            for load in some:
                load.start()

    w_load.start()

    def collect(i, carry):
        start, number = carry
        end = start + lengths_ref[0, i]
        on_left = jnp.logical_and(start < first, end > first)
        on_right = jnp.logical_and(start < last, end > last)
        within = jnp.logical_and(start >= first, end <= last)
        mine = (
            within
            | (on_left & jnp.logical_not(l_away))
            | (on_right & jnp.logical_not(r_away))
        )
        shared = (on_left & l_shared) | (on_right & r_shared)
        own_blocks = jnp.where(on_left, l_after, r_before)

        @pl.when(mine)
        def _():
            k_at = start - first + 2
            work[number, 0] = jnp.where(shared, own_blocks * 8 + end - start, end - start)
            work[number, 1] = jnp.where(shared & on_left, 2, k_at)
            work[number, 2] = k_at

        return end, number + mine.astype(jnp.int32)

    _, number = lax.fori_loop(
        0, lengths_ref.shape[1], collect, (jnp.int32(0), jnp.int32(0))
    )
    for load in loads:
        load.wait()
    for flag, some in halo_loads:
        @pl.when(flag)
        def _():
            for load in some:
                load.wait()

    w_load.wait()
    for side, (here, slot) in enumerate(((l_here, 1), (r_here, 6))):
        @pl.when(here)
        def _():
            dm_buf[block(slot)] = dot(dy_buf[side], w_buf[...], NT).astype(jnp.bfloat16)

    bufs = (q_buf, k_buf, v_buf, dm_buf, mixed, gq, gk, gv)

    def store(index, slot):
        if index == 0:
            return pltpu.make_async_copy(
                mixed.at[rows_of(slot)], mixed_out.at[rows_of(slot - 1)], store_sem.at[0, slot]
            )
        ref, out = ((gq, gq_out), (gk, gk_out), (gv, gv_out))[index - 1]
        return pltpu.make_async_copy(
            ref.at[rows_of(slot)], out.at[rows_of(slot - 2)], store_sem.at[index, slot]
        )

    def rows_of(slot):
        return pl.ds(pl.multiple_of(slot * BLOCK, BLOCK), BLOCK)

    def store_all(slot, indices):
        for index in indices:
            if index == 0:
                store(0, slot).start()
            else:
                @pl.when(jnp.logical_and(slot >= 2, slot < 2 + OWN))
                def _():
                    store(index, slot).start()

    def image(i, carry):
        kind, q_at, k_at = work[i, 0], work[i, 1], work[i, 2]
        for q_blocks, k_blocks in ((1, 1), (2, 2), (3, 3), (4, 4), (1, 2), (1, 3), (2, 3), (2, 4)):
            @pl.when(kind == (k_blocks if q_blocks == k_blocks else q_blocks * 8 + k_blocks))
            def _():
                attend(*bufs, q_at, q_blocks, k_at, k_blocks)
                for j in range(q_blocks):
                    store_all(q_at + j, range(4))

        return carry

    lax.fori_loop(0, number, image, 0)

    idle = (
        (jnp.logical_not(l_here), 1), (l_away, 2), (r_away, 5), (jnp.logical_not(r_here), 6)
    )
    for flag, slot in idle:
        @pl.when(flag)
        def _():
            mixed[block(slot)] = jnp.zeros((BLOCK, D), jnp.bfloat16)
            store_all(jnp.int32(slot), range(4))

    def give(side, slot, source):
        return pltpu.make_async_copy(source, ret_out.at[side, slot], halo_sem.at[side, slot])

    gives = []
    for side, (near, far, here, shared) in enumerate(
        ((1, 0, l_here, l_shared), (6, 7, r_here, r_shared))
    ):
        both = [give(side, 0, gk.at[block(near)]), give(side, 1, gv.at[block(near)])]
        if_here = [give(side, 2, gq.at[block(near)]), give(side, 3, att.at[side])]
        if_shared = [give(side, 2, gk.at[block(far)]), give(side, 3, gv.at[block(far)])]

        @pl.when(here)
        def _():
            for copy in both + if_here[:1]:
                copy.start()
            att[side] = dot(mixed[block(near)], w_buf[...], NN).astype(jnp.bfloat16)
            if_here[1].start()

        @pl.when(shared)
        def _():
            for copy in both + if_shared:
                copy.start()

        gives += [(here, both + if_here), (shared, both + if_shared)]
    for flag, some in gives:
        @pl.when(flag)
        def _():
            for copy in some:
                copy.wait()

    for slot in range(1, 3 + OWN):
        for index in range(4):
            if index == 0 or 2 <= slot < 2 + OWN:
                store(index, slot).wait()


def finish_kernel(
    count, ret_ref, mixed_ref, dy_ref, halo_ref, w_ref, back_ref, sum_ref, att_ref,
    mixed, turned_mixed, dy, w_buf, att, acc, stage, parts, sibling, total, second, half, third, whole, fourth, fifth,
    load_sem, ret_send, ret_recv, one_send, one_recv, sends, recvs, relay, relay_send, relay_recv,
):
    left, right = ring_neighbours(count)
    me, y = lax.axis_index("tok"), lax.axis_index("dp")
    core, z, x = lax.rem(me, 2), lax.rem(me // 2, SIDE), me // (2 * SIDE)
    loads = [
        (mixed_ref, mixed),
        (halo_ref.at[0, 3], dy.at[pl.ds(0, BLOCK)]),
        (dy_ref, dy.at[pl.ds(BLOCK, OWN * BLOCK)]),
        (halo_ref.at[1, 3], dy.at[pl.ds((OWN + 1) * BLOCK, BLOCK)]),
        (w_ref, w_buf),
    ]
    loads = [pltpu.make_async_copy(a, b, load_sem.at[i]) for i, (a, b) in enumerate(loads)]
    for load in loads:
        load.start()

    def device(x, y, z, core):
        return {"dp": y, "tok": (x * SIDE + z) * 2 + core}

    def turned(at, step):
        return lax.rem(at + step, SIDE)

    other = device(x, y, z, 1 - core)
    steps = range(1, SIDE)
    along_x = [device(turned(x, step), y, z, core) for step in steps]
    along_y = [device(x, turned(y, step), z, core) for step in steps]
    along_z = [device(x, y, turned(z, step), core) for step in steps]
    across = [device(turned(x, step), y, z, 1 - core) for step in (1, SIDE - 1)]
    others = [left, right, other] + across + along_x + along_y + along_z
    at_end = (z == 0) | (z == SIDE - 1)
    crosses = at_end & ((core == 1) == (z == SIDE - 1))
    forwards = at_end & jnp.logical_not(crosses)
    opposite = device(x, y, SIDE - 1 - z, core)
    beyond = device(turned(x, jnp.where(core == 1, 1, SIDE - 1)), y, z, 1 - core)

    def to_forwarder(slot):
        return remote(
            ret_ref.at[core, 2 + slot], relay.at[slot], relay_send.at[slot], relay_recv.at[slot],
            opposite,
        )

    def forward(slot):
        return remote(
            relay.at[slot], back_ref.at[1 - core, 2 + slot],
            relay_send.at[slot], ret_recv.at[1 - core, 2 + slot], beyond,
        )

    def pass_on(slot):
        @pl.when(forwards)
        def _():
            to_forwarder(slot).wait_recv()
            forward(slot).start()

    greet(others)
    copies = []

    def remote(source, landing, send_sem, recv_sem, where):
        return pltpu.make_async_remote_copy(
            src_ref=source, dst_ref=landing, send_sem=send_sem, recv_sem=recv_sem,
            device_id=where, device_id_type=MESH,
        )

    def send(*args):
        copy = remote(*args)
        copy.start()
        copies.append(copy)
        return copy

    for load in loads[:-1]:
        load.wait()
    for tile in range(D // 128):
        lanes = slice(tile * 128, (tile + 1) * 128)
        turned_mixed[lanes] = mixed[:, lanes].T
    stage[...] = jnp.zeros_like(stage)

    def x_first(piece, on_core_0):
        return on_core_0 if piece < PIECES - 1 else False

    def product(piece):
        columns = slice(piece * PIECE, (piece + 1) * PIECE)

        def weight(i, carry):
            at = pl.ds(pl.multiple_of(i * PIECE, PIECE), PIECE)
            acc[at] = dot(turned_mixed[at], dy[:, columns], NN)
            return carry

        lax.fori_loop(0, D // PIECE, weight, 0)
        for part in range(D // PART):
            px, pz, pcore = part // 8, part // 2 % 4, part % 2
            place = (px, pz) if x_first(piece, pcore == 0) else (pz, px)
            for tile in range(PIECE // 128):
                stage[tile * PART : (tile + 1) * PART] = acc[
                    part * PART : (part + 1) * PART, tile * 128 : (tile + 1) * 128
                ]
            parts[piece, pcore, place[0], place[1]] = stage[...].astype(jnp.bfloat16)

    def to_sibling(piece):
        return send(
            parts.at[piece, 1 - core], sibling.at[piece], one_send.at[piece], one_recv.at[piece],
            other,
        )

    def spread(stage_at, piece, source, landing, x_axis):
        at = jnp.where(x_axis, x, y)
        started = []
        for step in steps:
            there = turned(at, step)
            where = device(jnp.where(x_axis, there, x), jnp.where(x_axis, y, there), z, core)
            started.append(send(
                source.at[there], landing.at[step - 1],
                sends.at[stage_at, piece, step - 1], recvs.at[stage_at, piece, step - 1], where,
            ))
        return at, started

    def add(*values):
        result = values[0].astype(jnp.float32)
        for value in values[1:]:
            result = result + value.astype(jnp.float32)
        return result.astype(jnp.bfloat16)

    twos, threes = [], []

    def second_stage(piece):
        one[piece].wait_recv()
        for row in range(SIDE):
            total[piece, row] = add(parts[piece, core, row], sibling[piece, row])
        twos.append(spread(0, piece, total.at[piece], second.at[piece], x_first(piece, core == 0)))

    def third_stage(piece):
        at, started = twos[piece]
        for copy in started:
            copy.wait_recv()
        half[piece] = add(total[piece, at], *[second[piece, step - 1] for step in steps])
        threes.append(spread(1, piece, half.at[piece], third.at[piece], jnp.logical_not(x_first(piece, core == 0))))

    product(0)
    meet(others)
    one = [to_sibling(0)]
    @pl.when(crosses)
    def _():
        for slot in range(2):
            to_forwarder(slot).start()

    returns = []
    for side in range(2):
        for slot in range(4):
            copy = remote(
                ret_ref.at[side, slot], back_ref.at[1 - side, slot],
                ret_send.at[side, slot], ret_recv.at[1 - side, slot],
                {"tok": right if side else left},
            )
            direct = True if slot < 2 else jnp.logical_not(crosses & (core == side))
            returns.append((copy, direct))

            @pl.when(direct)
            def _():
                copy.start()

    for piece in range(1, PIECES):
        product(piece)
        one.append(to_sibling(piece))
        second_stage(piece - 1)
    second_stage(PIECES - 1)
    pass_on(0)

    loads[-1].wait()
    for part in range(OWN):
        rows = slice(part * BLOCK, (part + 1) * BLOCK)
        ours = mixed[(part + 1) * BLOCK : (part + 2) * BLOCK]
        att[rows] = dot(ours, w_buf[...], NN).astype(jnp.bfloat16)
    att_store = pltpu.make_async_copy(att, att_ref, load_sem.at[0])
    att_store.start()
    for piece in range(PIECES):
        third_stage(piece)
    pass_on(1)

    gap = lax.rem(z - y + SIDE, SIDE)

    def to_plane(piece, step):
        return remote(
            whole.at[piece], fourth.at[piece, step - 1],
            sends.at[2, piece, step - 1], recvs.at[2, piece, step - 1],
            device(x, y, turned(z, SIDE - step), core),
        )

    def to_row(piece, step):
        return remote(
            fifth.at[0, piece], fifth.at[1, piece],
            sends.at[3, piece, step - 1], recvs.at[3, piece, 0],
            device(x, turned(y, step), z, core),
        )

    for piece in range(PIECES):
        at, started = threes[piece]
        for copy in started:
            copy.wait_recv()
        whole[piece] = add(half[piece, at], *[third[piece, step - 1] for step in steps])
        for step in steps:
            @pl.when(gap == step)
            def _():
                to_plane(piece, step).start()

    @pl.when(gap == 0)
    def _():
        for piece in range(PIECES):
            for step in steps:
                to_plane(piece, step).wait_recv()
            fifth[0, piece] = add(whole[piece], *[fourth[piece, step - 1] for step in steps])
            for step in steps:
                to_row(piece, step).start()
        for piece in range(PIECES):
            for step in steps:
                to_row(piece, step).wait_send()
        sum_ref[...] = fifth[0]

    @pl.when(gap != 0)
    def _():
        for piece in range(PIECES):
            to_row(piece, 1).wait_recv()
        sum_ref[...] = fifth[1]

    for piece in range(PIECES):
        for step in steps:
            @pl.when(gap == step)
            def _():
                to_plane(piece, step).wait_send()

    for copy, direct in returns:
        copy.wait_recv()

        @pl.when(direct)
        def _():
            copy.wait_send()

    @pl.when(crosses)
    def _():
        for slot in range(2):
            to_forwarder(slot).wait_send()

    @pl.when(forwards)
    def _():
        for slot in range(2):
            forward(slot).wait_send()

    for copy in copies:
        copy.wait_send()
    att_store.wait()


def settle_kernel(
    norm, flags_ref, sum_ref, back_ref, att_in, gq_in, gk_in, gv_in,
    att_out, gq_out, gk_out, gv_out, rows_ref, own, extra, att, sem, att_sem,
):
    def block(i):
        return pl.ds(i * BLOCK, BLOCK)

    att_load = pltpu.make_async_copy(att_in, att, att_sem.at[0])
    att_load.start()
    sides = []
    for side, (near, far) in enumerate(((0, 1), (3, 2))):
        parts = ((gk_out, near, 0), (gv_out, near, 1), (gk_out, far, 2), (gv_out, far, 3))
        ours = [
            pltpu.make_async_copy(out.at[block(at)], own.at[side, slot], sem.at[side, slot])
            for out, at, slot in parts
        ]
        theirs = [
            pltpu.make_async_copy(
                back_ref.at[side, slot], extra.at[side, slot], sem.at[side, 4 + slot]
            )
            for slot in range(4)
        ]
        moved = [
            pltpu.make_async_copy(extra.at[side, slot], out.at[block(near)], sem.at[side, slot])
            for slot, out in enumerate((gk_out, gv_out, gq_out))
        ]
        added = [
            pltpu.make_async_copy(own.at[side, slot], out.at[block(at)], sem.at[side, slot])
            for out, at, slot in parts
        ]
        away, shared, both = (flags_ref[3 * side + i] == 1 for i in range(3))
        sides.append((side, ours, theirs, moved, added, away, shared, both))

    for side, ours, theirs, moved, added, away, shared, both in sides:
        for copy in theirs:
            copy.start()

        @pl.when(shared)
        def _():
            for copy in ours:
                copy.start()

    for piece in range(PIECES):
        for tile in range(PIECE // 128):
            lanes = slice(piece * PIECE + tile * 128, piece * PIECE + (tile + 1) * 128)
            part = sum_ref[piece].astype(jnp.float32)[tile * PART : (tile + 1) * PART]
            rows_ref[:, lanes] = part * norm

    att_load.wait()
    for side, ours, theirs, moved, added, away, shared, both in sides:
        for copy in theirs:
            copy.wait()

        @pl.when(away)
        def _():
            att[3 * side * BLOCK : (3 * side + 1) * BLOCK] = extra[side, 3]

        @pl.when(away)
        def _():
            for copy in moved:
                copy.start()

        @pl.when(shared)
        def _():
            for slot in range(4):
                ours[slot].wait()
                total = own[side, slot].astype(jnp.float32)
                other = extra[side, slot].astype(jnp.float32)
                if slot >= 2:
                    other = jnp.where(both, other, 0.0)
                own[side, slot] = (total + other).astype(jnp.bfloat16)
                added[slot].start()

    att_store = pltpu.make_async_copy(att, att_out, att_sem.at[0])
    att_store.start()
    for side, ours, theirs, moved, added, away, shared, both in sides:
        @pl.when(away)
        def _():
            for copy in moved:
                copy.wait()

        @pl.when(shared)
        def _():
            for copy in added:
                copy.wait()

    att_store.wait()


def on_device(q_tokens, k_tokens, v_tokens, d_attended, w_out, lengths):
    rows, width = q_tokens.shape[1:]
    count = lax.axis_size("tok")
    norm = 1.0 / math.sqrt(lax.axis_size("dp") * count * rows)
    q, k, v, dy = q_tokens[0], k_tokens[0], v_tokens[0], d_attended[0]
    low = jnp.bfloat16
    vmem, smem, anywhere = (
        pl.BlockSpec(memory_space=space) for space in (pltpu.VMEM, pltpu.SMEM, pl.ANY)
    )
    token_shape = jax.ShapeDtypeStruct((rows, width), low)
    halo_shape = jax.ShapeDtypeStruct((2, 4, BLOCK, width), low)
    big = 58 * 1024 * 1024

    halo, dm = pl.pallas_call(
        functools.partial(exchange_kernel, count),
        out_shape=(halo_shape, token_shape),
        in_specs=[smem] + [anywhere] * 5,
        out_specs=(anywhere, vmem),
        scratch_shapes=[
            pltpu.VMEM((rows, width), low),
            pltpu.VMEM((width, width), low),
            pltpu.VMEM((2, BLOCK, width), low),
            pltpu.VMEM((2, 2, BLOCK, width), low),
            pltpu.VMEM((2, 2, BLOCK, width), low),
            pltpu.SemaphoreType.DMA((8,)),
            pltpu.SemaphoreType.DMA((2, 4)),
            pltpu.SemaphoreType.DMA((2, 4)),
        ],
        compiler_params=pltpu.CompilerParams(
            collective_id=0, has_side_effects=True, vmem_limit_bytes=big
        ),
        name="exchange",
    )(lengths, q, k, v, dy, w_out)

    dma = pltpu.SemaphoreType.DMA
    slab = pltpu.VMEM((SLOTS * BLOCK, width), low)
    square = pltpu.VMEM((width, width), low)
    sides = pltpu.VMEM((2, BLOCK, width), low)
    mixed_shape = jax.ShapeDtypeStruct(((OWN + 2) * BLOCK, width), low)
    mixed, gq, gk, gv, ret, flags = pl.pallas_call(
        attention_kernel,
        out_shape=(
            mixed_shape, token_shape, token_shape, token_shape, halo_shape,
            jax.ShapeDtypeStruct((6,), jnp.int32),
        ),
        in_specs=[smem] + [anywhere] * 6,
        out_specs=(anywhere,) * 5 + (smem,),
        scratch_shapes=[slab] * 4 + [square, sides] + [slab] * 4
        + [sides, pltpu.SMEM((8, 3), jnp.int32), dma((5,)), dma((2, 4)), dma((4, SLOTS))],
        compiler_params=pltpu.CompilerParams(vmem_limit_bytes=big),
        name="attention",
    )(lengths, q, k, v, dm, halo, w_out)

    sum_shape = jax.ShapeDtypeStruct((PIECES, PACKED, 128), low)

    def pieces(*sizes):
        return pltpu.VMEM((PIECES, *sizes, PACKED, 128), low)

    slab = pltpu.VMEM(mixed_shape.shape, low)
    back, summed, att = pl.pallas_call(
        functools.partial(finish_kernel, count),
        out_shape=(halo_shape, sum_shape, token_shape),
        in_specs=[anywhere] * 5,
        out_specs=(anywhere, vmem, anywhere),
        scratch_shapes=[
            slab, pltpu.VMEM(mixed_shape.shape[::-1], low), slab, square,
            pltpu.VMEM((rows, width), low),
            pltpu.VMEM((width, PIECE), jnp.float32),
            pltpu.VMEM((PACKED, 128), jnp.float32),
            pieces(2, SIDE, SIDE), pieces(SIDE, SIDE), pieces(SIDE, SIDE),
            pieces(SIDE - 1, SIDE), pieces(SIDE), pieces(SIDE - 1),
            pieces(), pieces(SIDE - 1),
            pltpu.VMEM((2, PIECES, PACKED, 128), low),
            dma((5,)), dma((2, 4)), dma((2, 4)), dma((PIECES,)), dma((PIECES,)),
            dma((4, PIECES, SIDE - 1)), dma((4, PIECES, SIDE - 1)),
            sides, dma((2,)), dma((2,)),
        ],
        compiler_params=pltpu.CompilerParams(
            collective_id=1, has_side_effects=True, vmem_limit_bytes=big
        ),
        name="finish",
    )(ret, mixed, dy, halo, w_out)

    att, gq, gk, gv, grad_rows = pl.pallas_call(
        functools.partial(settle_kernel, norm),
        out_shape=(token_shape,) * 4 + (jax.ShapeDtypeStruct((PART, width), jnp.float32),),
        in_specs=[smem, vmem] + [anywhere] * 5,
        out_specs=(anywhere,) * 4 + (vmem,),
        scratch_shapes=[
            pltpu.VMEM((2, 4, BLOCK, width), low),
            pltpu.VMEM((2, 4, BLOCK, width), low),
            pltpu.VMEM((rows, width), low),
            dma((2, 8)), dma((1,)),
        ],
        input_output_aliases={4: 1, 5: 2, 6: 3},
        compiler_params=pltpu.CompilerParams(vmem_limit_bytes=big),
        name="settle",
    )(flags, summed, back, att, gq, gk, gv)
    return (att[None], gq[None], gk[None], gv[None], grad_rows)


def solution(mesh):
    tokens = P("dp", "tok", None)
    return jax.shard_map(
        on_device,
        mesh=mesh,
        in_specs=(tokens, tokens, tokens, tokens, P(), P("dp", None)),
        out_specs=(tokens, tokens, tokens, tokens, P("tok", None)),
        check_vma=False,
    )
```

```python
import functools
import math

import jax
import jax.numpy as jnp
from jax import lax
from jax.experimental import pallas as pl
from jax.experimental.pallas import tpu as pltpu
from jax.sharding import PartitionSpec as P

HEADS = 16
HEAD_DIM = 72
BLOCK = 128
D = 1152
OWN = 4
SLOTS = 8
WINDOW = 256
SCALE = HEAD_DIM ** (-0.5)
EXP2_SCALE = SCALE * math.log2(math.e)
PART = 36
PIECE = 384
PIECES = D // PIECE
PACKED = 112
SIDE = 4
MESH = pl.DeviceIdType.MESH
NN = (((1,), (0,)), ((), ()))
NT = (((1,), (1,)), ((), ()))
TN = (((0,), (0,)), ((), ()))


def dot(a, b, dims):
    return lax.dot_general(a, b, dims, preferred_element_type=jnp.float32)


def boundaries(lengths_ref, edges):
    def step(i, carry):
        start, counts = carry
        end = start + lengths_ref[0, i]
        new = []
        for edge, (before, after) in zip(edges, counts):
            hit = jnp.logical_and(start < edge, end > edge)
            new.append((jnp.where(hit, edge - start, before), jnp.where(hit, end - edge, after)))
        return end, tuple(new)

    zero = jnp.int32(0)
    start = (zero, tuple((zero, zero) for _ in edges))
    return lax.fori_loop(0, lengths_ref.shape[1], step, start)[1]


def plans(lengths_ref, first):
    counts = boundaries(lengths_ref, [first - OWN, first, first + OWN, first + 2 * OWN])

    def is_pair(pair, before, after):
        return jnp.logical_and(pair[0] == before, pair[1] == after)

    result = []
    for at in (1, 2):
        here = counts[at]
        left_full = is_pair(counts[at - 1], 1, 3)
        right_full = is_pair(counts[at + 1], 3, 1)
        only_left = jnp.logical_and(left_full, jnp.logical_not(right_full))
        only_right = jnp.logical_and(right_full, jnp.logical_not(left_full))
        to_left = (
            is_pair(here, 3, 1)
            | (is_pair(here, 2, 1) & right_full)
            | (is_pair(here, 1, 1) & only_right)
        )
        to_right = (
            is_pair(here, 1, 3)
            | (is_pair(here, 1, 2) & left_full)
            | (is_pair(here, 1, 1) & only_left)
        )
        shared = (here[0] > 0) & jnp.logical_not(to_left | to_right)
        result.append((here[0], here[1], to_left, to_right, shared))
    return result


def greet(others):
    for other in others:
        where = other if isinstance(other, dict) else {"tok": other}
        pl.semaphore_signal(
            pltpu.get_barrier_semaphore(), inc=1, device_id=where, device_id_type=MESH
        )


def meet(others):
    pl.semaphore_wait(pltpu.get_barrier_semaphore(), len(others))


def ring_neighbours(count):
    me = lax.axis_index("tok")
    return lax.rem(me + count - 1, count), lax.rem(me + 1, count)


def exchange_kernel(
    count, lengths_ref, q_ref, k_ref, v_ref, dy_ref, w_ref, halo_ref, dm_ref,
    dy_buf, w_buf, near_buf, far_buf, pack, dm_buf, load_sem, send_sem, recv_sem,
):
    left, right = ring_neighbours(count)
    first = lax.axis_index("tok") * OWN
    near = [pl.ds(0, BLOCK), pl.ds(3 * BLOCK, BLOCK)]
    far = [pl.ds(BLOCK, BLOCK), pl.ds(2 * BLOCK, BLOCK)]
    loads = []
    for side in range(2):
        loads += [
            (q_ref.at[near[side]], near_buf.at[side]),
            (k_ref.at[far[side]], far_buf.at[side, 0]),
            (v_ref.at[far[side]], far_buf.at[side, 1]),
        ]
    loads += [(dy_ref, dy_buf), (w_ref, w_buf)]
    loads = [pltpu.make_async_copy(a, b, load_sem.at[i]) for i, (a, b) in enumerate(loads)]
    for load in loads:
        load.start()
    greet((left, right))
    meet((left, right))
    copies = []

    def send(side, slot, source):
        copy = pltpu.make_async_remote_copy(
            src_ref=source,
            dst_ref=halo_ref.at[1 - side, slot],
            send_sem=send_sem.at[side, slot],
            recv_sem=recv_sem.at[1 - side, slot],
            device_id={"tok": right if side else left},
            device_id_type=MESH,
        )
        copy.start()
        copies.append(copy)

    for side in range(2):
        send(side, 0, k_ref.at[near[side]])
        send(side, 1, v_ref.at[near[side]])
    for load in loads[:-1]:
        load.wait()
    edges = plans(lengths_ref, first)
    for side in range(2):
        shared = edges[side][-1]
        pack[side, 0] = jnp.where(shared, far_buf[side, 0], near_buf[side])
        pack[side, 1] = jnp.where(shared, far_buf[side, 1], dy_buf[near[side]])
        send(side, 2, pack.at[side, 0])
        send(side, 3, pack.at[side, 1])
    loads[-1].wait()
    for part in range(OWN):
        rows = slice(part * BLOCK, (part + 1) * BLOCK)
        dm_buf[rows] = dot(dy_buf[rows], w_buf[...], NT).astype(jnp.bfloat16)
    dm_store = pltpu.make_async_copy(dm_buf, dm_ref, load_sem.at[0])
    dm_store.start()
    for copy in copies:
        copy.wait()
    dm_store.wait()


def attend(q_buf, k_buf, v_buf, dm_buf, mixed, gq, gk, gv, q_at, q_blocks, k_at, k_blocks):
    q_rows = pl.ds(pl.multiple_of(q_at * BLOCK, BLOCK), q_blocks * BLOCK)
    k_rows = pl.ds(pl.multiple_of(k_at * BLOCK, BLOCK), k_blocks * BLOCK)
    lane = lax.broadcasted_iota(jnp.int32, (1, WINDOW), 1)

    group = {1: 8, 2: 4, 3: 2, 4: 2}[k_blocks]

    def several(i, carry):
        heads = []
        for j in range(group):
            at = (group * i + j) * HEAD_DIM
            base = jnp.minimum(at // 128, (D - WINDOW) // 128) * 128
            offset = at - base
            window = pl.ds(pl.multiple_of(base, 128), WINDOW)
            inside = jnp.logical_and(lane >= offset, lane < offset + HEAD_DIM)
            keep = jnp.where(inside, 1.0, 0.0).astype(jnp.bfloat16)
            heads.append((offset, window, keep))
        probs_of, ds_of = [], []
        for offset, window, keep in heads:
            scores = dot(k_buf[k_rows, window] * keep, q_buf[q_rows, window], NT)
            d_probs = dot(v_buf[k_rows, window] * keep, dm_buf[q_rows, window], NT)
            top = jnp.max(scores, axis=0, keepdims=True)
            weights = jnp.exp2((scores - top) * EXP2_SCALE)
            probs = weights * (1.0 / jnp.sum(weights, axis=0, keepdims=True))
            product = probs * d_probs
            delta = jnp.sum(product, axis=0, keepdims=True)
            probs_of.append(probs.astype(jnp.bfloat16))
            ds_of.append((product - probs * delta).astype(jnp.bfloat16))
        news = []
        for (offset, window, keep), p, ds in zip(heads, probs_of, ds_of):
            news.append((
                dot(p, v_buf[k_rows, window], TN), dot(p, dm_buf[q_rows, window], NN),
                dot(ds, k_buf[k_rows, window], TN) * SCALE, dot(ds, q_buf[q_rows, window], NN) * SCALE,
            ))
        for (offset, window, keep), new in zip(heads, news):
            for ref, rows, value in zip((mixed, gv, gq, gk), (q_rows, k_rows, q_rows, k_rows), new):
                old = ref[rows, window]
                ref[rows, window] = jnp.where(lane < offset, old, value.astype(jnp.bfloat16))
        return carry

    lax.fori_loop(0, HEADS // group, several, 0)


def attention_kernel(
    lengths_ref, q_ref, k_ref, v_ref, dm_ref, halo_ref, w_ref,
    mixed_out, gq_out, gk_out, gv_out, ret_out, flags_out,
    q_buf, k_buf, v_buf, dm_buf, w_buf, dy_buf, mixed, gq, gk, gv, att, work, sem, halo_sem, store_sem,
):
    first = lax.axis_index("tok") * OWN
    last = first + OWN
    own = pl.ds(2 * BLOCK, OWN * BLOCK)

    def block(i):
        return pl.ds(i * BLOCK, BLOCK)

    loads = [
        (q_ref, q_buf.at[own]), (k_ref, k_buf.at[own]), (v_ref, v_buf.at[own]),
        (dm_ref, dm_buf.at[own]),
    ]
    for i in range(4):
        part = pl.ds(i * (D // 4), D // 4)
        loads.append((w_ref.at[part], w_buf.at[part]))
    loads = [pltpu.make_async_copy(a, b, sem.at[i]) for i, (a, b) in enumerate(loads)]
    loads, w_loads = loads[:4], loads[4:]
    for load in loads:
        load.start()

    left_edge, right_edge = plans(lengths_ref, first)
    l_before, l_after, l_away, l_here, l_shared = left_edge
    r_before, r_after, r_here, r_away, r_shared = right_edge
    flags = (
        l_away, l_shared, l_shared & (l_after == 2), r_away, r_shared, r_shared & (r_before == 2)
    )
    for i, flag in enumerate(flags):
        flags_out[i] = flag.astype(jnp.int32)

    halo_loads = []
    for side, (near, far, here, shared) in enumerate(
        ((1, 0, l_here, l_shared), (6, 7, r_here, r_shared))
    ):
        def load(slot, to, side=side):
            return pltpu.make_async_copy(halo_ref.at[side, slot], to, halo_sem.at[side, slot])

        both = [load(0, k_buf.at[block(near)]), load(1, v_buf.at[block(near)])]
        if_here = [load(2, q_buf.at[block(near)]), load(3, dy_buf.at[side])]
        if_shared = [load(2, k_buf.at[block(far)]), load(3, v_buf.at[block(far)])]
        halo_loads += [(here, both + if_here), (shared, both + if_shared)]
    for flag, some in halo_loads:
        @pl.when(flag)
        def _():
            for load in some:
                load.start()

    for load in w_loads:
        load.start()

    def collect(i, carry):
        start, number = carry
        end = start + lengths_ref[0, i]
        on_left = jnp.logical_and(start < first, end > first)
        on_right = jnp.logical_and(start < last, end > last)
        within = jnp.logical_and(start >= first, end <= last)
        mine = (
            within
            | (on_left & jnp.logical_not(l_away))
            | (on_right & jnp.logical_not(r_away))
        )
        shared = (on_left & l_shared) | (on_right & r_shared)
        own_blocks = jnp.where(on_left, l_after, r_before)

        @pl.when(mine)
        def _():
            k_at = start - first + 2
            work[number, 0] = jnp.where(shared, own_blocks * 8 + end - start, end - start)
            work[number, 1] = jnp.where(shared & on_left, 2, k_at)
            work[number, 2] = k_at

        return end, number + mine.astype(jnp.int32)

    _, number = lax.fori_loop(
        0, lengths_ref.shape[1], collect, (jnp.int32(0), jnp.int32(0))
    )
    for load in loads:
        load.wait()
    for flag, some in halo_loads:
        @pl.when(flag)
        def _():
            for load in some:
                load.wait()

    @pl.when(l_here | r_here)
    def _():
        for load in w_loads:
            load.wait()

    for side, (here, slot) in enumerate(((l_here, 1), (r_here, 6))):
        @pl.when(here)
        def _():
            dm_buf[block(slot)] = dot(dy_buf[side], w_buf[...], NT).astype(jnp.bfloat16)

    bufs = (q_buf, k_buf, v_buf, dm_buf, mixed, gq, gk, gv)

    def store(index, slot):
        if index == 0:
            return pltpu.make_async_copy(
                mixed.at[rows_of(slot)], mixed_out.at[rows_of(slot - 1)], store_sem.at[0, slot]
            )
        ref, out = ((gq, gq_out), (gk, gk_out), (gv, gv_out))[index - 1]
        return pltpu.make_async_copy(
            ref.at[rows_of(slot)], out.at[rows_of(slot - 2)], store_sem.at[index, slot]
        )

    def rows_of(slot):
        return pl.ds(pl.multiple_of(slot * BLOCK, BLOCK), BLOCK)

    def store_all(slot, indices):
        for index in indices:
            if index == 0:
                store(0, slot).start()
            else:
                @pl.when(jnp.logical_and(slot >= 2, slot < 2 + OWN))
                def _():
                    store(index, slot).start()

    def image(i, carry):
        kind, q_at, k_at = work[i, 0], work[i, 1], work[i, 2]
        for q_blocks, k_blocks in ((1, 1), (2, 2), (3, 3), (4, 4), (1, 2), (1, 3), (2, 3), (2, 4)):
            @pl.when(kind == (k_blocks if q_blocks == k_blocks else q_blocks * 8 + k_blocks))
            def _():
                attend(*bufs, q_at, q_blocks, k_at, k_blocks)
                for j in range(q_blocks):
                    store_all(q_at + j, range(4))

        return carry

    lax.fori_loop(0, number, image, 0)

    idle = (
        (jnp.logical_not(l_here), 1), (l_away, 2), (r_away, 5), (jnp.logical_not(r_here), 6)
    )
    for flag, slot in idle:
        @pl.when(flag)
        def _():
            mixed[block(slot)] = jnp.zeros((BLOCK, D), jnp.bfloat16)
            store_all(jnp.int32(slot), range(4))

    def give(side, slot, source):
        return pltpu.make_async_copy(source, ret_out.at[side, slot], halo_sem.at[side, slot])

    gives = []
    for side, (near, far, here, shared) in enumerate(
        ((1, 0, l_here, l_shared), (6, 7, r_here, r_shared))
    ):
        both = [give(side, 0, gk.at[block(near)]), give(side, 1, gv.at[block(near)])]
        if_here = [give(side, 2, gq.at[block(near)]), give(side, 3, att.at[side])]
        if_shared = [give(side, 2, gk.at[block(far)]), give(side, 3, gv.at[block(far)])]

        @pl.when(here)
        def _():
            for copy in both + if_here[:1]:
                copy.start()
            att[side] = dot(mixed[block(near)], w_buf[...], NN).astype(jnp.bfloat16)
            if_here[1].start()

        @pl.when(shared)
        def _():
            for copy in both + if_shared:
                copy.start()

        gives += [(here, both + if_here), (shared, both + if_shared)]
    for flag, some in gives:
        @pl.when(flag)
        def _():
            for copy in some:
                copy.wait()

    @pl.when(jnp.logical_not(l_here | r_here))
    def _():
        for load in w_loads:
            load.wait()

    for slot in range(1, 3 + OWN):
        for index in range(4):
            if index == 0 or 2 <= slot < 2 + OWN:
                store(index, slot).wait()


def finish_kernel(
    count, ret_ref, mixed_ref, dy_ref, halo_ref, w_ref, back_ref, sum_ref, att_ref,
    mixed, turned_mixed, dy, w_buf, att, acc, stage, parts, sibling, total, second, half, third, whole, fourth, fifth,
    load_sem, ret_send, ret_recv, one_send, one_recv, sends, recvs, relay, relay_send, relay_recv,
):
    left, right = ring_neighbours(count)
    me, y = lax.axis_index("tok"), lax.axis_index("dp")
    core, z, x = lax.rem(me, 2), lax.rem(me // 2, SIDE), me // (2 * SIDE)
    loads = []
    for i in range(OWN + 2):
        part = pl.ds(i * BLOCK, BLOCK)
        loads.append((mixed_ref.at[part], mixed.at[part]))
    for i in range(2):
        part = i * 2 * BLOCK
        loads.append((dy_ref.at[pl.ds(part, 2 * BLOCK)], dy.at[pl.ds(part + BLOCK, 2 * BLOCK)]))
    loads += [
        (halo_ref.at[0, 3], dy.at[pl.ds(0, BLOCK)]),
        (halo_ref.at[1, 3], dy.at[pl.ds((OWN + 1) * BLOCK, BLOCK)]),
        (w_ref, w_buf),
    ]
    loads = [pltpu.make_async_copy(a, b, load_sem.at[i]) for i, (a, b) in enumerate(loads)]
    for load in loads:
        load.start()

    def device(x, y, z, core):
        return {"dp": y, "tok": (x * SIDE + z) * 2 + core}

    def turned(at, step):
        return lax.rem(at + step, SIDE)

    other = device(x, y, z, 1 - core)
    steps = range(1, SIDE)
    along_x = [device(turned(x, step), y, z, core) for step in steps]
    along_y = [device(x, turned(y, step), z, core) for step in steps]
    along_z = [device(x, y, turned(z, step), core) for step in steps]
    across = [device(turned(x, step), y, z, 1 - core) for step in (1, SIDE - 1)]
    others = [left, right, other] + across + along_x + along_y + along_z
    at_end = (z == 0) | (z == SIDE - 1)
    crosses = at_end & ((core == 1) == (z == SIDE - 1))
    forwards = at_end & jnp.logical_not(crosses)
    opposite = device(x, y, SIDE - 1 - z, core)
    beyond = device(turned(x, jnp.where(core == 1, 1, SIDE - 1)), y, z, 1 - core)

    def to_forwarder(slot):
        return remote(
            ret_ref.at[core, 2 + slot], relay.at[slot], relay_send.at[slot], relay_recv.at[slot],
            opposite,
        )

    def forward(slot):
        return remote(
            relay.at[slot], back_ref.at[1 - core, 2 + slot],
            relay_send.at[slot], ret_recv.at[1 - core, 2 + slot], beyond,
        )

    def pass_on(slot):
        @pl.when(forwards)
        def _():
            to_forwarder(slot).wait_recv()
            forward(slot).start()

    greet(others)
    copies = []

    def remote(source, landing, send_sem, recv_sem, where):
        return pltpu.make_async_remote_copy(
            src_ref=source, dst_ref=landing, send_sem=send_sem, recv_sem=recv_sem,
            device_id=where, device_id_type=MESH,
        )

    def send(*args):
        copy = remote(*args)
        copy.start()
        copies.append(copy)
        return copy

    for load in loads[:-1]:
        load.wait()
    for tile in range(D // 128):
        lanes = slice(tile * 128, (tile + 1) * 128)
        turned_mixed[lanes] = mixed[:, lanes].T
    stage[...] = jnp.zeros_like(stage)

    def x_first(piece, on_core_0):
        return on_core_0 if piece < PIECES - 1 else False

    def product(piece):
        columns = slice(piece * PIECE, (piece + 1) * PIECE)

        def weight(i, carry):
            at = pl.ds(pl.multiple_of(i * PIECE, PIECE), PIECE)
            acc[at] = dot(turned_mixed[at], dy[:, columns], NN)
            return carry

        lax.fori_loop(0, D // PIECE, weight, 0)
        for part in range(D // PART):
            px, pz, pcore = part // 8, part // 2 % 4, part % 2
            place = (px, pz) if x_first(piece, pcore == 0) else (pz, px)
            for tile in range(PIECE // 128):
                stage[tile * PART : (tile + 1) * PART] = acc[
                    part * PART : (part + 1) * PART, tile * 128 : (tile + 1) * 128
                ]
            parts[piece, pcore, place[0], place[1]] = stage[...].astype(jnp.bfloat16)

    def to_sibling(piece):
        return send(
            parts.at[piece, 1 - core], sibling.at[piece], one_send.at[piece], one_recv.at[piece],
            other,
        )

    def spread(stage_at, piece, source, landing, x_axis):
        at = jnp.where(x_axis, x, y)
        started = []
        for step in steps:
            there = turned(at, step)
            where = device(jnp.where(x_axis, there, x), jnp.where(x_axis, y, there), z, core)
            started.append(send(
                source.at[there], landing.at[step - 1],
                sends.at[stage_at, piece, step - 1], recvs.at[stage_at, piece, step - 1], where,
            ))
        return at, started

    def add(*values):
        result = values[0].astype(jnp.float32)
        for value in values[1:]:
            result = result + value.astype(jnp.float32)
        return result.astype(jnp.bfloat16)

    twos, threes = [], []

    def second_stage(piece):
        one[piece].wait_recv()
        for row in range(SIDE):
            total[piece, row] = add(parts[piece, core, row], sibling[piece, row])
        twos.append(spread(0, piece, total.at[piece], second.at[piece], x_first(piece, core == 0)))

    def third_stage(piece):
        at, started = twos[piece]
        for copy in started:
            copy.wait_recv()
        half[piece] = add(total[piece, at], *[second[piece, step - 1] for step in steps])
        threes.append(spread(1, piece, half.at[piece], third.at[piece], jnp.logical_not(x_first(piece, core == 0))))

    product(0)
    meet(others)
    one = [to_sibling(0)]
    @pl.when(crosses)
    def _():
        for slot in range(2):
            to_forwarder(slot).start()

    returns = []
    for side in range(2):
        for slot in range(4):
            copy = remote(
                ret_ref.at[side, slot], back_ref.at[1 - side, slot],
                ret_send.at[side, slot], ret_recv.at[1 - side, slot],
                {"tok": right if side else left},
            )
            over_x = crosses & (core == side)
            returns.append((copy, over_x, slot))

            @pl.when(jnp.logical_not(over_x))
            def _():
                copy.start()

    for piece in range(1, PIECES):
        product(piece)
        one.append(to_sibling(piece))
        second_stage(piece - 1)
    second_stage(PIECES - 1)
    for copy, over_x, slot in returns:
        if slot < 2:
            @pl.when(over_x)
            def _():
                copy.start()

    loads[-1].wait()
    for part in range(OWN):
        rows = slice(part * BLOCK, (part + 1) * BLOCK)
        ours = mixed[(part + 1) * BLOCK : (part + 2) * BLOCK]
        att[rows] = dot(ours, w_buf[...], NN).astype(jnp.bfloat16)
    att_store = pltpu.make_async_copy(att, att_ref, load_sem.at[0])
    att_store.start()
    for piece in range(PIECES):
        third_stage(piece)
    pass_on(0)
    pass_on(1)

    gap = lax.rem(z - y + SIDE, SIDE)

    def to_plane(piece, step):
        return remote(
            whole.at[piece], fourth.at[piece, step - 1],
            sends.at[2, piece, step - 1], recvs.at[2, piece, step - 1],
            device(x, y, turned(z, SIDE - step), core),
        )

    def to_row(piece, step):
        return remote(
            fifth.at[0, piece], fifth.at[1, piece],
            sends.at[3, piece, step - 1], recvs.at[3, piece, 0],
            device(x, turned(y, step), z, core),
        )

    for piece in range(PIECES):
        at, started = threes[piece]
        for copy in started:
            copy.wait_recv()
        whole[piece] = add(half[piece, at], *[third[piece, step - 1] for step in steps])
        for step in steps:
            @pl.when(gap == step)
            def _():
                to_plane(piece, step).start()

    @pl.when(gap == 0)
    def _():
        for piece in range(PIECES):
            for step in steps:
                to_plane(piece, step).wait_recv()
            fifth[0, piece] = add(whole[piece], *[fourth[piece, step - 1] for step in steps])
            for step in steps:
                to_row(piece, step).start()
        for piece in range(PIECES):
            for step in steps:
                to_row(piece, step).wait_send()
        sum_ref[...] = fifth[0]

    @pl.when(gap != 0)
    def _():
        for piece in range(PIECES):
            to_row(piece, 1).wait_recv()
        sum_ref[...] = fifth[1]

    for piece in range(PIECES):
        for step in steps:
            @pl.when(gap == step)
            def _():
                to_plane(piece, step).wait_send()

    for copy, over_x, slot in returns:
        copy.wait_recv()

        @pl.when(True if slot < 2 else jnp.logical_not(over_x))
        def _():
            copy.wait_send()

    @pl.when(crosses)
    def _():
        for slot in range(2):
            to_forwarder(slot).wait_send()

    @pl.when(forwards)
    def _():
        for slot in range(2):
            forward(slot).wait_send()

    for copy in copies:
        copy.wait_send()
    att_store.wait()


def settle_kernel(
    norm, flags_ref, sum_ref, back_ref, att_in, gq_in, gk_in, gv_in,
    att_out, gq_out, gk_out, gv_out, rows_ref, own, extra, att, sem, att_sem,
):
    def block(i):
        return pl.ds(i * BLOCK, BLOCK)

    att_loads = [
        pltpu.make_async_copy(att_in.at[block(i)], att.at[block(i)], att_sem.at[i])
        for i in range(OWN)
    ]
    att_stores = [
        pltpu.make_async_copy(att.at[block(i)], att_out.at[block(i)], att_sem.at[i])
        for i in range(OWN)
    ]
    for copy in att_loads:
        copy.start()
    sides = []
    for side, (near, far) in enumerate(((0, 1), (3, 2))):
        parts = ((gk_out, near, 0), (gv_out, near, 1), (gk_out, far, 2), (gv_out, far, 3))
        ours = [
            pltpu.make_async_copy(out.at[block(at)], own.at[side, slot], sem.at[side, slot])
            for out, at, slot in parts
        ]
        theirs = [
            pltpu.make_async_copy(
                back_ref.at[side, slot], extra.at[side, slot], sem.at[side, 4 + slot]
            )
            for slot in range(4)
        ]
        moved = [
            pltpu.make_async_copy(extra.at[side, slot], out.at[block(near)], sem.at[side, slot])
            for slot, out in enumerate((gk_out, gv_out, gq_out))
        ]
        added = [
            pltpu.make_async_copy(own.at[side, slot], out.at[block(at)], sem.at[side, slot])
            for out, at, slot in parts
        ]
        away, shared, both = (flags_ref[3 * side + i] == 1 for i in range(3))
        sides.append((side, ours, theirs, moved, added, away, shared, both))

    for side, ours, theirs, moved, added, away, shared, both in sides:
        @pl.when(jnp.logical_or(away, shared))
        def _():
            for copy in theirs:
                copy.start()

        @pl.when(shared)
        def _():
            for copy in ours:
                copy.start()

    for piece in range(PIECES):
        for tile in range(PIECE // 128):
            lanes = slice(piece * PIECE + tile * 128, piece * PIECE + (tile + 1) * 128)
            part = sum_ref[piece].astype(jnp.float32)[tile * PART : (tile + 1) * PART]
            rows_ref[:, lanes] = part * norm

    for copy in att_loads:
        copy.wait()
    for side, ours, theirs, moved, added, away, shared, both in sides:
        @pl.when(jnp.logical_or(away, shared))
        def _():
            for copy in theirs:
                copy.wait()

        @pl.when(away)
        def _():
            att[3 * side * BLOCK : (3 * side + 1) * BLOCK] = extra[side, 3]

        att_stores[3 * side].start()
        att_stores[1 + side].start()

        @pl.when(away)
        def _():
            for copy in moved:
                copy.start()

        @pl.when(shared)
        def _():
            for slot in range(4):
                ours[slot].wait()
                total = own[side, slot].astype(jnp.float32)
                other = extra[side, slot].astype(jnp.float32)
                if slot >= 2:
                    other = jnp.where(both, other, 0.0)
                own[side, slot] = (total + other).astype(jnp.bfloat16)
                added[slot].start()

    for side, ours, theirs, moved, added, away, shared, both in sides:
        @pl.when(away)
        def _():
            for copy in moved:
                copy.wait()

        @pl.when(shared)
        def _():
            for copy in added:
                copy.wait()

    for copy in att_stores:
        copy.wait()


def on_device(q_tokens, k_tokens, v_tokens, d_attended, w_out, lengths):
    rows, width = q_tokens.shape[1:]
    count = lax.axis_size("tok")
    norm = 1.0 / math.sqrt(lax.axis_size("dp") * count * rows)
    q, k, v, dy = q_tokens[0], k_tokens[0], v_tokens[0], d_attended[0]
    low = jnp.bfloat16
    vmem, smem, anywhere = (
        pl.BlockSpec(memory_space=space) for space in (pltpu.VMEM, pltpu.SMEM, pl.ANY)
    )
    token_shape = jax.ShapeDtypeStruct((rows, width), low)
    halo_shape = jax.ShapeDtypeStruct((2, 4, BLOCK, width), low)
    big = 58 * 1024 * 1024

    halo, dm = pl.pallas_call(
        functools.partial(exchange_kernel, count),
        out_shape=(halo_shape, token_shape),
        in_specs=[smem] + [anywhere] * 5,
        out_specs=(anywhere, anywhere),
        scratch_shapes=[
            pltpu.VMEM((rows, width), low),
            pltpu.VMEM((width, width), low),
            pltpu.VMEM((2, BLOCK, width), low),
            pltpu.VMEM((2, 2, BLOCK, width), low),
            pltpu.VMEM((2, 2, BLOCK, width), low),
            pltpu.VMEM((rows, width), low),
            pltpu.SemaphoreType.DMA((8,)),
            pltpu.SemaphoreType.DMA((2, 4)),
            pltpu.SemaphoreType.DMA((2, 4)),
        ],
        compiler_params=pltpu.CompilerParams(
            collective_id=0, has_side_effects=True, vmem_limit_bytes=big
        ),
        name="exchange",
    )(lengths, q, k, v, dy, w_out)

    dma = pltpu.SemaphoreType.DMA
    slab = pltpu.VMEM((SLOTS * BLOCK, width), low)
    square = pltpu.VMEM((width, width), low)
    sides = pltpu.VMEM((2, BLOCK, width), low)
    mixed_shape = jax.ShapeDtypeStruct(((OWN + 2) * BLOCK, width), low)
    mixed, gq, gk, gv, ret, flags = pl.pallas_call(
        attention_kernel,
        out_shape=(
            mixed_shape, token_shape, token_shape, token_shape, halo_shape,
            jax.ShapeDtypeStruct((6,), jnp.int32),
        ),
        in_specs=[smem] + [anywhere] * 6,
        out_specs=(anywhere,) * 5 + (smem,),
        scratch_shapes=[slab] * 4 + [square, sides] + [slab] * 4
        + [sides, pltpu.SMEM((8, 3), jnp.int32), dma((8,)), dma((2, 4)), dma((4, SLOTS))],
        compiler_params=pltpu.CompilerParams(vmem_limit_bytes=big),
        name="attention",
    )(lengths, q, k, v, dm, halo, w_out)

    sum_shape = jax.ShapeDtypeStruct((PIECES, PACKED, 128), low)

    def pieces(*sizes):
        return pltpu.VMEM((PIECES, *sizes, PACKED, 128), low)

    slab = pltpu.VMEM(mixed_shape.shape, low)
    back, summed, att = pl.pallas_call(
        functools.partial(finish_kernel, count),
        out_shape=(halo_shape, sum_shape, token_shape),
        in_specs=[anywhere] * 5,
        out_specs=(anywhere, vmem, anywhere),
        scratch_shapes=[
            slab, pltpu.VMEM(mixed_shape.shape[::-1], low), slab, square,
            pltpu.VMEM((rows, width), low),
            pltpu.VMEM((width, PIECE), jnp.float32),
            pltpu.VMEM((PACKED, 128), jnp.float32),
            pieces(2, SIDE, SIDE), pieces(SIDE, SIDE), pieces(SIDE, SIDE),
            pieces(SIDE - 1, SIDE), pieces(SIDE), pieces(SIDE - 1),
            pieces(), pieces(SIDE - 1),
            pltpu.VMEM((2, PIECES, PACKED, 128), low),
            dma((11,)), dma((2, 4)), dma((2, 4)), dma((PIECES,)), dma((PIECES,)),
            dma((4, PIECES, SIDE - 1)), dma((4, PIECES, SIDE - 1)),
            sides, dma((2,)), dma((2,)),
        ],
        compiler_params=pltpu.CompilerParams(
            collective_id=1, has_side_effects=True, vmem_limit_bytes=big
        ),
        name="finish",
    )(ret, mixed, dy, halo, w_out)

    att, gq, gk, gv, grad_rows = pl.pallas_call(
        functools.partial(settle_kernel, norm),
        out_shape=(token_shape,) * 4 + (jax.ShapeDtypeStruct((PART, width), jnp.float32),),
        in_specs=[smem, vmem] + [anywhere] * 5,
        out_specs=(anywhere,) * 4 + (vmem,),
        scratch_shapes=[
            pltpu.VMEM((2, 4, BLOCK, width), low),
            pltpu.VMEM((2, 4, BLOCK, width), low),
            pltpu.VMEM((rows, width), low),
            dma((2, 8)), dma((OWN,)),
        ],
        input_output_aliases={4: 1, 5: 2, 6: 3},
        compiler_params=pltpu.CompilerParams(vmem_limit_bytes=big),
        name="settle",
    )(flags, summed, back, att, gq, gk, gv)
    return (att[None], gq[None], gk[None], gv[None], grad_rows)


def solution(mesh):
    tokens = P("dp", "tok", None)
    return jax.shard_map(
        on_device,
        mesh=mesh,
        in_specs=(tokens, tokens, tokens, tokens, P(), P("dp", None)),
        out_specs=(tokens, tokens, tokens, tokens, P("tok", None)),
        check_vma=False,
    )
```

```python
import functools
import math

import jax
import jax.numpy as jnp
from jax import lax
from jax.experimental import pallas as pl
from jax.experimental.pallas import tpu as pltpu
from jax.sharding import PartitionSpec as P

HEADS = 16
HEAD_DIM = 72
BLOCK = 128
D = 1152
OWN = 4
SLOTS = 8
WINDOW = 256
SCALE = HEAD_DIM ** (-0.5)
EXP2_SCALE = SCALE * math.log2(math.e)
PART = 36
PIECE = 384
PIECES = D // PIECE
PACKED = 112
SIDE = 4
MESH = pl.DeviceIdType.MESH
NN = (((1,), (0,)), ((), ()))
NT = (((1,), (1,)), ((), ()))
TN = (((0,), (0,)), ((), ()))


def dot(a, b, dims):
    return lax.dot_general(a, b, dims, preferred_element_type=jnp.float32)


def boundaries(lengths_ref, edges):
    def step(i, carry):
        start, counts = carry
        end = start + lengths_ref[0, i]
        new = []
        for edge, (before, after) in zip(edges, counts):
            hit = jnp.logical_and(start < edge, end > edge)
            new.append((jnp.where(hit, edge - start, before), jnp.where(hit, end - edge, after)))
        return end, tuple(new)

    zero = jnp.int32(0)
    start = (zero, tuple((zero, zero) for _ in edges))
    return lax.fori_loop(0, lengths_ref.shape[1], step, start)[1]


def plans(lengths_ref, first):
    counts = boundaries(lengths_ref, [first - OWN, first, first + OWN, first + 2 * OWN])

    def is_pair(pair, before, after):
        return jnp.logical_and(pair[0] == before, pair[1] == after)

    result = []
    for at in (1, 2):
        here = counts[at]
        left_full = is_pair(counts[at - 1], 1, 3)
        right_full = is_pair(counts[at + 1], 3, 1)
        only_left = jnp.logical_and(left_full, jnp.logical_not(right_full))
        only_right = jnp.logical_and(right_full, jnp.logical_not(left_full))
        to_left = (
            is_pair(here, 3, 1)
            | (is_pair(here, 2, 1) & right_full)
            | (is_pair(here, 1, 1) & only_right)
        )
        to_right = (
            is_pair(here, 1, 3)
            | (is_pair(here, 1, 2) & left_full)
            | (is_pair(here, 1, 1) & only_left)
        )
        shared = (here[0] > 0) & jnp.logical_not(to_left | to_right)
        result.append((here[0], here[1], to_left, to_right, shared))
    return result


def greet(others):
    for other in others:
        where = other if isinstance(other, dict) else {"tok": other}
        pl.semaphore_signal(
            pltpu.get_barrier_semaphore(), inc=1, device_id=where, device_id_type=MESH
        )


def meet(others):
    pl.semaphore_wait(pltpu.get_barrier_semaphore(), len(others))


def ring_neighbours(count):
    me = lax.axis_index("tok")
    return lax.rem(me + count - 1, count), lax.rem(me + 1, count)


def exchange_kernel(
    count, lengths_ref, q_ref, k_ref, v_ref, dy_ref, w_ref, halo_ref, dm_ref,
    dy_buf, w_buf, near_buf, far_buf, pack, dm_buf, load_sem, send_sem, recv_sem,
):
    left, right = ring_neighbours(count)
    first = lax.axis_index("tok") * OWN
    near = [pl.ds(0, BLOCK), pl.ds(3 * BLOCK, BLOCK)]
    far = [pl.ds(BLOCK, BLOCK), pl.ds(2 * BLOCK, BLOCK)]
    loads = []
    for side in range(2):
        loads += [
            (q_ref.at[near[side]], near_buf.at[side]),
            (k_ref.at[far[side]], far_buf.at[side, 0]),
            (v_ref.at[far[side]], far_buf.at[side, 1]),
        ]
    loads += [(dy_ref, dy_buf), (w_ref, w_buf)]
    loads = [pltpu.make_async_copy(a, b, load_sem.at[i]) for i, (a, b) in enumerate(loads)]
    for load in loads:
        load.start()
    greet((left, right))
    meet((left, right))
    copies = []

    def send(side, slot, source):
        copy = pltpu.make_async_remote_copy(
            src_ref=source,
            dst_ref=halo_ref.at[1 - side, slot],
            send_sem=send_sem.at[side, slot],
            recv_sem=recv_sem.at[1 - side, slot],
            device_id={"tok": right if side else left},
            device_id_type=MESH,
        )
        copy.start()
        copies.append(copy)

    for side in range(2):
        send(side, 0, k_ref.at[near[side]])
        send(side, 1, v_ref.at[near[side]])
    for load in loads[:-1]:
        load.wait()
    edges = plans(lengths_ref, first)
    for side in range(2):
        shared = edges[side][-1]
        pack[side, 0] = jnp.where(shared, far_buf[side, 0], near_buf[side])
        pack[side, 1] = jnp.where(shared, far_buf[side, 1], dy_buf[near[side]])
        send(side, 2, pack.at[side, 0])
        send(side, 3, pack.at[side, 1])
    loads[-1].wait()
    for part in range(OWN):
        rows = slice(part * BLOCK, (part + 1) * BLOCK)
        dm_buf[rows] = dot(dy_buf[rows], w_buf[...], NT).astype(jnp.bfloat16)
    dm_store = pltpu.make_async_copy(dm_buf, dm_ref, load_sem.at[0])
    dm_store.start()
    for copy in copies:
        copy.wait()
    dm_store.wait()


def attend(q_buf, k_buf, v_buf, dm_buf, mixed, gq, gk, gv, q_at, q_blocks, k_at, k_blocks):
    q_rows = pl.ds(pl.multiple_of(q_at * BLOCK, BLOCK), q_blocks * BLOCK)
    k_rows = pl.ds(pl.multiple_of(k_at * BLOCK, BLOCK), k_blocks * BLOCK)
    lane = lax.broadcasted_iota(jnp.int32, (1, WINDOW), 1)

    group = {1: 8, 2: 8, 3: 4, 4: 8}[k_blocks]

    def several(i, carry):
        heads = []
        for j in range(group):
            at = (group * i + j) * HEAD_DIM
            base = jnp.minimum(at // 128, (D - WINDOW) // 128) * 128
            offset = at - base
            window = pl.ds(pl.multiple_of(base, 128), WINDOW)
            inside = jnp.logical_and(lane >= offset, lane < offset + HEAD_DIM)
            keep = jnp.where(inside, 1.0, 0.0).astype(jnp.bfloat16)
            heads.append((offset, window, keep))
        def score(head):
            offset, window, keep = head
            return (
                dot(k_buf[k_rows, window] * keep, q_buf[q_rows, window], NT),
                dot(v_buf[k_rows, window] * keep, dm_buf[q_rows, window], NT),
            )

        def soften(scores, d_probs):
            top = jnp.max(scores, axis=0, keepdims=True)
            weights = jnp.exp2((scores - top) * EXP2_SCALE)
            probs = weights * (1.0 / jnp.sum(weights, axis=0, keepdims=True))
            probs_low = probs.astype(jnp.bfloat16)
            delta = jnp.sum(probs * d_probs, axis=0, keepdims=True)
            return probs_low, probs_low * (d_probs - delta).astype(jnp.bfloat16)

        def combine(head, p, ds):
            offset, window, keep = head
            return (
                dot(p, v_buf[k_rows, window], TN), dot(p, dm_buf[q_rows, window], NN),
                dot(ds, k_buf[k_rows, window], TN) * SCALE, dot(ds, q_buf[q_rows, window], NN) * SCALE,
            )

        news = []
        raw = score(heads[0])
        for at, head in enumerate(heads):
            soft = soften(*raw)
            if at + 1 < len(heads):
                raw = score(heads[at + 1])
            news.append(combine(head, *soft))

        for (offset, window, keep), new in zip(heads, news):
            for ref, rows, value in zip((mixed, gv, gq, gk), (q_rows, k_rows, q_rows, k_rows), new):
                old = ref[rows, window]
                ref[rows, window] = jnp.where(lane < offset, old, value.astype(jnp.bfloat16))
        return carry

    lax.fori_loop(0, HEADS // group, several, 0)


def attention_kernel(
    lengths_ref, q_ref, k_ref, v_ref, dm_ref, halo_ref, w_ref,
    mixed_out, gq_out, gk_out, gv_out, ret_out, flags_out,
    q_buf, k_buf, v_buf, dm_buf, w_buf, dy_buf, mixed, gq, gk, gv, att, work, sem, halo_sem, store_sem,
):
    first = lax.axis_index("tok") * OWN
    last = first + OWN
    own = pl.ds(2 * BLOCK, OWN * BLOCK)

    def block(i):
        return pl.ds(i * BLOCK, BLOCK)

    loads = [
        (q_ref, q_buf.at[own]), (k_ref, k_buf.at[own]), (v_ref, v_buf.at[own]),
        (dm_ref, dm_buf.at[own]),
    ]
    for i in range(4):
        part = pl.ds(i * (D // 4), D // 4)
        loads.append((w_ref.at[part], w_buf.at[part]))
    loads = [pltpu.make_async_copy(a, b, sem.at[i]) for i, (a, b) in enumerate(loads)]
    loads, w_loads = loads[:4], loads[4:]
    for load in loads:
        load.start()

    left_edge, right_edge = plans(lengths_ref, first)
    l_before, l_after, l_away, l_here, l_shared = left_edge
    r_before, r_after, r_here, r_away, r_shared = right_edge
    flags = (
        l_away, l_shared, l_shared & (l_after == 2), r_away, r_shared, r_shared & (r_before == 2)
    )
    for i, flag in enumerate(flags):
        flags_out[i] = flag.astype(jnp.int32)

    halo_loads = []
    for side, (near, far, here, shared) in enumerate(
        ((1, 0, l_here, l_shared), (6, 7, r_here, r_shared))
    ):
        def load(slot, to, side=side):
            return pltpu.make_async_copy(halo_ref.at[side, slot], to, halo_sem.at[side, slot])

        both = [load(0, k_buf.at[block(near)]), load(1, v_buf.at[block(near)])]
        if_here = [load(2, q_buf.at[block(near)]), load(3, dy_buf.at[side])]
        if_shared = [load(2, k_buf.at[block(far)]), load(3, v_buf.at[block(far)])]
        halo_loads += [(here, both + if_here), (shared, both + if_shared)]
    for flag, some in halo_loads:
        @pl.when(flag)
        def _():
            for load in some:
                load.start()

    for load in w_loads:
        load.start()

    def collect(i, carry):
        start, number = carry
        end = start + lengths_ref[0, i]
        on_left = jnp.logical_and(start < first, end > first)
        on_right = jnp.logical_and(start < last, end > last)
        within = jnp.logical_and(start >= first, end <= last)
        mine = (
            within
            | (on_left & jnp.logical_not(l_away))
            | (on_right & jnp.logical_not(r_away))
        )
        shared = (on_left & l_shared) | (on_right & r_shared)
        own_blocks = jnp.where(on_left, l_after, r_before)

        @pl.when(mine)
        def _():
            k_at = start - first + 2
            work[number, 0] = jnp.where(shared, own_blocks * 8 + end - start, end - start)
            work[number, 1] = jnp.where(shared & on_left, 2, k_at)
            work[number, 2] = k_at

        return end, number + mine.astype(jnp.int32)

    _, number = lax.fori_loop(
        0, lengths_ref.shape[1], collect, (jnp.int32(0), jnp.int32(0))
    )
    for load in loads:
        load.wait()
    for flag, some in halo_loads:
        @pl.when(flag)
        def _():
            for load in some:
                load.wait()

    @pl.when(l_here | r_here)
    def _():
        for load in w_loads:
            load.wait()

    for side, (here, slot) in enumerate(((l_here, 1), (r_here, 6))):
        @pl.when(here)
        def _():
            dm_buf[block(slot)] = dot(dy_buf[side], w_buf[...], NT).astype(jnp.bfloat16)

    bufs = (q_buf, k_buf, v_buf, dm_buf, mixed, gq, gk, gv)

    def store(index, slot):
        if index == 0:
            return pltpu.make_async_copy(
                mixed.at[rows_of(slot)], mixed_out.at[rows_of(slot - 1)], store_sem.at[0, slot]
            )
        ref, out = ((gq, gq_out), (gk, gk_out), (gv, gv_out))[index - 1]
        return pltpu.make_async_copy(
            ref.at[rows_of(slot)], out.at[rows_of(slot - 2)], store_sem.at[index, slot]
        )

    def rows_of(slot):
        return pl.ds(pl.multiple_of(slot * BLOCK, BLOCK), BLOCK)

    def store_all(slot, indices):
        for index in indices:
            if index == 0:
                store(0, slot).start()
            else:
                @pl.when(jnp.logical_and(slot >= 2, slot < 2 + OWN))
                def _():
                    store(index, slot).start()

    def image(i, carry):
        kind, q_at, k_at = work[i, 0], work[i, 1], work[i, 2]
        for q_blocks, k_blocks in ((1, 1), (2, 2), (3, 3), (4, 4), (1, 2), (1, 3), (2, 3), (2, 4)):
            @pl.when(kind == (k_blocks if q_blocks == k_blocks else q_blocks * 8 + k_blocks))
            def _():
                attend(*bufs, q_at, q_blocks, k_at, k_blocks)
                for j in range(q_blocks):
                    store_all(q_at + j, range(4))

        return carry

    lax.fori_loop(0, number, image, 0)

    idle = (
        (jnp.logical_not(l_here), 1), (l_away, 2), (r_away, 5), (jnp.logical_not(r_here), 6)
    )
    for flag, slot in idle:
        @pl.when(flag)
        def _():
            mixed[block(slot)] = jnp.zeros((BLOCK, D), jnp.bfloat16)
            store_all(jnp.int32(slot), range(4))

    def give(side, slot, source):
        return pltpu.make_async_copy(source, ret_out.at[side, slot], halo_sem.at[side, slot])

    gives = []
    for side, (near, far, here, shared) in enumerate(
        ((1, 0, l_here, l_shared), (6, 7, r_here, r_shared))
    ):
        both = [give(side, 0, gk.at[block(near)]), give(side, 1, gv.at[block(near)])]
        if_here = [give(side, 2, gq.at[block(near)]), give(side, 3, att.at[side])]
        if_shared = [give(side, 2, gk.at[block(far)]), give(side, 3, gv.at[block(far)])]

        @pl.when(here)
        def _():
            for copy in both + if_here[:1]:
                copy.start()
            att[side] = dot(mixed[block(near)], w_buf[...], NN).astype(jnp.bfloat16)
            if_here[1].start()

        @pl.when(shared)
        def _():
            for copy in both + if_shared:
                copy.start()

        gives += [(here, both + if_here), (shared, both + if_shared)]
    for flag, some in gives:
        @pl.when(flag)
        def _():
            for copy in some:
                copy.wait()

    @pl.when(jnp.logical_not(l_here | r_here))
    def _():
        for load in w_loads:
            load.wait()

    for slot in range(1, 3 + OWN):
        for index in range(4):
            if index == 0 or 2 <= slot < 2 + OWN:
                store(index, slot).wait()


def finish_kernel(
    count, ret_ref, mixed_ref, dy_ref, halo_ref, w_ref, back_ref, sum_ref, att_ref,
    mixed, turned_mixed, dy, w_buf, att, acc, stage, parts, sibling, total, second, half, third, whole, fourth, fifth,
    load_sem, ret_send, ret_recv, one_send, one_recv, sends, recvs, relay, relay_send, relay_recv,
):
    left, right = ring_neighbours(count)
    me, y = lax.axis_index("tok"), lax.axis_index("dp")
    core, z, x = lax.rem(me, 2), lax.rem(me // 2, SIDE), me // (2 * SIDE)
    loads = []
    for i in range(OWN + 2):
        part = pl.ds(i * BLOCK, BLOCK)
        loads.append((mixed_ref.at[part], mixed.at[part]))
    for i in range(2):
        part = i * 2 * BLOCK
        loads.append((dy_ref.at[pl.ds(part, 2 * BLOCK)], dy.at[pl.ds(part + BLOCK, 2 * BLOCK)]))
    loads += [
        (halo_ref.at[0, 3], dy.at[pl.ds(0, BLOCK)]),
        (halo_ref.at[1, 3], dy.at[pl.ds((OWN + 1) * BLOCK, BLOCK)]),
        (w_ref, w_buf),
    ]
    loads = [pltpu.make_async_copy(a, b, load_sem.at[i]) for i, (a, b) in enumerate(loads)]
    for load in loads:
        load.start()

    def device(x, y, z, core):
        return {"dp": y, "tok": (x * SIDE + z) * 2 + core}

    def turned(at, step):
        return lax.rem(at + step, SIDE)

    other = device(x, y, z, 1 - core)
    steps = range(1, SIDE)
    along_x = [device(turned(x, step), y, z, core) for step in steps]
    along_y = [device(x, turned(y, step), z, core) for step in steps]
    along_z = [device(x, y, turned(z, step), core) for step in steps]
    across = [device(turned(x, step), y, z, 1 - core) for step in (1, SIDE - 1)]
    others = [left, right, other] + across + along_x + along_y + along_z
    at_end = (z == 0) | (z == SIDE - 1)
    crosses = at_end & ((core == 1) == (z == SIDE - 1))
    forwards = at_end & jnp.logical_not(crosses)
    opposite = device(x, y, SIDE - 1 - z, core)
    beyond = device(turned(x, jnp.where(core == 1, 1, SIDE - 1)), y, z, 1 - core)

    def to_forwarder(slot):
        return remote(
            ret_ref.at[core, 2 + slot], relay.at[slot], relay_send.at[slot], relay_recv.at[slot],
            opposite,
        )

    def forward(slot):
        return remote(
            relay.at[slot], back_ref.at[1 - core, 2 + slot],
            relay_send.at[slot], ret_recv.at[1 - core, 2 + slot], beyond,
        )

    def pass_on(slot):
        @pl.when(forwards)
        def _():
            to_forwarder(slot).wait_recv()
            forward(slot).start()

    greet(others)
    copies = []

    def remote(source, landing, send_sem, recv_sem, where):
        return pltpu.make_async_remote_copy(
            src_ref=source, dst_ref=landing, send_sem=send_sem, recv_sem=recv_sem,
            device_id=where, device_id_type=MESH,
        )

    def send(*args):
        copy = remote(*args)
        copy.start()
        copies.append(copy)
        return copy

    for load in loads[:-1]:
        load.wait()
    for tile in range(D // 128):
        lanes = slice(tile * 128, (tile + 1) * 128)
        turned_mixed[lanes] = mixed[:, lanes].T
    stage[...] = jnp.zeros_like(stage)

    def x_first(piece, on_core_0):
        return on_core_0 if piece < PIECES - 1 else False

    def product(piece):
        columns = slice(piece * PIECE, (piece + 1) * PIECE)

        def weight(i, carry):
            at = pl.ds(pl.multiple_of(i * PIECE, PIECE), PIECE)
            acc[at] = dot(turned_mixed[at], dy[:, columns], NN)
            return carry

        lax.fori_loop(0, D // PIECE, weight, 0)
        for part in range(D // PART):
            px, pz, pcore = part // 8, part // 2 % 4, part % 2
            place = (px, pz) if x_first(piece, pcore == 0) else (pz, px)
            for tile in range(PIECE // 128):
                stage[tile * PART : (tile + 1) * PART] = acc[
                    part * PART : (part + 1) * PART, tile * 128 : (tile + 1) * 128
                ]
            parts[piece, pcore, place[0], place[1]] = stage[...].astype(jnp.bfloat16)

    def to_sibling(piece):
        return send(
            parts.at[piece, 1 - core], sibling.at[piece], one_send.at[piece], one_recv.at[piece],
            other,
        )

    def spread(stage_at, piece, source, landing, x_axis):
        at = jnp.where(x_axis, x, y)
        started = []
        for step in steps:
            there = turned(at, step)
            where = device(jnp.where(x_axis, there, x), jnp.where(x_axis, y, there), z, core)
            started.append(send(
                source.at[there], landing.at[step - 1],
                sends.at[stage_at, piece, step - 1], recvs.at[stage_at, piece, step - 1], where,
            ))
        return at, started

    def add(*values):
        result = values[0].astype(jnp.float32)
        for value in values[1:]:
            result = result + value.astype(jnp.float32)
        return result.astype(jnp.bfloat16)

    twos, threes = [], []

    def second_stage(piece):
        one[piece].wait_recv()
        for row in range(SIDE):
            total[piece, row] = add(parts[piece, core, row], sibling[piece, row])
        twos.append(spread(0, piece, total.at[piece], second.at[piece], x_first(piece, core == 0)))

    def third_stage(piece):
        at, started = twos[piece]
        for copy in started:
            copy.wait_recv()
        half[piece] = add(total[piece, at], *[second[piece, step - 1] for step in steps])
        threes.append(spread(1, piece, half.at[piece], third.at[piece], jnp.logical_not(x_first(piece, core == 0))))

    product(0)
    meet(others)
    one = [to_sibling(0)]
    @pl.when(crosses)
    def _():
        for slot in range(2):
            to_forwarder(slot).start()

    returns = []
    for side in range(2):
        for slot in range(4):
            copy = remote(
                ret_ref.at[side, slot], back_ref.at[1 - side, slot],
                ret_send.at[side, slot], ret_recv.at[1 - side, slot],
                {"tok": right if side else left},
            )
            over_x = crosses & (core == side)
            returns.append((copy, over_x, slot))

            @pl.when(jnp.logical_not(over_x))
            def _():
                copy.start()

    for piece in range(1, PIECES):
        product(piece)
        one.append(to_sibling(piece))
        second_stage(piece - 1)
    second_stage(PIECES - 1)
    for copy, over_x, slot in returns:
        if slot < 2:
            @pl.when(over_x)
            def _():
                copy.start()

    loads[-1].wait()
    for part in range(OWN):
        rows = slice(part * BLOCK, (part + 1) * BLOCK)
        ours = mixed[(part + 1) * BLOCK : (part + 2) * BLOCK]
        att[rows] = dot(ours, w_buf[...], NN).astype(jnp.bfloat16)
    att_store = pltpu.make_async_copy(att, att_ref, load_sem.at[0])
    att_store.start()
    for piece in range(PIECES):
        third_stage(piece)
    pass_on(0)
    pass_on(1)

    gap = lax.rem(z - y + SIDE, SIDE)

    def to_plane(piece, step):
        return remote(
            whole.at[piece], fourth.at[piece, step - 1],
            sends.at[2, piece, step - 1], recvs.at[2, piece, step - 1],
            device(x, y, turned(z, SIDE - step), core),
        )

    def to_row(piece, step):
        return remote(
            fifth.at[0, piece], fifth.at[1, piece],
            sends.at[3, piece, step - 1], recvs.at[3, piece, 0],
            device(x, turned(y, step), z, core),
        )

    for piece in range(PIECES):
        at, started = threes[piece]
        for copy in started:
            copy.wait_recv()
        whole[piece] = add(half[piece, at], *[third[piece, step - 1] for step in steps])
        for step in steps:
            @pl.when(gap == step)
            def _():
                to_plane(piece, step).start()

    @pl.when(gap == 0)
    def _():
        for piece in range(PIECES):
            for step in steps:
                to_plane(piece, step).wait_recv()
            fifth[0, piece] = add(whole[piece], *[fourth[piece, step - 1] for step in steps])
            for step in steps:
                to_row(piece, step).start()
        for piece in range(PIECES):
            for step in steps:
                to_row(piece, step).wait_send()
        sum_ref[...] = fifth[0]

    @pl.when(gap != 0)
    def _():
        for piece in range(PIECES):
            to_row(piece, 1).wait_recv()
        sum_ref[...] = fifth[1]

    for piece in range(PIECES):
        for step in steps:
            @pl.when(gap == step)
            def _():
                to_plane(piece, step).wait_send()

    for copy, over_x, slot in returns:
        copy.wait_recv()

        @pl.when(True if slot < 2 else jnp.logical_not(over_x))
        def _():
            copy.wait_send()

    @pl.when(crosses)
    def _():
        for slot in range(2):
            to_forwarder(slot).wait_send()

    @pl.when(forwards)
    def _():
        for slot in range(2):
            forward(slot).wait_send()

    for copy in copies:
        copy.wait_send()
    att_store.wait()


def settle_kernel(
    norm, flags_ref, sum_ref, back_ref, att_in, gq_in, gk_in, gv_in,
    att_out, gq_out, gk_out, gv_out, rows_ref, own, extra, att, sem, att_sem,
):
    def block(i):
        return pl.ds(i * BLOCK, BLOCK)

    att_loads = [
        pltpu.make_async_copy(att_in.at[block(i)], att.at[block(i)], att_sem.at[i])
        for i in range(OWN)
    ]
    att_stores = [
        pltpu.make_async_copy(att.at[block(i)], att_out.at[block(i)], att_sem.at[i])
        for i in range(OWN)
    ]
    for copy in att_loads:
        copy.start()
    sides = []
    for side, (near, far) in enumerate(((0, 1), (3, 2))):
        parts = ((gk_out, near, 0), (gv_out, near, 1), (gk_out, far, 2), (gv_out, far, 3))
        ours = [
            pltpu.make_async_copy(out.at[block(at)], own.at[side, slot], sem.at[side, slot])
            for out, at, slot in parts
        ]
        theirs = [
            pltpu.make_async_copy(
                back_ref.at[side, slot], extra.at[side, slot], sem.at[side, 4 + slot]
            )
            for slot in range(4)
        ]
        moved = [
            pltpu.make_async_copy(extra.at[side, slot], out.at[block(near)], sem.at[side, slot])
            for slot, out in enumerate((gk_out, gv_out, gq_out))
        ]
        added = [
            pltpu.make_async_copy(own.at[side, slot], out.at[block(at)], sem.at[side, slot])
            for out, at, slot in parts
        ]
        away, shared, both = (flags_ref[3 * side + i] == 1 for i in range(3))
        sides.append((side, ours, theirs, moved, added, away, shared, both))

    for side, ours, theirs, moved, added, away, shared, both in sides:
        @pl.when(jnp.logical_or(away, shared))
        def _():
            for copy in theirs:
                copy.start()

        @pl.when(shared)
        def _():
            for copy in ours:
                copy.start()

    for piece in range(PIECES):
        for tile in range(PIECE // 128):
            lanes = slice(piece * PIECE + tile * 128, piece * PIECE + (tile + 1) * 128)
            part = sum_ref[piece].astype(jnp.float32)[tile * PART : (tile + 1) * PART]
            rows_ref[:, lanes] = part * norm

    for copy in att_loads:
        copy.wait()
    for side, ours, theirs, moved, added, away, shared, both in sides:
        @pl.when(jnp.logical_or(away, shared))
        def _():
            for copy in theirs:
                copy.wait()

        @pl.when(away)
        def _():
            att[3 * side * BLOCK : (3 * side + 1) * BLOCK] = extra[side, 3]

        att_stores[3 * side].start()
        att_stores[1 + side].start()

        @pl.when(away)
        def _():
            for copy in moved:
                copy.start()

        @pl.when(shared)
        def _():
            for slot in range(4):
                ours[slot].wait()
                total = own[side, slot].astype(jnp.float32)
                other = extra[side, slot].astype(jnp.float32)
                if slot >= 2:
                    other = jnp.where(both, other, 0.0)
                own[side, slot] = (total + other).astype(jnp.bfloat16)
                added[slot].start()

    for side, ours, theirs, moved, added, away, shared, both in sides:
        @pl.when(away)
        def _():
            for copy in moved:
                copy.wait()

        @pl.when(shared)
        def _():
            for copy in added:
                copy.wait()

    for copy in att_stores:
        copy.wait()


def on_device(q_tokens, k_tokens, v_tokens, d_attended, w_out, lengths):
    rows, width = q_tokens.shape[1:]
    count = lax.axis_size("tok")
    norm = 1.0 / math.sqrt(lax.axis_size("dp") * count * rows)
    q, k, v, dy = q_tokens[0], k_tokens[0], v_tokens[0], d_attended[0]
    low = jnp.bfloat16
    vmem, smem, anywhere = (
        pl.BlockSpec(memory_space=space) for space in (pltpu.VMEM, pltpu.SMEM, pl.ANY)
    )
    token_shape = jax.ShapeDtypeStruct((rows, width), low)
    halo_shape = jax.ShapeDtypeStruct((2, 4, BLOCK, width), low)
    big = 58 * 1024 * 1024

    halo, dm = pl.pallas_call(
        functools.partial(exchange_kernel, count),
        out_shape=(halo_shape, token_shape),
        in_specs=[smem] + [anywhere] * 5,
        out_specs=(anywhere, anywhere),
        scratch_shapes=[
            pltpu.VMEM((rows, width), low),
            pltpu.VMEM((width, width), low),
            pltpu.VMEM((2, BLOCK, width), low),
            pltpu.VMEM((2, 2, BLOCK, width), low),
            pltpu.VMEM((2, 2, BLOCK, width), low),
            pltpu.VMEM((rows, width), low),
            pltpu.SemaphoreType.DMA((8,)),
            pltpu.SemaphoreType.DMA((2, 4)),
            pltpu.SemaphoreType.DMA((2, 4)),
        ],
        compiler_params=pltpu.CompilerParams(
            collective_id=0, has_side_effects=True, vmem_limit_bytes=big
        ),
        name="exchange",
    )(lengths, q, k, v, dy, w_out)

    dma = pltpu.SemaphoreType.DMA
    slab = pltpu.VMEM((SLOTS * BLOCK, width), low)
    square = pltpu.VMEM((width, width), low)
    sides = pltpu.VMEM((2, BLOCK, width), low)
    mixed_shape = jax.ShapeDtypeStruct(((OWN + 2) * BLOCK, width), low)
    mixed, gq, gk, gv, ret, flags = pl.pallas_call(
        attention_kernel,
        out_shape=(
            mixed_shape, token_shape, token_shape, token_shape, halo_shape,
            jax.ShapeDtypeStruct((6,), jnp.int32),
        ),
        in_specs=[smem] + [anywhere] * 6,
        out_specs=(anywhere,) * 5 + (smem,),
        scratch_shapes=[slab] * 4 + [square, sides] + [slab] * 4
        + [sides, pltpu.SMEM((8, 3), jnp.int32), dma((8,)), dma((2, 4)), dma((4, SLOTS))],
        compiler_params=pltpu.CompilerParams(vmem_limit_bytes=big),
        name="attention",
    )(lengths, q, k, v, dm, halo, w_out)

    sum_shape = jax.ShapeDtypeStruct((PIECES, PACKED, 128), low)

    def pieces(*sizes):
        return pltpu.VMEM((PIECES, *sizes, PACKED, 128), low)

    slab = pltpu.VMEM(mixed_shape.shape, low)
    back, summed, att = pl.pallas_call(
        functools.partial(finish_kernel, count),
        out_shape=(halo_shape, sum_shape, token_shape),
        in_specs=[anywhere] * 5,
        out_specs=(anywhere, vmem, anywhere),
        scratch_shapes=[
            slab, pltpu.VMEM(mixed_shape.shape[::-1], low), slab, square,
            pltpu.VMEM((rows, width), low),
            pltpu.VMEM((width, PIECE), jnp.float32),
            pltpu.VMEM((PACKED, 128), jnp.float32),
            pieces(2, SIDE, SIDE), pieces(SIDE, SIDE), pieces(SIDE, SIDE),
            pieces(SIDE - 1, SIDE), pieces(SIDE), pieces(SIDE - 1),
            pieces(), pieces(SIDE - 1),
            pltpu.VMEM((2, PIECES, PACKED, 128), low),
            dma((11,)), dma((2, 4)), dma((2, 4)), dma((PIECES,)), dma((PIECES,)),
            dma((4, PIECES, SIDE - 1)), dma((4, PIECES, SIDE - 1)),
            sides, dma((2,)), dma((2,)),
        ],
        compiler_params=pltpu.CompilerParams(
            collective_id=1, has_side_effects=True, vmem_limit_bytes=big
        ),
        name="finish",
    )(ret, mixed, dy, halo, w_out)

    att, gq, gk, gv, grad_rows = pl.pallas_call(
        functools.partial(settle_kernel, norm),
        out_shape=(token_shape,) * 4 + (jax.ShapeDtypeStruct((PART, width), jnp.float32),),
        in_specs=[smem, vmem] + [anywhere] * 5,
        out_specs=(anywhere,) * 4 + (vmem,),
        scratch_shapes=[
            pltpu.VMEM((2, 4, BLOCK, width), low),
            pltpu.VMEM((2, 4, BLOCK, width), low),
            pltpu.VMEM((rows, width), low),
            dma((2, 8)), dma((OWN,)),
        ],
        input_output_aliases={4: 1, 5: 2, 6: 3},
        compiler_params=pltpu.CompilerParams(vmem_limit_bytes=big),
        name="settle",
    )(flags, summed, back, att, gq, gk, gv)
    return (att[None], gq[None], gk[None], gv[None], grad_rows)


def solution(mesh):
    tokens = P("dp", "tok", None)
    return jax.shard_map(
        on_device,
        mesh=mesh,
        in_specs=(tokens, tokens, tokens, tokens, P(), P("dp", None)),
        out_specs=(tokens, tokens, tokens, tokens, P("tok", None)),
        check_vma=False,
    )
```
